256 devices in a mesh: ctx: 32 (over x, y, core), tp: 8 (over z).
Axes of the slice: x: 4, y: 4, z: 8, core: 2. Of those that a mesh axis runs over, the one named last changes fastest.
Arguments:
- query: bfloat16 [8192, 4096], P('ctx', 'tp'), may hold values from -6 to 6
- key_branch: bfloat16 [8192, 4096], P('ctx', 'tp'), may hold values from -6 to 6
- value_branch: bfloat16 [8192, 4096], P('ctx', 'tp'), may hold values from -6 to 6
- decay: float32 [16, 4096], P(None, 'tp'), may hold values from 1.2207031e-06 to 0.05
- frequency: float32 [16, 4096], P(None, 'tp'), may hold values from -3.140625 to 3.140625
- residue: float32 [2, 16, 4096], P(None, None, 'tp'), may hold values from -1.5 to 1.5
- skip_gain: float32 [4096], P('tp'), may hold values from -6 to 6
- out_weight: bfloat16 [4096, 4096], P('ctx', 'tp'), may hold values from -0.09375 to 0.09375
- doc_starts: int32 [8192], P('ctx'), may hold values from 0 to 1, as said below
Outputs:
- mixed: bfloat16 [8192, 4096], P('ctx', 'tp')
The draws below stay inside these ranges and needn't reach their ends.
Inputs may be any that keep to these rules, and one draw needn't show every extreme that they name: `doc_starts`: token 0 starts a document; documents between starts are 256 to 4096 tokens long, the last one possibly shorter.
All inputs are finite; a program needn't handle non-finite values.
Results may differ from the reference program's by a relative error of at most 0.0049.
Values may be sent and summed in bfloat16 or wider, within the bound.
No kernel may reach another device: no remote copies, remote signals or barrier semaphores. Data moves between devices by JAX's collectives and lax.ppermute only.
A program may use at most 128 MiB of HBM per device.

```python
import math
import jax
import jax.numpy as jnp
from jax import lax

D = 4096
MODES = 16
BLOCK = 64
TOK_DEV = 256
SEQ = 8192


def draw_doc_starts(key, part):
    key = jax.random.fold_in(key, 7)
    shards = SEQ // TOK_DEV
    longest = min(20, shards // 2) * TOK_DEV
    count = SEQ // TOK_DEV + 1
    lengths = jax.random.randint(key, (count,), TOK_DEV, longest + 1).astype(jnp.int32)
    ends = jnp.cumsum(lengths).astype(jnp.int32)
    begins = jnp.concatenate([jnp.zeros((1,), jnp.int32), ends[:-1]])
    places = jnp.arange(SEQ, dtype=jnp.int32)
    return jnp.any(places[:, None] == begins[None, :], axis=1).astype(jnp.int32)


def shard_levels(rng, shape, split, low, high):
    loudness = 1.0
    for dim, blocks in split:
        draws = jax.random.uniform(jax.random.fold_in(jax.random.fold_in(rng, 6), dim), (blocks,), jnp.float32, low / len(split), high / len(split))
        loudness = loudness * jnp.repeat(jnp.exp(draws), shape[dim] // blocks).reshape((-1,) + (1,) * (len(shape) - 1 - dim))
    return loudness


def normal_values(own_key, shape, width, most, split=(), kind=jnp.bfloat16):
    array = width * jax.random.normal(own_key, shape, jnp.float32)
    if split:
        array = array * shard_levels(own_key, shape, split, -0.22, 0.18)
    return jnp.clip(array, -most, most).astype(kind)


def setup_inputs(seed: int = 0) -> dict:
    keys = jax.random.split(jax.random.key(seed), 10)
    return {
        "query": normal_values(keys[0], (SEQ, D), 1.0, 6.0, ((0, 32), (1, 8))),
        "key_branch": normal_values(keys[1], (SEQ, D), 1.0, 6.0, ((0, 32), (1, 8))),
        "value_branch": normal_values(keys[2], (SEQ, D), 1.0, 6.0, ((0, 32), (1, 8))),
        "decay": jnp.clip(jnp.exp(math.log(0.05) - 10.620351 * jax.random.uniform(keys[3], (MODES, D), jnp.float32) ** shard_levels(keys[3], (MODES, D), ((1, 8),), -0.2, 0.2)), 1.220703097715159e-06, 0.05),
        "frequency": jnp.clip(jax.random.uniform(keys[4], (MODES, D), jnp.float32, -3.140625, 3.140625), -3.140625, 3.140625),
        "residue": normal_values(keys[5], (2, MODES, D), 0.25, 1.5, ((2, 8),), jnp.float32),
        "skip_gain": normal_values(keys[6], (D,), 1.0, 6.0, ((0, 8),), jnp.float32),
        "out_weight": normal_values(keys[7], (D, D), D ** -0.5, 0.09375, ((0, 32), (1, 8))),
        "doc_starts": draw_doc_starts(jax.random.fold_in(keys[9], 71), 0),
    }


def build_tables(decay, frequency, residue, blen):
    steps = jnp.arange(blen + 1, dtype=jnp.float32)[:, None, None]
    magnitude = jnp.exp(-decay[None] * steps)
    pole_re = magnitude * jnp.cos(frequency[None] * steps)
    pole_im = magnitude * jnp.sin(frequency[None] * steps)
    scaling = jnp.sqrt(-jnp.expm1(-2.0 * decay))
    weight_re = residue[0] * scaling
    weight_im = residue[1] * scaling
    taps = lax.optimization_barrier(jnp.sum(weight_re * pole_re[:blen] - weight_im * pole_im[:blen], axis=1))
    lagged = jnp.arange(blen)[:, None] - jnp.arange(blen)[None, :]
    toeplitz = jnp.where((lagged >= 0)[:, :, None], taps[jnp.clip(lagged, 0, blen - 1)], 0.0)
    out_re = weight_re * pole_re[1:] - weight_im * pole_im[1:]
    out_im = weight_re * pole_im[1:] + weight_im * pole_re[1:]
    into_re = pole_re[:blen][::-1]
    into_im = pole_im[:blen][::-1]
    return (toeplitz, out_re, out_im, into_re, into_im, pole_re[blen], pole_im[blen])

def block_step(tables, carry, signal_blk, starts_blk, with_local, want_out):
    toeplitz, out_re, out_im, into_re, into_im, jump_re, jump_im = tables
    hp = lax.Precision.HIGHEST
    state_re, state_im = carry
    running = jnp.cumsum(starts_blk)
    keep = (running == 0).astype(jnp.float32)
    result = None
    if want_out:
        result = keep[:, None] * (jnp.einsum('tmc,mc->tc', out_re, state_re, precision=hp) - jnp.einsum('tmc,mc->tc', out_im, state_im, precision=hp))
        if with_local:
            same = (running[:, None] == running[None, :]).astype(jnp.float32)
            result = result + jnp.einsum('tsc,sc->tc', toeplitz * same[:, :, None], signal_blk, precision=hp)
    through = keep[-1]
    new_re = through * (jump_re * state_re - jump_im * state_im)
    new_im = through * (jump_re * state_im + jump_im * state_re)
    if with_local:
        tail = (running == running[-1]).astype(jnp.float32)
        weighted = signal_blk * tail[:, None]
        new_re = new_re + jnp.einsum('smc,sc->mc', into_re, weighted, precision=hp)
        new_im = new_im + jnp.einsum('smc,sc->mc', into_im, weighted, precision=hp)
    return ((new_re, new_im), result)

def run_blocks(tables, carry, signal, starts, with_local, want_out):
    blocks = signal.shape[0] // BLOCK
    sig_blocks = signal.reshape(blocks, BLOCK, signal.shape[1])
    start_blocks = starts.reshape(blocks, BLOCK)

    def stepper(state, pieces):
        return block_step(tables, state, pieces[0], pieces[1], with_local, want_out)
    final, outs = lax.scan(stepper, carry, (sig_blocks, start_blocks))
    if want_out:
        outs = outs.reshape(signal.shape)
    return (final, outs)

def reference(query, key_branch, value_branch, decay, frequency, residue, skip_gain, out_weight, doc_starts):
    signal = key_branch.astype(jnp.float32) * value_branch.astype(jnp.float32)
    tables = build_tables(decay, frequency, residue, BLOCK)
    zeros = jnp.zeros(decay.shape, jnp.float32)
    final, conv = run_blocks(tables, (zeros, zeros), signal, doc_starts, True, True)
    conv = conv + skip_gain[None, :] * signal
    hidden = (query.astype(jnp.float32) * conv).astype(jnp.bfloat16)
    return jnp.dot(hidden, out_weight, preferred_element_type=jnp.float32).astype(jnp.bfloat16)
```

```python
import jax
import jax.numpy as jnp
from jax import lax
from jax.experimental import pallas as pl
from jax.experimental.pallas import tpu as pltpu
from jax.sharding import PartitionSpec as P

F32 = jnp.float32
BF16 = jnp.bfloat16
NX, NY, NC, NZ = 4, 4, 2, 8
TOK, CH, MODES = 256, 512, 16
LANES = 128
GROUPS = CH // LANES
STEPS = 32
BLOCKS = TOK // STEPS
ROWS = 2 * MODES
PAY = ROWS + 8
VMEM = pl.BlockSpec(memory_space=pltpu.VMEM)
PARAMS = pltpu.CompilerParams(vmem_limit_bytes=48 * 1024 * 1024)


def call(kernel, outs, args, scratch=(), flops=0, nbytes=0):
    return pl.pallas_call(
        kernel,
        out_shape=outs,
        in_specs=[VMEM] * len(args),
        out_specs=jax.tree.map(lambda unused: VMEM, outs),
        scratch_shapes=list(scratch),
        compiler_params=PARAMS,
        cost_estimate=pl.CostEstimate(flops=flops, bytes_accessed=nbytes, transcendentals=0),
    )(*args)


def struct(*shape, dtype=F32):
    return jax.ShapeDtypeStruct(shape, dtype)


def cmul(a, b):
    return a[0] * b[0] - a[1] * b[1], a[0] * b[1] + a[1] * b[0]


def cadd(a, b):
    return a[0] + b[0], a[1] + b[1]


def square(a):
    return a[0] * a[0] - a[1] * a[1], 2.0 * a[0] * a[1]


def halves(ref):
    return ref[:MODES, :], ref[MODES:ROWS, :]


def first_start(starts_ref):
    starts = starts_ref[...]
    at = lax.broadcasted_iota(jnp.int32, starts.shape, 0) * LANES
    at = at + lax.broadcasted_iota(jnp.int32, starts.shape, 1)
    where = jnp.where(starts > 0, at, TOK)
    return jnp.min(jnp.min(where, axis=1, keepdims=True), axis=0, keepdims=True)


def poles(decay_ref, freq_ref):
    magnitude = jnp.exp(-decay_ref[...])
    freq = freq_ref[...]
    return magnitude * jnp.cos(freq), magnitude * jnp.sin(freq)


def fill_powers(pole, table_re, table_im, count):
    def put(k, value):
        for g in range(GROUPS):
            rows = pl.ds(pl.multiple_of(k * MODES, MODES), MODES)
            lanes = slice(g * LANES, (g + 1) * LANES)
            table_re[g, rows, :] = value[0][:, lanes]
            table_im[g, rows, :] = value[1][:, lanes]

    def step(k, value):
        put(k, value)
        return cmul(value, pole)

    one = (jnp.ones((MODES, CH), F32), jnp.zeros((MODES, CH), F32))
    last = lax.fori_loop(0, count, step, one)
    return last


def fill_signal(key_ref, value_ref, sig):
    for g in range(GROUPS):
        lanes = slice(g * LANES, (g + 1) * LANES)
        sig[g] = key_ref[:, lanes].astype(F32) * value_ref[:, lanes].astype(F32)


def block_iota():
    return lax.broadcasted_iota(jnp.int32, (BLOCKS, LANES), 0)


def ends_kernel(key_ref, value_ref, decay_ref, freq_ref, starts_ref, pay_ref, eb_ref, p256_ref,
                sig, tre, tim, qre, qim):
    s0 = first_start(starts_ref)
    b0 = s0 // STEPS
    fill_signal(key_ref, value_ref, sig)
    pole = poles(decay_ref, freq_ref)
    q = fill_powers(pole, tre, tim, STEPS)
    one = (jnp.ones((MODES, CH), F32), jnp.zeros((MODES, CH), F32))
    value = one
    for n in range(BLOCKS):
        row = (BLOCKS - 1 - n) * MODES
        for g in range(GROUPS):
            lanes = slice(g * LANES, (g + 1) * LANES)
            qre[g, row:row + MODES, :] = value[0][:, lanes]
            qim[g, row:row + MODES, :] = value[1][:, lanes]
        value = cmul(value, q)
    p256_ref[:MODES, :] = value[0]
    p256_ref[MODES:, :] = value[1]
    blocks = block_iota()
    reach = (s0 >= TOK) | (blocks >= b0)

    def group(g, unused):
        def step(j, acc):
            x = sig[g, pl.ds(j, BLOCKS, stride=STEPS), :]
            x = jnp.where((blocks * STEPS + j >= s0) | (blocks != b0), x, 0.0)
            base = (STEPS - 1 - j) * MODES
            out = []
            for m in range(MODES):
                out.append(acc[2 * m] + tre[g, pl.ds(base + m, 1), :] * x)
                out.append(acc[2 * m + 1] + tim[g, pl.ds(base + m, 1), :] * x)
            return tuple(out)

        zero = jnp.zeros((BLOCKS, LANES), F32)
        acc = lax.fori_loop(0, STEPS, step, (zero,) * ROWS, unroll=4)
        for m in range(MODES):
            re, im = acc[2 * m], acc[2 * m + 1]
            eb_ref[g, m] = re
            eb_ref[g, MODES + m] = im
            w = (qre[g, pl.ds(m, BLOCKS, stride=MODES), :], qim[g, pl.ds(m, BLOCKS, stride=MODES), :])
            end = cmul(w, (re, im))
            pay3 = pl.ds(pl.multiple_of(g * LANES, LANES), LANES)
            pay_ref[pl.ds(m, 1), pay3] = jnp.sum(jnp.where(reach, end[0], 0.0), axis=0, keepdims=True)
            pay_ref[pl.ds(MODES + m, 1), pay3] = jnp.sum(jnp.where(reach, end[1], 0.0), axis=0, keepdims=True)
        return unused

    lax.fori_loop(0, GROUPS, group, 0)
    pay_ref[ROWS:, :] = jnp.broadcast_to((s0 >= TOK).astype(F32), (PAY - ROWS, CH))


def local_kernel(key_ref, value_ref, decay_ref, freq_ref, res_ref, skip_ref, starts_ref, eb_ref,
                 y_ref, pz_ref, gz_ref, tre, tim, sig, qre, qim, taps, rows_):
    s0 = first_start(starts_ref)
    b0 = s0 // STEPS
    blocks = block_iota()
    fill_signal(key_ref, value_ref, sig)
    pole = poles(decay_ref, freq_ref)
    q = fill_powers(pole, tre, tim, STEPS + 1)
    q = (jnp.concatenate([tre[g, STEPS * MODES:, :] for g in range(GROUPS)], axis=1),
         jnp.concatenate([tim[g, STEPS * MODES:, :] for g in range(GROUPS)], axis=1))
    y = 2.0 * decay_ref[...]
    series = jnp.ones_like(y)
    for n in range(10, 1, -1):
        series = 1.0 - y * (1.0 / n) * series
    scale = jnp.sqrt(y * series)
    weight = (res_ref[0] * scale, res_ref[1] * scale)
    for g in range(GROUPS):
        lanes = slice(g * LANES, (g + 1) * LANES)
        w_re, w_im = weight[0][:, lanes], weight[1][:, lanes]
        for k in range(STEPS):
            term = w_re * tre[g, k * MODES:(k + 1) * MODES, :] - w_im * tim[g, k * MODES:(k + 1) * MODES, :]
            row = jnp.sum(term, axis=0, keepdims=True)
            if k == 0:
                row = row + skip_ref[:, lanes]
            taps[g, k:k + 1, :] = row
    value = weight
    for n in range(BLOCKS):
        for g in range(GROUPS):
            lanes = slice(g * LANES, (g + 1) * LANES)
            qre[g, n * MODES:(n + 1) * MODES, :] = value[0][:, lanes]
            qim[g, n * MODES:(n + 1) * MODES, :] = value[1][:, lanes]
        value = cmul(value, q)
    power = q
    for n in range(3):
        for g in range(GROUPS):
            lanes = slice(g * LANES, (g + 1) * LANES)
            rows_[g, n * ROWS:n * ROWS + MODES, :] = power[0][:, lanes]
            rows_[g, n * ROWS + MODES:(n + 1) * ROWS, :] = power[1][:, lanes]
        power = square(power)
    for g in range(GROUPS):
        lanes = slice(g * LANES, (g + 1) * LANES)
        rows_[g, 3 * ROWS:3 * ROWS + MODES, :] = weight[0][:, lanes]
        rows_[g, 3 * ROWS + MODES:4 * ROWS, :] = weight[1][:, lanes]

    keeps = []
    for n in range(3):
        s = 1 << n
        keeps.append((blocks >= s) & jnp.logical_not((blocks - s < b0) & (b0 <= blocks)))
    heard = blocks <= b0

    def group(g, unused):
        for m in range(MODES):
            state = (eb_ref[g, m], eb_ref[g, MODES + m])
            for n in range(3):
                moved = [jnp.where(keeps[n], pltpu.roll(part, 1 << n, 0), 0.0) for part in state]
                step = (rows_[g, n * ROWS + m:n * ROWS + m + 1, :],
                        rows_[g, n * ROWS + MODES + m:n * ROWS + MODES + m + 1, :])
                state = cadd(state, cmul(step, moved))
            before = [jnp.where(blocks >= 1, pltpu.roll(part, 1, 0), 0.0) for part in state]
            w = (rows_[g, 3 * ROWS + m:3 * ROWS + m + 1, :],
                 rows_[g, 3 * ROWS + MODES + m:3 * ROWS + MODES + m + 1, :])
            scaled = cmul(w, before)
            pz_ref[g, m] = scaled[0]
            pz_ref[g, MODES + m] = scaled[1]
            gz_ref[g, m] = jnp.where(heard, qre[g, pl.ds(m, BLOCKS, stride=MODES), :], 0.0)
            gz_ref[g, MODES + m] = jnp.where(heard, qim[g, pl.ds(m, BLOCKS, stride=MODES), :], 0.0)

        tile = 8

        def fir(select):
            xs = []
            for j in range(STEPS):
                x = sig[g, pl.ds(j, BLOCKS, stride=STEPS), :]
                late = (blocks * STEPS + j >= s0) | (blocks != b0)
                xs.append(jnp.where(late if select else jnp.logical_not(late), x, 0.0))
            for top in range(0, STEPS, tile):
                acc = [jnp.zeros((BLOCKS, LANES), F32)] * tile
                for k in range(top + tile):
                    tap = taps[g, k:k + 1, :]
                    for i in range(tile):
                        if top + i - k >= 0:
                            acc[i] = acc[i] + tap * xs[top + i - k]
                for i in range(tile):
                    if select:
                        y_ref[g, top + i] = acc[i]
                    else:
                        early = (blocks * STEPS + top + i < s0) & (blocks == b0)
                        y_ref[g, top + i] = y_ref[g, top + i] + jnp.where(early, acc[i], 0.0)

        fir(True)
        fir(False)
        return unused

    lax.fori_loop(0, GROUPS, group, 0)


def chip_kernel(own_ref, other_ref, p256_ref, pay_ref):
    core = lax.axis_index("ctx") % NC
    first = (core == 0).astype(F32)
    own, other = halves(own_ref), halves(other_ref)
    own_thru, other_thru = own_ref[ROWS:ROWS + 1, :], other_ref[ROWS:ROWS + 1, :]
    early = [first * a + (1.0 - first) * b for a, b in zip(own, other)]
    late = [first * b + (1.0 - first) * a for a, b in zip(own, other)]
    late_thru = first * other_thru + (1.0 - first) * own_thru
    moved = cmul(halves(p256_ref), early)
    pay_ref[:MODES, :] = late_thru * moved[0] + late[0]
    pay_ref[MODES:ROWS, :] = late_thru * moved[1] + late[1]
    pay_ref[ROWS:, :] = jnp.broadcast_to(own_thru * other_thru, (PAY - ROWS, CH))


def row_kernel(own_ref, one_ref, two_ref, three_ref, p256_ref, pay_ref, before_ref, factor_ref, held):
    mine = (lax.axis_index("ctx") // NC) % NY
    for k, ref in enumerate((own_ref, one_ref, two_ref, three_ref)):
        held[lax.rem(mine - k + NY, NY)] = ref[...]
    p512 = square(halves(p256_ref))
    state = (jnp.zeros((MODES, CH), F32),) * 2
    factor = (jnp.ones((MODES, CH), F32), jnp.zeros((MODES, CH), F32))
    thru = jnp.ones((1, CH), F32)
    for i in range(NY):
        @pl.when(mine == i)
        def put():
            before_ref[:MODES, :] = state[0]
            before_ref[MODES:, :] = state[1]
            factor_ref[:MODES, :] = factor[0]
            factor_ref[MODES:, :] = factor[1]
        open_ = held[i, ROWS:ROWS + 1, :]
        step = (open_ * p512[0], open_ * p512[1])
        state = cadd(cmul(step, state), (held[i, :MODES, :], held[i, MODES:ROWS, :]))
        factor = cmul(step, factor)
        thru = thru * open_
    pay_ref[:MODES, :] = state[0]
    pay_ref[MODES:ROWS, :] = state[1]
    pay_ref[ROWS:, :] = jnp.broadcast_to(thru, (PAY - ROWS, CH))


def gate_kernel(query_ref, y_ref, pz_ref, gz_ref, tre, tim, starts_ref, own_ref, other_ref, p256_ref,
                before_ref, factor_ref, one_ref, two_ref, hidden_ref, conv, sin):
    index = lax.axis_index("ctx")
    core, row = index % NC, index // (NC * NY)
    p256 = halves(p256_ref)
    p2048 = square(square(square(p256)))
    has_one = (row >= 1).astype(F32)
    has_two = (row >= 2).astype(F32)
    far = cmul(p2048, halves(two_ref))
    open_one = has_two * one_ref[ROWS:ROWS + 1, :]
    incoming = [has_one * a + open_one * b for a, b in zip(halves(one_ref), far)]
    state = cadd(halves(before_ref), cmul(halves(factor_ref), incoming))
    second = (core == 1).astype(F32)
    moved = cmul(p256, state)
    early_thru = other_ref[ROWS:ROWS + 1, :]
    state = [(1.0 - second) * a + second * (early_thru * b + c)
             for a, b, c in zip(state, moved, halves(other_ref))]
    for g in range(GROUPS):
        lanes = slice(g * LANES, (g + 1) * LANES)
        sin[g, :MODES, :] = state[0][:, lanes]
        sin[g, MODES:, :] = state[1][:, lanes]
    s0 = first_start(starts_ref)
    b0 = s0 // STEPS
    blocks = block_iota()

    def group(g, unused):
        z = []
        for m in range(MODES):
            s = (sin[g, m:m + 1, :], sin[g, MODES + m:MODES + m + 1, :])
            z.append(cadd((pz_ref[g, m], pz_ref[g, MODES + m]),
                          cmul((gz_ref[g, m], gz_ref[g, MODES + m]), s)))

        def step(j, unused):
            base = (j + 1) * MODES
            total = [None] * 4
            for m in range(MODES):
                term = tre[g, pl.ds(base + m, 1), :] * z[m][0] - tim[g, pl.ds(base + m, 1), :] * z[m][1]
                total[m % 4] = term if total[m % 4] is None else total[m % 4] + term
            total = (total[0] + total[1]) + (total[2] + total[3])
            late = (blocks * STEPS + j >= s0) & (blocks == b0)
            conv[g, pl.ds(j, BLOCKS, stride=STEPS), :] = y_ref[g, j] + jnp.where(late, 0.0, total)
            return unused

        return lax.fori_loop(0, STEPS, step, unused, unroll=4)

    lax.fori_loop(0, GROUPS, group, 0)
    for g in range(GROUPS):
        lanes = slice(g * LANES, (g + 1) * LANES)
        hidden_ref[:, lanes] = (query_ref[:, lanes].astype(F32) * conv[g]).astype(BF16)


def weight_kernel(*refs):
    pieces, out_ref = refs[:8], refs[8]
    index = lax.axis_index("ctx")
    core, y, x = index % NC, (index // NC) % NY, index // (NC * NY)
    for side in range(2):
        c = core if side == 0 else 1 - core
        for dx in range(NX):
            there = lax.rem(x - dx + NX, NX)
            for dy in range(NY):
                chip = there * NY + lax.rem(y - dy + NY, NY)
                rows = pl.ds(pl.multiple_of((chip * NC + c) * 128, 128), 128)
                out_ref[rows, :] = pieces[side * NX + dx][dy * 128:(dy + 1) * 128, :]


def near_kernel(own, up1, down1, up2, down2, weight_ref, out_ref):
    z = lax.axis_index("tp")
    total = None
    for k, ref in ((0, own), (1, up1), (-1, down1), (2, up2), (-2, down2)):
        rows = pl.ds(pl.multiple_of(lax.rem(z - k + NZ, NZ) * CH, CH), CH)
        term = jnp.dot(ref[...], weight_ref[rows, :], preferred_element_type=F32)
        total = term if total is None else total + term
    out_ref[...] = total


def far_kernel(near_ref, up3, down3, up4, down4, weight_ref, out_ref):
    z = lax.axis_index("tp")

    def rows(k):
        return pl.ds(pl.multiple_of(lax.rem(z - k + NZ, NZ) * CH, CH), CH)

    total = near_ref[...]
    for k, ref in ((3, up3), (-3, down3)):
        total = total + jnp.dot(ref[...], weight_ref[rows(k), :], preferred_element_type=F32)
    half = TOK // 2
    last = weight_ref[rows(4), :]
    out_ref[:half, :] = (total[:half] + jnp.dot(up4[...], last, preferred_element_type=F32)).astype(BF16)
    out_ref[half:, :] = (total[half:] + jnp.dot(down4[...], last, preferred_element_type=F32)).astype(BF16)


def ctx_index(x, y, c):
    return ((x % NX) * NY + y % NY) * NC + c % NC


def move(value, dx, dy, dc):
    pairs = [(ctx_index(x, y, c), ctx_index(x + dx, y + dy, c + dc))
             for x in range(NX) for y in range(NY) for c in range(NC)]
    return lax.ppermute(value, "ctx", pairs)


def turn(value, k):
    return lax.ppermute(value, "tp", [(i, (i + k) % NZ) for i in range(NZ)])


def shards(query, key, value, decay, freq, residue, skip, out_weight, doc_starts):
    starts = doc_starts.reshape(TOK // LANES, LANES)
    skip = skip.reshape(1, CH)
    sig = pltpu.VMEM((GROUPS, TOK, LANES), F32)
    qs = pltpu.VMEM((GROUPS, BLOCKS * MODES, LANES), F32)
    state_shape = struct(ROWS, CH)
    pay_shape = struct(PAY, CH)
    block_shape = struct(GROUPS, ROWS, BLOCKS, LANES)
    table = (GROUPS, (STEPS + 1) * MODES, LANES)

    pay, eb, p256 = call(
        ends_kernel, (pay_shape, block_shape, state_shape), (key, value, decay, freq, starts),
        [sig, pltpu.VMEM(table, F32), pltpu.VMEM(table, F32), qs, qs], 20_000_000, 1_500_000)
    other = move(pay, 0, 0, 1)

    wy = jnp.concatenate([out_weight] + [move(out_weight, 0, k, 0) for k in (1, 2, 3)], axis=0)
    wx = [wy] + [move(wy, k, 0, 0) for k in (1, 2, 3)]
    wo = [move(w, 0, 0, 1) for w in wx]
    weight = call(weight_kernel, struct(NZ * CH, CH, dtype=BF16), (*wx, *wo), (), 0, 8_000_000)

    chip = call(chip_kernel, pay_shape, (pay, other, p256))
    near = [move(chip, 0, k, 0) for k in (1, 2, 3)]
    y, pz, gz, tre, tim = call(
        local_kernel,
        (struct(GROUPS, STEPS, BLOCKS, LANES), block_shape, block_shape, struct(*table), struct(*table)),
        (key, value, decay, freq, residue, skip, starts, eb),
        [sig, qs, qs, pltpu.VMEM((GROUPS, STEPS, LANES), F32), pltpu.VMEM((GROUPS, 4 * ROWS, LANES), F32)],
        30_000_000, 5_000_000)
    row, before, factor = call(
        row_kernel, (pay_shape, state_shape, state_shape), (chip, *near, p256),
        [pltpu.VMEM((NY, PAY, CH), F32)])
    back = [move(row, k, 0, 0) for k in (1, 2)]
    hidden = call(
        gate_kernel, struct(TOK, CH, dtype=BF16),
        (query, y, pz, gz, tre, tim, starts, pay, other, p256, before, factor, *back),
        [sig, pltpu.VMEM((GROUPS, ROWS, LANES), F32)], 20_000_000, 5_000_000)

    half = TOK // 2
    up1, down1, up2, down2 = turn(hidden, 1), turn(hidden, -1), turn(hidden, 2), turn(hidden, -2)
    up3, down3 = turn(up2, 1), turn(down2, -1)
    up4, down4 = turn(up2[:half], 2), turn(down2[half:], -2)
    total = call(near_kernel, struct(TOK, CH), (hidden, up1, down1, up2, down2, weight), (),
                 5 * 2 * TOK * CH * CH, 4_000_000)
    return call(far_kernel, struct(TOK, CH, dtype=BF16), (total, up3, down3, up4, down4, weight), (),
                3 * 2 * TOK * CH * CH, 4_000_000)


def solution(mesh):
    in_specs = (
        P("ctx", "tp"),
        P("ctx", "tp"),
        P("ctx", "tp"),
        P(None, "tp"),
        P(None, "tp"),
        P(None, None, "tp"),
        P("tp"),
        P("ctx", "tp"),
        P("ctx"),
    )
    return jax.shard_map(
        shards, mesh=mesh, in_specs=in_specs, out_specs=P("ctx", "tp"), check_vma=False
    )
```

```python
import jax
import jax.numpy as jnp
from jax import lax
from jax.experimental import pallas as pl
from jax.experimental.pallas import tpu as pltpu
from jax.sharding import PartitionSpec as P

F32 = jnp.float32
BF16 = jnp.bfloat16
NX, NY, NC, NZ = 4, 4, 2, 8
TOK, CH, MODES = 256, 512, 16
LANES = 128
GROUPS = CH // LANES
STEPS = 32
BLOCKS = TOK // STEPS
ROWS = 2 * MODES
PAY = ROWS + 8
VMEM = pl.BlockSpec(memory_space=pltpu.VMEM)
FLAG = 16
SENT = 2 * ROWS + FLAG
WROWS = 128
PARAMS = pltpu.CompilerParams(vmem_limit_bytes=48 * 1024 * 1024)


def call(kernel, outs, args, scratch=(), flops=0, nbytes=0):
    return pl.pallas_call(
        kernel,
        out_shape=outs,
        in_specs=[VMEM] * len(args),
        out_specs=jax.tree.map(lambda unused: VMEM, outs),
        scratch_shapes=list(scratch),
        compiler_params=PARAMS,
        cost_estimate=pl.CostEstimate(flops=flops, bytes_accessed=nbytes, transcendentals=0),
    )(*args)


def struct(*shape, dtype=F32):
    return jax.ShapeDtypeStruct(shape, dtype)


def cmul(a, b):
    return a[0] * b[0] - a[1] * b[1], a[0] * b[1] + a[1] * b[0]


def cadd(a, b):
    return a[0] + b[0], a[1] + b[1]


def square(a):
    return a[0] * a[0] - a[1] * a[1], 2.0 * a[0] * a[1]


def halves(ref):
    return ref[:MODES, :], ref[MODES:ROWS, :]


def first_start(starts_ref):
    starts = starts_ref[...]
    at = lax.broadcasted_iota(jnp.int32, starts.shape, 0) * LANES
    at = at + lax.broadcasted_iota(jnp.int32, starts.shape, 1)
    where = jnp.where(starts > 0, at, TOK)
    return jnp.min(jnp.min(where, axis=1, keepdims=True), axis=0, keepdims=True)


def fill_powers(pole, table_re, table_im, count):
    def put(k, value):
        for g in range(GROUPS):
            rows = pl.ds(pl.multiple_of(k * MODES, MODES), MODES)
            lanes = slice(g * LANES, (g + 1) * LANES)
            table_re[g, rows, :] = value[0][:, lanes]
            table_im[g, rows, :] = value[1][:, lanes]

    def step(k, value):
        put(k, value)
        return cmul(value, pole)

    one = (jnp.ones((MODES, CH), F32), jnp.zeros((MODES, CH), F32))
    last = lax.fori_loop(0, count, step, one)
    return last


def fill_signal(key_ref, value_ref, sig):
    for g in range(GROUPS):
        lanes = slice(g * LANES, (g + 1) * LANES)
        sig[g] = key_ref[:, lanes].astype(F32) * value_ref[:, lanes].astype(F32)


def block_iota():
    return lax.broadcasted_iota(jnp.int32, (BLOCKS, LANES), 0)


def powers_kernel(pole_re, pole_im, tre, tim, qre, qim, p256_ref):
    fill_powers((pole_re[...], pole_im[...]), tre, tim, STEPS + 1)
    q = last_power(tre, tim)
    value = (jnp.ones((MODES, CH), F32), jnp.zeros((MODES, CH), F32))
    for n in range(BLOCKS):
        row = (BLOCKS - 1 - n) * MODES
        for g in range(GROUPS):
            lanes = slice(g * LANES, (g + 1) * LANES)
            qre[g, row:row + MODES, :] = value[0][:, lanes]
            qim[g, row:row + MODES, :] = value[1][:, lanes]
        value = cmul(value, q)
    p256_ref[:MODES, :] = value[0]
    p256_ref[MODES:, :] = value[1]


def ends_kernel(key_ref, value_ref, starts_ref, tre, tim, qre, qim, pay_ref, eb_ref, sig):
    s0 = first_start(starts_ref)
    b0 = s0 // STEPS
    fill_signal(key_ref, value_ref, sig)
    blocks = block_iota()
    reach = (s0 >= TOK) | (blocks >= b0)

    def group(g, unused):
        def step(j, acc):
            x = sig[g, pl.ds(j, BLOCKS, stride=STEPS), :]
            x = jnp.where((blocks * STEPS + j >= s0) | (blocks != b0), x, 0.0)
            base = (STEPS - 1 - j) * MODES
            out = []
            for m in range(MODES):
                out.append(acc[2 * m] + tre[g, pl.ds(base + m, 1), :] * x)
                out.append(acc[2 * m + 1] + tim[g, pl.ds(base + m, 1), :] * x)
            return tuple(out)

        zero = jnp.zeros((BLOCKS, LANES), F32)
        acc = lax.fori_loop(0, STEPS, step, (zero,) * ROWS, unroll=4)
        for m in range(MODES):
            re, im = acc[2 * m], acc[2 * m + 1]
            eb_ref[g, m] = re
            eb_ref[g, MODES + m] = im
            w = (qre[g, pl.ds(m, BLOCKS, stride=MODES), :], qim[g, pl.ds(m, BLOCKS, stride=MODES), :])
            end = cmul(w, (re, im))
            lanes = pl.ds(pl.multiple_of(g * LANES, LANES), LANES)
            pay_ref[pl.ds(m, 1), lanes] = jnp.sum(jnp.where(reach, end[0], 0.0), axis=0, keepdims=True)
            pay_ref[pl.ds(MODES + m, 1), lanes] = jnp.sum(jnp.where(reach, end[1], 0.0), axis=0, keepdims=True)
        return unused

    lax.fori_loop(0, GROUPS, group, 0)
    pay_ref[ROWS:, :] = jnp.broadcast_to((s0 >= TOK).astype(F32), (PAY - ROWS, CH))


def last_power(tre, tim):
    return [jnp.concatenate([t[g, STEPS * MODES:, :] for g in range(GROUPS)], axis=1) for t in (tre, tim)]


def local_kernel(sig, tre, tim, decay_ref, res_ref, skip_ref, starts_ref, y_ref, weight_ref, taps):
    s0 = first_start(starts_ref)
    b0 = s0 // STEPS
    blocks = block_iota()
    y = 2.0 * decay_ref[...]
    series = jnp.ones_like(y)
    for n in range(10, 1, -1):
        series = 1.0 - y * (1.0 / n) * series
    scale = jnp.sqrt(y * series)
    weight = (res_ref[0] * scale, res_ref[1] * scale)
    weight_ref[:MODES, :] = weight[0]
    weight_ref[MODES:, :] = weight[1]
    for g in range(GROUPS):
        lanes = slice(g * LANES, (g + 1) * LANES)
        w_re, w_im = weight[0][:, lanes], weight[1][:, lanes]
        for k in range(STEPS):
            term = w_re * tre[g, k * MODES:(k + 1) * MODES, :] - w_im * tim[g, k * MODES:(k + 1) * MODES, :]
            row = jnp.sum(term, axis=0, keepdims=True)
            if k == 0:
                row = row + skip_ref[:, lanes]
            taps[g, k:k + 1, :] = row

    def group(g, unused):
        tile = 8

        def fir(select):
            xs = []
            for j in range(STEPS):
                x = sig[g, pl.ds(j, BLOCKS, stride=STEPS), :]
                late = (blocks * STEPS + j >= s0) | (blocks != b0)
                xs.append(jnp.where(late if select else jnp.logical_not(late), x, 0.0))
            for top in range(0, STEPS, tile):
                acc = [jnp.zeros((BLOCKS, LANES), F32)] * tile
                for k in range(top + tile):
                    tap = taps[g, k:k + 1, :]
                    for i in range(tile):
                        if top + i - k >= 0:
                            acc[i] = acc[i] + tap * xs[top + i - k]
                for i in range(tile):
                    if select:
                        y_ref[g, top + i] = acc[i]
                    else:
                        early = (blocks * STEPS + top + i < s0) & (blocks == b0)
                        y_ref[g, top + i] = y_ref[g, top + i] + jnp.where(early, acc[i], 0.0)

        fir(True)
        fir(False)
        return unused

    lax.fori_loop(0, GROUPS, group, 0)


def carry_kernel(eb_ref, tre, tim, weight_ref, starts_ref, wy_ref, pz_ref, gz_ref, later_ref, qre, qim, rows_):
    later_ref[...] = wy_ref[...]
    s0 = first_start(starts_ref)
    b0 = s0 // STEPS
    blocks = block_iota()
    weight = (weight_ref[:MODES, :], weight_ref[MODES:, :])
    q = last_power(tre, tim)
    value = weight
    for n in range(BLOCKS):
        for g in range(GROUPS):
            lanes = slice(g * LANES, (g + 1) * LANES)
            qre[g, n * MODES:(n + 1) * MODES, :] = value[0][:, lanes]
            qim[g, n * MODES:(n + 1) * MODES, :] = value[1][:, lanes]
        value = cmul(value, q)
    power = q
    for n in range(3):
        for g in range(GROUPS):
            lanes = slice(g * LANES, (g + 1) * LANES)
            rows_[g, n * ROWS:n * ROWS + MODES, :] = power[0][:, lanes]
            rows_[g, n * ROWS + MODES:(n + 1) * ROWS, :] = power[1][:, lanes]
        power = square(power)
    for g in range(GROUPS):
        lanes = slice(g * LANES, (g + 1) * LANES)
        rows_[g, 3 * ROWS:3 * ROWS + MODES, :] = weight[0][:, lanes]
        rows_[g, 3 * ROWS + MODES:4 * ROWS, :] = weight[1][:, lanes]

    keeps = []
    for n in range(3):
        s = 1 << n
        keeps.append((blocks >= s) & jnp.logical_not((blocks - s < b0) & (b0 <= blocks)))
    heard = blocks <= b0

    def group(g, unused):
        for m in range(MODES):
            state = (eb_ref[g, m], eb_ref[g, MODES + m])
            for n in range(3):
                moved = [jnp.where(keeps[n], pltpu.roll(part, 1 << n, 0), 0.0) for part in state]
                step = (rows_[g, n * ROWS + m:n * ROWS + m + 1, :],
                        rows_[g, n * ROWS + MODES + m:n * ROWS + MODES + m + 1, :])
                state = cadd(state, cmul(step, moved))
            before = [jnp.where(blocks >= 1, pltpu.roll(part, 1, 0), 0.0) for part in state]
            w = (rows_[g, 3 * ROWS + m:3 * ROWS + m + 1, :],
                 rows_[g, 3 * ROWS + MODES + m:3 * ROWS + MODES + m + 1, :])
            scaled = cmul(w, before)
            pz_ref[g, m] = scaled[0]
            pz_ref[g, MODES + m] = scaled[1]
            gz_ref[g, m] = jnp.where(heard, qre[g, pl.ds(m, BLOCKS, stride=MODES), :], 0.0)
            gz_ref[g, MODES + m] = jnp.where(heard, qim[g, pl.ds(m, BLOCKS, stride=MODES), :], 0.0)

        return unused

    lax.fori_loop(0, GROUPS, group, 0)


def put_state(ref, state, thru):
    for part, at in zip(state, (0, MODES)):
        high = part.astype(BF16)
        ref[at:at + MODES, :] = high
        ref[ROWS + at:ROWS + at + MODES, :] = (part - high.astype(F32)).astype(BF16)
    ref[2 * ROWS:SENT, :] = jnp.broadcast_to(thru, (FLAG, CH)).astype(BF16)


def get_state(ref):
    parts = [ref[at:at + MODES, :].astype(F32) + ref[ROWS + at:ROWS + at + MODES, :].astype(F32)
             for at in (0, MODES)]
    return parts, ref[2 * ROWS:2 * ROWS + 8, :].astype(F32)[:1]


def chip_kernel(own_ref, other_ref, p256_ref, weight_ref, sent_ref):
    core = lax.axis_index("ctx") % NC
    first = (core == 0).astype(F32)
    own, other = halves(own_ref), halves(other_ref)
    own_thru, other_thru = own_ref[ROWS:ROWS + 1, :], other_ref[ROWS:ROWS + 1, :]
    early = [first * a + (1.0 - first) * b for a, b in zip(own, other)]
    late = [first * b + (1.0 - first) * a for a, b in zip(own, other)]
    late_thru = first * other_thru + (1.0 - first) * own_thru
    moved = cmul(halves(p256_ref), early)
    put_state(sent_ref, [late_thru * a + b for a, b in zip(moved, late)], own_thru * other_thru)
    sent_ref[SENT:, :] = weight_ref[...]


def row_kernel(own_ref, one_ref, two_ref, three_ref, p256_ref, pay_ref, before_ref, factor_ref, wy_ref,
               held):
    mine = (lax.axis_index("ctx") // NC) % NY
    for k, ref in enumerate((own_ref, one_ref, two_ref, three_ref)):
        there = lax.rem(mine - k + NY, NY)
        state, thru = get_state(ref)
        held[there, :MODES, :] = state[0]
        held[there, MODES:ROWS, :] = state[1]
        held[there, ROWS:, :] = jnp.broadcast_to(thru, (PAY - ROWS, CH))
        wy_ref[pl.ds(pl.multiple_of(there * WROWS, WROWS), WROWS), :] = ref[SENT:, :]
    p512 = square(halves(p256_ref))
    state = (jnp.zeros((MODES, CH), F32),) * 2
    factor = (jnp.ones((MODES, CH), F32), jnp.zeros((MODES, CH), F32))
    thru = jnp.ones((1, CH), F32)
    for i in range(NY):
        @pl.when(mine == i)
        def put(state=state, factor=factor):
            before_ref[:MODES, :] = state[0]
            before_ref[MODES:, :] = state[1]
            factor_ref[:MODES, :] = factor[0]
            factor_ref[MODES:, :] = factor[1]
        open_ = held[i, ROWS:ROWS + 1, :]
        step = (open_ * p512[0], open_ * p512[1])
        state = cadd(cmul(step, state), (held[i, :MODES, :], held[i, MODES:ROWS, :]))
        factor = cmul(step, factor)
        thru = thru * open_
    pay_ref[:MODES, :] = state[0]
    pay_ref[MODES:ROWS, :] = state[1]
    pay_ref[ROWS:, :] = jnp.broadcast_to(thru, (PAY - ROWS, CH))


def gate_kernel(query_ref, y_ref, pz_ref, gz_ref, tre, tim, starts_ref, own_ref, other_ref, p256_ref,
                before_ref, factor_ref, one_ref, two_ref, hidden_ref, conv, sin):
    index = lax.axis_index("ctx")
    core, row = index % NC, index // (NC * NY)
    p256 = halves(p256_ref)
    p2048 = square(square(square(p256)))
    has_one = (row >= 1).astype(F32)
    has_two = (row >= 2).astype(F32)
    far = cmul(p2048, halves(two_ref))
    open_one = has_two * one_ref[ROWS:ROWS + 1, :]
    incoming = [has_one * a + open_one * b for a, b in zip(halves(one_ref), far)]
    state = cadd(halves(before_ref), cmul(halves(factor_ref), incoming))
    second = (core == 1).astype(F32)
    moved = cmul(p256, state)
    early_thru = other_ref[ROWS:ROWS + 1, :]
    state = [(1.0 - second) * a + second * (early_thru * b + c)
             for a, b, c in zip(state, moved, halves(other_ref))]
    for g in range(GROUPS):
        lanes = slice(g * LANES, (g + 1) * LANES)
        sin[g, :MODES, :] = state[0][:, lanes]
        sin[g, MODES:, :] = state[1][:, lanes]
    s0 = first_start(starts_ref)
    b0 = s0 // STEPS
    blocks = block_iota()

    def group(g, unused):
        z = []
        for m in range(MODES):
            s = (sin[g, m:m + 1, :], sin[g, MODES + m:MODES + m + 1, :])
            z.append(cadd((pz_ref[g, m], pz_ref[g, MODES + m]),
                          cmul((gz_ref[g, m], gz_ref[g, MODES + m]), s)))

        def step(j, unused):
            base = (j + 1) * MODES
            total = [None] * 4
            for m in range(MODES):
                term = tre[g, pl.ds(base + m, 1), :] * z[m][0] - tim[g, pl.ds(base + m, 1), :] * z[m][1]
                total[m % 4] = term if total[m % 4] is None else total[m % 4] + term
            total = (total[0] + total[1]) + (total[2] + total[3])
            late = (blocks * STEPS + j >= s0) & (blocks == b0)
            conv[g, pl.ds(j, BLOCKS, stride=STEPS), :] = y_ref[g, j] + jnp.where(late, 0.0, total)
            return unused

        return lax.fori_loop(0, STEPS, step, unused, unroll=4)

    lax.fori_loop(0, GROUPS, group, 0)
    for g in range(GROUPS):
        lanes = slice(g * LANES, (g + 1) * LANES)
        hidden_ref[:, lanes] = (query_ref[:, lanes].astype(F32) * conv[g]).astype(BF16)


def weight_kernel(token_ref, *refs):
    pieces, out_ref = refs[:NX], refs[NX]
    x = lax.axis_index("ctx") // (NC * NY)
    for dx in range(NX):
        there = lax.rem(x - dx + NX, NX)
        rows = pl.ds(pl.multiple_of(there * NY * WROWS, NY * WROWS), NY * WROWS)
        out_ref[rows, :] = pieces[dx][...]


def relay_kernel(up1, down1, up2, down2, up2_ref, down2_ref, top_ref, bottom_ref, token_ref):
    half = TOK // 2
    up2_ref[...] = up2[...]
    down2_ref[...] = down2[...]
    top_ref[...] = up2[:half, :]
    bottom_ref[...] = down2[half:, :]
    token_ref[...] = up1[:16, :LANES] + down1[:16, :LANES]


def project(z, hidden, own_ref, other_ref):
    core = lax.axis_index("ctx") % NC
    rows = pl.ds(pl.multiple_of(z * 2 * WROWS, 2 * WROWS), 2 * WROWS)
    total = None
    for side, weight_ref in ((core, own_ref), (1 - core, other_ref)):
        lanes = [pl.ds(pl.multiple_of((2 * h + side) * WROWS, WROWS), WROWS) for h in range(2)]
        part = jnp.concatenate([hidden[:, at] for at in lanes], axis=1)
        term = jnp.dot(part, weight_ref[rows, :], preferred_element_type=F32)
        total = term if total is None else total + term
    return total


def near_kernel(here, up1, down1, up2, down2, own_ref, other_ref, out_ref):
    z = lax.axis_index("tp")
    total = None
    for k, ref in ((0, here), (1, up1), (-1, down1), (2, up2), (-2, down2)):
        term = project(lax.rem(z - k + NZ, NZ), ref, own_ref, other_ref)
        total = term if total is None else total + term
    out_ref[...] = total


def far_kernel(near_ref, up3, down3, up4, down4, own_ref, other_ref, out_ref, last):
    z = lax.axis_index("tp")
    half = TOK // 2
    last[:half, :] = up4[...]
    last[half:, :] = down4[...]
    total = near_ref[...]
    for k, ref in ((3, up3), (-3, down3), (4, last)):
        total = total + project(lax.rem(z - k + NZ, NZ), ref, own_ref, other_ref)
    out_ref[...] = total.astype(BF16)


def ctx_index(x, y, c):
    return ((x % NX) * NY + y % NY) * NC + c % NC


def move(value, dx, dy, dc):
    pairs = [(ctx_index(x, y, c), ctx_index(x + dx, y + dy, c + dc))
             for x in range(NX) for y in range(NY) for c in range(NC)]
    return lax.ppermute(value, "ctx", pairs)


def turn(value, k):
    return lax.ppermute(value, "tp", [(i, (i + k) % NZ) for i in range(NZ)])


def shards(query, key, value, decay, freq, residue, skip, out_weight, doc_starts):
    starts = doc_starts.reshape(TOK // LANES, LANES)
    skip = skip.reshape(1, CH)
    sig = pltpu.VMEM((GROUPS, TOK, LANES), F32)
    qs = pltpu.VMEM((GROUPS, BLOCKS * MODES, LANES), F32)
    state_shape = struct(ROWS, CH)
    pay_shape = struct(PAY, CH)
    block_shape = struct(GROUPS, ROWS, BLOCKS, LANES)
    table = (GROUPS, (STEPS + 1) * MODES, LANES)

    magnitude = jnp.exp(-decay)
    q_shape = struct(GROUPS, BLOCKS * MODES, LANES)
    tre, tim, qre, qim, p256 = call(
        powers_kernel, (struct(*table), struct(*table), q_shape, q_shape, state_shape),
        (magnitude * jnp.cos(freq), magnitude * jnp.sin(freq)), (), 2_000_000_000, 5_000_000)
    pay, eb, signal = call(
        ends_kernel, (pay_shape, block_shape, struct(GROUPS, TOK, LANES)),
        (key, value, starts, tre, tim, qre, qim), (), 20_000_000, 5_000_000)
    other = move(pay, 0, 0, 1)
    chip = call(chip_kernel, struct(SENT + WROWS, CH, dtype=BF16), (pay, other, p256, out_weight))
    near = [move(chip, 0, k, 0) for k in (1, 2, 3)]
    y, gain = call(
        local_kernel, (struct(GROUPS, STEPS, BLOCKS, LANES), state_shape),
        (signal, tre, tim, decay, residue, skip, starts),
        [pltpu.VMEM((GROUPS, STEPS, LANES), F32)], 30_000_000, 5_000_000)
    row, before, factor, wy = call(
        row_kernel, (pay_shape, state_shape, state_shape, struct(NY * WROWS, CH, dtype=BF16)),
        (chip, *near, p256), [pltpu.VMEM((NY, PAY, CH), F32)])
    back = [move(row, k, 0, 0) for k in (1, 2)]
    pz, gz, wy = call(
        carry_kernel, (block_shape, block_shape, struct(NY * WROWS, CH, dtype=BF16)),
        (eb, tre, tim, gain, starts, wy),
        [qs, qs, pltpu.VMEM((GROUPS, 4 * ROWS, LANES), F32)], 30_000_000, 5_000_000)
    wx = [wy] + [move(wy, k, 0, 0) for k in (1, 2, 3)]
    hidden = call(
        gate_kernel, struct(TOK, CH, dtype=BF16),
        (query, y, pz, gz, tre, tim, starts, pay, other, p256, before, factor, *back),
        [sig, pltpu.VMEM((GROUPS, ROWS, LANES), F32)], 20_000_000, 5_000_000)

    full, part = struct(TOK, CH, dtype=BF16), struct(TOK // 2, CH, dtype=BF16)
    up1, down1, up2, down2 = turn(hidden, 1), turn(hidden, -1), turn(hidden, 2), turn(hidden, -2)
    up2, down2, top, bottom, token = call(
        relay_kernel, (full, full, part, part, struct(16, LANES, dtype=BF16)), (up1, down1, up2, down2))
    up3, down3 = turn(up2, 1), turn(down2, -1)
    up4, down4 = turn(top, 2), turn(bottom, -2)
    own = call(weight_kernel, struct(NZ * CH // 2, CH, dtype=BF16), (move(token, 0, 0, 1), *wx), (), 0, 4_000_000)
    swapped = move(own, 0, 0, 1)
    total = call(near_kernel, struct(TOK, CH), (hidden, up1, down1, up2, down2, own, swapped), (),
                 5 * 2 * TOK * CH * CH, 4_000_000)
    return call(far_kernel, full, (total, up3, down3, up4, down4, own, swapped),
                [pltpu.VMEM((TOK, CH), BF16)], 3 * 2 * TOK * CH * CH, 4_000_000)


def solution(mesh):
    in_specs = (
        P("ctx", "tp"),
        P("ctx", "tp"),
        P("ctx", "tp"),
        P(None, "tp"),
        P(None, "tp"),
        P(None, None, "tp"),
        P("tp"),
        P("ctx", "tp"),
        P("ctx"),
    )
    return jax.shard_map(
        shards, mesh=mesh, in_specs=in_specs, out_specs=P("ctx", "tp"), check_vma=False
    )
```

```python
import jax
import jax.numpy as jnp
from jax import lax
from jax.experimental import pallas as pl
from jax.experimental.pallas import tpu as pltpu
from jax.sharding import PartitionSpec as P

F32 = jnp.float32
BF16 = jnp.bfloat16
NX, NY, NC, NZ = 4, 4, 2, 8
TOK, CH, MODES = 256, 512, 16
LANES = 128
GROUPS = CH // LANES
STEPS = 32
BLOCKS = TOK // STEPS
ROWS = 2 * MODES
PAY = ROWS + 8
VMEM = pl.BlockSpec(memory_space=pltpu.VMEM)
FLAG = 16
SENT = 2 * ROWS + FLAG
WROWS = 128
PARAMS = pltpu.CompilerParams(vmem_limit_bytes=48 * 1024 * 1024)


def call(kernel, outs, args, scratch=(), flops=0, nbytes=0):
    return pl.pallas_call(
        kernel,
        out_shape=outs,
        in_specs=[VMEM] * len(args),
        out_specs=jax.tree.map(lambda unused: VMEM, outs),
        scratch_shapes=list(scratch),
        compiler_params=PARAMS,
        cost_estimate=pl.CostEstimate(flops=flops, bytes_accessed=nbytes, transcendentals=0),
    )(*args)


def struct(*shape, dtype=F32):
    return jax.ShapeDtypeStruct(shape, dtype)


def cmul(a, b):
    return a[0] * b[0] - a[1] * b[1], a[0] * b[1] + a[1] * b[0]


def cadd(a, b):
    return a[0] + b[0], a[1] + b[1]


def square(a):
    return a[0] * a[0] - a[1] * a[1], 2.0 * a[0] * a[1]


def halves(ref):
    return ref[:MODES, :], ref[MODES:ROWS, :]


def first_start(starts_ref):
    starts = starts_ref[...]
    at = lax.broadcasted_iota(jnp.int32, starts.shape, 0) * LANES
    at = at + lax.broadcasted_iota(jnp.int32, starts.shape, 1)
    where = jnp.where(starts > 0, at, TOK)
    return jnp.min(jnp.min(where, axis=1, keepdims=True), axis=0, keepdims=True)


def fill_powers(pole, table_re, table_im, count):
    def put(k, value):
        for g in range(GROUPS):
            rows = pl.ds(pl.multiple_of(k * MODES, MODES), MODES)
            lanes = slice(g * LANES, (g + 1) * LANES)
            table_re[g, rows, :] = value[0][:, lanes]
            table_im[g, rows, :] = value[1][:, lanes]

    def step(k, value):
        put(k, value)
        return cmul(value, pole)

    one = (jnp.ones((MODES, CH), F32), jnp.zeros((MODES, CH), F32))
    last = lax.fori_loop(0, count, step, one)
    return last


def fill_signal(key_ref, value_ref, sig):
    for g in range(GROUPS):
        lanes = slice(g * LANES, (g + 1) * LANES)
        sig[g] = key_ref[:, lanes].astype(F32) * value_ref[:, lanes].astype(F32)


def block_iota():
    return lax.broadcasted_iota(jnp.int32, (BLOCKS, LANES), 0)


def powers_kernel(pole_re, pole_im, tre, tim, qre, qim, p256_ref):
    fill_powers((pole_re[...], pole_im[...]), tre, tim, STEPS + 1)
    q = last_power(tre, tim)
    value = (jnp.ones((MODES, CH), F32), jnp.zeros((MODES, CH), F32))
    for n in range(BLOCKS):
        row = (BLOCKS - 1 - n) * MODES
        for g in range(GROUPS):
            lanes = slice(g * LANES, (g + 1) * LANES)
            qre[g, row:row + MODES, :] = value[0][:, lanes]
            qim[g, row:row + MODES, :] = value[1][:, lanes]
        value = cmul(value, q)
    p256_ref[:MODES, :] = value[0]
    p256_ref[MODES:, :] = value[1]


def ends_kernel(key_ref, value_ref, starts_ref, tre, tim, qre, qim, pay_ref, eb_ref, sig):
    s0 = first_start(starts_ref)
    b0 = s0 // STEPS
    fill_signal(key_ref, value_ref, sig)
    blocks = block_iota()
    reach = (s0 >= TOK) | (blocks >= b0)

    def group(g, unused):
        def step(j, acc):
            x = sig[g, pl.ds(j, BLOCKS, stride=STEPS), :]
            x = jnp.where((blocks * STEPS + j >= s0) | (blocks != b0), x, 0.0)
            base = (STEPS - 1 - j) * MODES
            out = []
            for m in range(MODES):
                out.append(acc[2 * m] + tre[g, pl.ds(base + m, 1), :] * x)
                out.append(acc[2 * m + 1] + tim[g, pl.ds(base + m, 1), :] * x)
            return tuple(out)

        zero = jnp.zeros((BLOCKS, LANES), F32)
        acc = lax.fori_loop(0, STEPS, step, (zero,) * ROWS, unroll=4)
        for m in range(MODES):
            re, im = acc[2 * m], acc[2 * m + 1]
            eb_ref[g, m] = re
            eb_ref[g, MODES + m] = im
            w = (qre[g, pl.ds(m, BLOCKS, stride=MODES), :], qim[g, pl.ds(m, BLOCKS, stride=MODES), :])
            end = cmul(w, (re, im))
            lanes = pl.ds(pl.multiple_of(g * LANES, LANES), LANES)
            pay_ref[pl.ds(m, 1), lanes] = jnp.sum(jnp.where(reach, end[0], 0.0), axis=0, keepdims=True)
            pay_ref[pl.ds(MODES + m, 1), lanes] = jnp.sum(jnp.where(reach, end[1], 0.0), axis=0, keepdims=True)
        return unused

    lax.fori_loop(0, GROUPS, group, 0)
    pay_ref[ROWS:, :] = jnp.broadcast_to((s0 >= TOK).astype(F32), (PAY - ROWS, CH))


def last_power(tre, tim):
    return [jnp.concatenate([t[g, STEPS * MODES:, :] for g in range(GROUPS)], axis=1) for t in (tre, tim)]


def local_kernel(sig, tre, tim, decay_ref, res_ref, skip_ref, starts_ref, y_ref, weight_ref, taps):
    s0 = first_start(starts_ref)
    b0 = s0 // STEPS
    blocks = block_iota()
    y = 2.0 * decay_ref[...]
    series = jnp.ones_like(y)
    for n in range(10, 1, -1):
        series = 1.0 - y * (1.0 / n) * series
    scale = jnp.sqrt(y * series)
    weight = (res_ref[0] * scale, res_ref[1] * scale)
    weight_ref[:MODES, :] = weight[0]
    weight_ref[MODES:, :] = weight[1]
    for g in range(GROUPS):
        lanes = slice(g * LANES, (g + 1) * LANES)
        w_re, w_im = weight[0][:, lanes], weight[1][:, lanes]
        for k in range(STEPS):
            term = w_re * tre[g, k * MODES:(k + 1) * MODES, :] - w_im * tim[g, k * MODES:(k + 1) * MODES, :]
            row = jnp.sum(term, axis=0, keepdims=True)
            if k == 0:
                row = row + skip_ref[:, lanes]
            taps[g, k:k + 1, :] = row

    def group(g, unused):
        tile = 8

        def fir(select):
            xs = []
            for j in range(STEPS):
                x = sig[g, pl.ds(j, BLOCKS, stride=STEPS), :]
                late = (blocks * STEPS + j >= s0) | (blocks != b0)
                xs.append(jnp.where(late if select else jnp.logical_not(late), x, 0.0))
            for top in range(0, STEPS, tile):
                acc = [jnp.zeros((BLOCKS, LANES), F32)] * tile
                for k in range(top + tile):
                    tap = taps[g, k:k + 1, :]
                    for i in range(tile):
                        if top + i - k >= 0:
                            acc[i] = acc[i] + tap * xs[top + i - k]
                for i in range(tile):
                    if select:
                        y_ref[g, top + i] = acc[i]
                    else:
                        early = (blocks * STEPS + top + i < s0) & (blocks == b0)
                        y_ref[g, top + i] = y_ref[g, top + i] + jnp.where(early, acc[i], 0.0)

        fir(True)
        fir(False)
        return unused

    lax.fori_loop(0, GROUPS, group, 0)


def carry_kernel(eb_ref, tre, tim, weight_ref, starts_ref, after_ref,
                 pz_ref, gz_ref, qre, qim, rows_):
    s0 = first_start(starts_ref)
    b0 = s0 // STEPS
    blocks = block_iota()
    weight = (weight_ref[:MODES, :], weight_ref[MODES:, :])
    q = last_power(tre, tim)
    value = weight
    for n in range(BLOCKS):
        for g in range(GROUPS):
            lanes = slice(g * LANES, (g + 1) * LANES)
            qre[g, n * MODES:(n + 1) * MODES, :] = value[0][:, lanes]
            qim[g, n * MODES:(n + 1) * MODES, :] = value[1][:, lanes]
        value = cmul(value, q)
    power = q
    for n in range(3):
        for g in range(GROUPS):
            lanes = slice(g * LANES, (g + 1) * LANES)
            rows_[g, n * ROWS:n * ROWS + MODES, :] = power[0][:, lanes]
            rows_[g, n * ROWS + MODES:(n + 1) * ROWS, :] = power[1][:, lanes]
        power = square(power)
    for g in range(GROUPS):
        lanes = slice(g * LANES, (g + 1) * LANES)
        rows_[g, 3 * ROWS:3 * ROWS + MODES, :] = weight[0][:, lanes]
        rows_[g, 3 * ROWS + MODES:4 * ROWS, :] = weight[1][:, lanes]

    keeps = []
    for n in range(3):
        s = 1 << n
        keeps.append((blocks >= s) & jnp.logical_not((blocks - s < b0) & (b0 <= blocks)))
    heard = blocks <= b0

    def group(g, unused):
        for m in range(MODES):
            state = (eb_ref[g, m], eb_ref[g, MODES + m])
            for n in range(3):
                moved = [jnp.where(keeps[n], pltpu.roll(part, 1 << n, 0), 0.0) for part in state]
                step = (rows_[g, n * ROWS + m:n * ROWS + m + 1, :],
                        rows_[g, n * ROWS + MODES + m:n * ROWS + MODES + m + 1, :])
                state = cadd(state, cmul(step, moved))
            before = [jnp.where(blocks >= 1, pltpu.roll(part, 1, 0), 0.0) for part in state]
            w = (rows_[g, 3 * ROWS + m:3 * ROWS + m + 1, :],
                 rows_[g, 3 * ROWS + MODES + m:3 * ROWS + MODES + m + 1, :])
            scaled = cmul(w, before)
            pz_ref[g, m] = scaled[0]
            pz_ref[g, MODES + m] = scaled[1]
            gz_ref[g, m] = jnp.where(heard, qre[g, pl.ds(m, BLOCKS, stride=MODES), :], 0.0)
            gz_ref[g, MODES + m] = jnp.where(heard, qim[g, pl.ds(m, BLOCKS, stride=MODES), :], 0.0)

        return unused

    lax.fori_loop(0, GROUPS, group, 0)


def put_state(ref, state, thru):
    for part, at in zip(state, (0, MODES)):
        high = part.astype(BF16)
        ref[at:at + MODES, :] = high
        ref[ROWS + at:ROWS + at + MODES, :] = (part - high.astype(F32)).astype(BF16)
    ref[2 * ROWS:SENT, :] = jnp.broadcast_to(thru, (FLAG, CH)).astype(BF16)


def get_state(ref):
    parts = [ref[at:at + MODES, :].astype(F32) + ref[ROWS + at:ROWS + at + MODES, :].astype(F32)
             for at in (0, MODES)]
    return parts, ref[2 * ROWS:2 * ROWS + 8, :].astype(F32)[:1]


def chip_kernel(own_ref, other_ref, p256_ref, sent_ref):
    core = lax.axis_index("ctx") % NC
    first = (core == 0).astype(F32)
    own, other = halves(own_ref), halves(other_ref)
    own_thru, other_thru = own_ref[ROWS:ROWS + 1, :], other_ref[ROWS:ROWS + 1, :]
    early = [first * a + (1.0 - first) * b for a, b in zip(own, other)]
    late = [first * b + (1.0 - first) * a for a, b in zip(own, other)]
    late_thru = first * other_thru + (1.0 - first) * own_thru
    moved = cmul(halves(p256_ref), early)
    put_state(sent_ref, [late_thru * a + b for a, b in zip(moved, late)], own_thru * other_thru)


def row_kernel(own_ref, one_ref, two_ref, three_ref, p256_ref, pay_ref, before_ref, factor_ref, held):
    mine = (lax.axis_index("ctx") // NC) % NY
    for k, ref in enumerate((own_ref, one_ref, two_ref, three_ref)):
        there = lax.rem(mine - k + NY, NY)
        state, thru = get_state(ref)
        held[there, :MODES, :] = state[0]
        held[there, MODES:ROWS, :] = state[1]
        held[there, ROWS:, :] = jnp.broadcast_to(thru, (PAY - ROWS, CH))
    p512 = square(halves(p256_ref))
    state = (jnp.zeros((MODES, CH), F32),) * 2
    factor = (jnp.ones((MODES, CH), F32), jnp.zeros((MODES, CH), F32))
    thru = jnp.ones((1, CH), F32)
    for i in range(NY):
        @pl.when(mine == i)
        def put(state=state, factor=factor):
            before_ref[:MODES, :] = state[0]
            before_ref[MODES:, :] = state[1]
            factor_ref[:MODES, :] = factor[0]
            factor_ref[MODES:, :] = factor[1]
        open_ = held[i, ROWS:ROWS + 1, :]
        step = (open_ * p512[0], open_ * p512[1])
        state = cadd(cmul(step, state), (held[i, :MODES, :], held[i, MODES:ROWS, :]))
        factor = cmul(step, factor)
        thru = thru * open_
    pay_ref[:MODES, :] = state[0]
    pay_ref[MODES:ROWS, :] = state[1]
    pay_ref[ROWS:, :] = jnp.broadcast_to(thru, (PAY - ROWS, CH))


def gate_kernel(query_ref, y_ref, pz_ref, gz_ref, tre, tim, starts_ref, own_ref, other_ref, p256_ref,
                before_ref, factor_ref, one_ref, two_ref, hidden_ref, conv, sin):
    index = lax.axis_index("ctx")
    core, row = index % NC, index // (NC * NY)
    p256 = halves(p256_ref)
    p2048 = square(square(square(p256)))
    has_one = (row >= 1).astype(F32)
    has_two = (row >= 2).astype(F32)
    far = cmul(p2048, halves(two_ref))
    open_one = has_two * one_ref[ROWS:ROWS + 1, :]
    incoming = [has_one * a + open_one * b for a, b in zip(halves(one_ref), far)]
    state = cadd(halves(before_ref), cmul(halves(factor_ref), incoming))
    second = (core == 1).astype(F32)
    moved = cmul(p256, state)
    early_thru = other_ref[ROWS:ROWS + 1, :]
    state = [(1.0 - second) * a + second * (early_thru * b + c)
             for a, b, c in zip(state, moved, halves(other_ref))]
    for g in range(GROUPS):
        lanes = slice(g * LANES, (g + 1) * LANES)
        sin[g, :MODES, :] = state[0][:, lanes]
        sin[g, MODES:, :] = state[1][:, lanes]
    s0 = first_start(starts_ref)
    b0 = s0 // STEPS
    blocks = block_iota()

    def group(g, unused):
        z = []
        for m in range(MODES):
            s = (sin[g, m:m + 1, :], sin[g, MODES + m:MODES + m + 1, :])
            z.append(cadd((pz_ref[g, m], pz_ref[g, MODES + m]),
                          cmul((gz_ref[g, m], gz_ref[g, MODES + m]), s)))

        def step(j, unused):
            base = (j + 1) * MODES
            total = [None] * 4
            for m in range(MODES):
                term = tre[g, pl.ds(base + m, 1), :] * z[m][0] - tim[g, pl.ds(base + m, 1), :] * z[m][1]
                total[m % 4] = term if total[m % 4] is None else total[m % 4] + term
            total = (total[0] + total[1]) + (total[2] + total[3])
            late = (blocks * STEPS + j >= s0) & (blocks == b0)
            conv[g, pl.ds(j, BLOCKS, stride=STEPS), :] = y_ref[g, j] + jnp.where(late, 0.0, total)
            return unused

        return lax.fori_loop(0, STEPS, step, unused, unroll=4)

    lax.fori_loop(0, GROUPS, group, 0)
    for g in range(GROUPS):
        lanes = slice(g * LANES, (g + 1) * LANES)
        hidden_ref[:, lanes] = (query_ref[:, lanes].astype(F32) * conv[g]).astype(BF16)


def relay_kernel(up1, down1, up2, down2, up2_ref, down2_ref, top_ref, bottom_ref):
    half = TOK // 2
    up2_ref[...] = up2[...]
    down2_ref[...] = down2[...]
    top_ref[...] = up2[:half, :]
    bottom_ref[...] = down2[half:, :]


def project_kernel(here, up1, down1, up2, down2, up3, down3, up4, down4, weight_ref, out_ref, last):
    z = lax.axis_index("tp")
    half = TOK // 2
    last[:half, :] = up4[...]
    last[half:, :] = down4[...]
    total = None
    for k, hidden in enumerate((here, up1, up2, up3, last, down3, down2, down1)):
        rows = pl.ds(pl.multiple_of(lax.rem(z - k + NZ, NZ) * CH, CH), CH)
        term = jnp.dot(hidden[...], weight_ref[rows, :], preferred_element_type=F32)
        total = term if total is None else total + term
    out_ref[...] = total.astype(BF16)


def ctx_index(x, y, c):
    return ((x % NX) * NY + y % NY) * NC + c % NC


def move(value, dx, dy, dc):
    pairs = [(ctx_index(x, y, c), ctx_index(x + dx, y + dy, c + dc))
             for x in range(NX) for y in range(NY) for c in range(NC)]
    return lax.ppermute(value, "ctx", pairs)


def turn(value, k):
    return lax.ppermute(value, "tp", [(i, (i + k) % NZ) for i in range(NZ)])


def shards(query, key, value, decay, freq, residue, skip, out_weight, doc_starts):
    starts = doc_starts.reshape(TOK // LANES, LANES)
    skip = skip.reshape(1, CH)
    sig = pltpu.VMEM((GROUPS, TOK, LANES), F32)
    qs = pltpu.VMEM((GROUPS, BLOCKS * MODES, LANES), F32)
    state_shape = struct(ROWS, CH)
    pay_shape = struct(PAY, CH)
    block_shape = struct(GROUPS, ROWS, BLOCKS, LANES)
    table = (GROUPS, (STEPS + 1) * MODES, LANES)

    weight = lax.all_gather(out_weight, "ctx", axis=0, tiled=True)
    magnitude = jnp.exp(-decay)
    q_shape = struct(GROUPS, BLOCKS * MODES, LANES)
    tre, tim, qre, qim, p256 = call(
        powers_kernel, (struct(*table), struct(*table), q_shape, q_shape, state_shape),
        (magnitude * jnp.cos(freq), magnitude * jnp.sin(freq)), (), 2_000_000_000, 5_000_000)
    pay, eb, signal = call(
        ends_kernel, (pay_shape, block_shape, struct(GROUPS, TOK, LANES)),
        (key, value, starts, tre, tim, qre, qim), (), 20_000_000, 5_000_000)
    other = move(pay, 0, 0, 1)
    chip = call(chip_kernel, struct(SENT, CH, dtype=BF16), (pay, other, p256))
    near = [move(chip, 0, k, 0) for k in (1, 2, 3)]
    y, gain = call(
        local_kernel, (struct(GROUPS, STEPS, BLOCKS, LANES), state_shape),
        (signal, tre, tim, decay, residue, skip, starts),
        [pltpu.VMEM((GROUPS, STEPS, LANES), F32)], 30_000_000, 5_000_000)
    row, before, factor = call(
        row_kernel, (pay_shape, state_shape, state_shape),
        (chip, *near, p256), [pltpu.VMEM((NY, PAY, CH), F32)])
    back = [move(row, k, 0, 0) for k in (1, 2)]
    pz, gz = call(
        carry_kernel, (block_shape, block_shape), (eb, tre, tim, gain, starts, row),
        [qs, qs, pltpu.VMEM((GROUPS, 4 * ROWS, LANES), F32)], 30_000_000, 5_000_000)
    hidden = call(
        gate_kernel, struct(TOK, CH, dtype=BF16),
        (query, y, pz, gz, tre, tim, starts, pay, other, p256, before, factor, *back),
        [sig, pltpu.VMEM((GROUPS, ROWS, LANES), F32)], 20_000_000, 5_000_000)

    full, part = struct(TOK, CH, dtype=BF16), struct(TOK // 2, CH, dtype=BF16)
    up1, down1, up2, down2 = turn(hidden, 1), turn(hidden, -1), turn(hidden, 2), turn(hidden, -2)
    up2, down2, top, bottom = call(relay_kernel, (full, full, part, part), (up1, down1, up2, down2))
    up3, down3 = turn(up2, 1), turn(down2, -1)
    up4, down4 = turn(top, 2), turn(bottom, -2)
    return call(
        project_kernel, full,
        (hidden, up1, down1, up2, down2, up3, down3, up4, down4, weight),
        [pltpu.VMEM((TOK, CH), BF16)], 2 * TOK * CH * CH * NZ, 7_000_000)


def solution(mesh):
    in_specs = (
        P("ctx", "tp"),
        P("ctx", "tp"),
        P("ctx", "tp"),
        P(None, "tp"),
        P(None, "tp"),
        P(None, None, "tp"),
        P("tp"),
        P("ctx", "tp"),
        P("ctx"),
    )
    return jax.shard_map(
        shards, mesh=mesh, in_specs=in_specs, out_specs=P("ctx", "tp"), check_vma=False
    )
```

```python
import jax
import jax.numpy as jnp
from jax import lax
from jax.experimental import pallas as pl
from jax.experimental.pallas import tpu as pltpu
from jax.sharding import PartitionSpec as P

F32 = jnp.float32
BF16 = jnp.bfloat16
NX, NY, NC, NZ = 4, 4, 2, 8
TOK, CH, MODES = 256, 512, 16
LANES = 128
GROUPS = CH // LANES
STEPS = 32
BLOCKS = TOK // STEPS
ROWS = 2 * MODES
PAY = ROWS + 8
VMEM = pl.BlockSpec(memory_space=pltpu.VMEM)
FLAG = 16
SENT = 2 * ROWS + FLAG
WROWS = 128
FOLD = 4
THIN = TOK // FOLD
PARAMS = pltpu.CompilerParams(vmem_limit_bytes=24 * 1024 * 1024)


def call(kernel, outs, args, scratch=(), flops=0, nbytes=0):
    return pl.pallas_call(
        kernel,
        out_shape=outs,
        in_specs=[VMEM] * len(args),
        out_specs=jax.tree.map(lambda unused: VMEM, outs),
        scratch_shapes=list(scratch),
        compiler_params=PARAMS,
        cost_estimate=pl.CostEstimate(flops=flops, bytes_accessed=nbytes, transcendentals=0),
    )(*args)


def struct(*shape, dtype=F32):
    return jax.ShapeDtypeStruct(shape, dtype)


def cmul(a, b):
    return a[0] * b[0] - a[1] * b[1], a[0] * b[1] + a[1] * b[0]


def cadd(a, b):
    return a[0] + b[0], a[1] + b[1]


def square(a):
    return a[0] * a[0] - a[1] * a[1], 2.0 * a[0] * a[1]


def halves(ref):
    return ref[:MODES, :], ref[MODES:ROWS, :]


def first_start(starts_ref):
    starts = starts_ref[...]
    at = lax.broadcasted_iota(jnp.int32, starts.shape, 0) * LANES
    at = at + lax.broadcasted_iota(jnp.int32, starts.shape, 1)
    where = jnp.where(starts > 0, at, TOK)
    return jnp.min(jnp.min(where, axis=1, keepdims=True), axis=0, keepdims=True)


def fill_powers(pole, table_re, table_im, count):
    def put(k, value):
        for g in range(GROUPS):
            rows = pl.ds(pl.multiple_of(k * MODES, MODES), MODES)
            lanes = slice(g * LANES, (g + 1) * LANES)
            table_re[g, rows, :] = value[0][:, lanes]
            table_im[g, rows, :] = value[1][:, lanes]

    def step(k, value):
        put(k, value)
        return cmul(value, pole)

    one = (jnp.ones((MODES, CH), F32), jnp.zeros((MODES, CH), F32))
    last = lax.fori_loop(0, count, step, one)
    return last


def fill_signal(key_ref, value_ref, sig):
    for g in range(GROUPS):
        lanes = slice(g * LANES, (g + 1) * LANES)
        sig[g] = key_ref[:, lanes].astype(F32) * value_ref[:, lanes].astype(F32)


def block_iota():
    return lax.broadcasted_iota(jnp.int32, (BLOCKS, LANES), 0)


def powers_kernel(pole_re, pole_im, tre, tim, qre, qim, p256_ref):
    fill_powers((pole_re[...], pole_im[...]), tre, tim, STEPS + 1)
    q = last_power(tre, tim)
    value = (jnp.ones((MODES, CH), F32), jnp.zeros((MODES, CH), F32))
    for n in range(BLOCKS):
        row = (BLOCKS - 1 - n) * MODES
        for g in range(GROUPS):
            lanes = slice(g * LANES, (g + 1) * LANES)
            qre[g, row:row + MODES, :] = value[0][:, lanes]
            qim[g, row:row + MODES, :] = value[1][:, lanes]
        value = cmul(value, q)
    p256_ref[:MODES, :] = value[0]
    p256_ref[MODES:, :] = value[1]


def ends_kernel(key_ref, value_ref, starts_ref, tre, tim, qre, qim, pay_ref, eb_ref, sig):
    s0 = first_start(starts_ref)
    b0 = s0 // STEPS
    fill_signal(key_ref, value_ref, sig)
    blocks = block_iota()
    reach = (s0 >= TOK) | (blocks >= b0)

    def group(g, unused):
        def step(j, acc):
            x = sig[g, pl.ds(j, BLOCKS, stride=STEPS), :]
            x = jnp.where((blocks * STEPS + j >= s0) | (blocks != b0), x, 0.0)
            base = (STEPS - 1 - j) * MODES
            out = []
            for m in range(MODES):
                out.append(acc[2 * m] + tre[g, pl.ds(base + m, 1), :] * x)
                out.append(acc[2 * m + 1] + tim[g, pl.ds(base + m, 1), :] * x)
            return tuple(out)

        zero = jnp.zeros((BLOCKS, LANES), F32)
        acc = lax.fori_loop(0, STEPS, step, (zero,) * ROWS, unroll=4)
        for m in range(MODES):
            re, im = acc[2 * m], acc[2 * m + 1]
            eb_ref[g, m] = re
            eb_ref[g, MODES + m] = im
            w = (qre[g, pl.ds(m, BLOCKS, stride=MODES), :], qim[g, pl.ds(m, BLOCKS, stride=MODES), :])
            end = cmul(w, (re, im))
            lanes = pl.ds(pl.multiple_of(g * LANES, LANES), LANES)
            pay_ref[pl.ds(m, 1), lanes] = jnp.sum(jnp.where(reach, end[0], 0.0), axis=0, keepdims=True)
            pay_ref[pl.ds(MODES + m, 1), lanes] = jnp.sum(jnp.where(reach, end[1], 0.0), axis=0, keepdims=True)
        return unused

    lax.fori_loop(0, GROUPS, group, 0)
    pay_ref[ROWS:, :] = jnp.broadcast_to((s0 >= TOK).astype(F32), (PAY - ROWS, CH))


def last_power(tre, tim):
    return [jnp.concatenate([t[g, STEPS * MODES:, :] for g in range(GROUPS)], axis=1) for t in (tre, tim)]


def local_kernel(sig, tre, tim, decay_ref, res_ref, skip_ref, starts_ref, after_ref,
                 y_ref, weight_ref, taps):
    s0 = first_start(starts_ref)
    b0 = s0 // STEPS
    blocks = block_iota()
    y = 2.0 * decay_ref[...]
    series = jnp.ones_like(y)
    for n in range(10, 1, -1):
        series = 1.0 - y * (1.0 / n) * series
    scale = jnp.sqrt(y * series)
    weight = (res_ref[0] * scale, res_ref[1] * scale)
    weight_ref[:MODES, :] = weight[0]
    weight_ref[MODES:, :] = weight[1]
    for g in range(GROUPS):
        lanes = slice(g * LANES, (g + 1) * LANES)
        w_re, w_im = weight[0][:, lanes], weight[1][:, lanes]
        for k in range(STEPS):
            term = w_re * tre[g, k * MODES:(k + 1) * MODES, :] - w_im * tim[g, k * MODES:(k + 1) * MODES, :]
            row = jnp.sum(term, axis=0, keepdims=True)
            if k == 0:
                row = row + skip_ref[:, lanes]
            taps[g, k:k + 1, :] = row

    def group(g, unused):
        tile = 8

        def fir(select):
            xs = []
            for j in range(STEPS):
                x = sig[g, pl.ds(j, BLOCKS, stride=STEPS), :]
                late = (blocks * STEPS + j >= s0) | (blocks != b0)
                xs.append(jnp.where(late if select else jnp.logical_not(late), x, 0.0))
            for top in range(0, STEPS, tile):
                acc = [jnp.zeros((BLOCKS, LANES), F32)] * tile
                for k in range(top + tile):
                    tap = taps[g, k:k + 1, :]
                    for i in range(tile):
                        if top + i - k >= 0:
                            acc[i] = acc[i] + tap * xs[top + i - k]
                for i in range(tile):
                    if select:
                        y_ref[g, top + i] = acc[i]
                    else:
                        early = (blocks * STEPS + top + i < s0) & (blocks == b0)
                        y_ref[g, top + i] = y_ref[g, top + i] + jnp.where(early, acc[i], 0.0)

        fir(True)
        fir(False)
        return unused

    lax.fori_loop(0, GROUPS, group, 0)


def carry_kernel(eb_ref, tre, tim, weight_ref, starts_ref, pz_ref, gz_ref, qre, qim, rows_):
    s0 = first_start(starts_ref)
    b0 = s0 // STEPS
    blocks = block_iota()
    weight = (weight_ref[:MODES, :], weight_ref[MODES:, :])
    q = last_power(tre, tim)
    value = weight
    for n in range(BLOCKS):
        for g in range(GROUPS):
            lanes = slice(g * LANES, (g + 1) * LANES)
            qre[g, n * MODES:(n + 1) * MODES, :] = value[0][:, lanes]
            qim[g, n * MODES:(n + 1) * MODES, :] = value[1][:, lanes]
        value = cmul(value, q)
    power = q
    for n in range(3):
        for g in range(GROUPS):
            lanes = slice(g * LANES, (g + 1) * LANES)
            rows_[g, n * ROWS:n * ROWS + MODES, :] = power[0][:, lanes]
            rows_[g, n * ROWS + MODES:(n + 1) * ROWS, :] = power[1][:, lanes]
        power = square(power)
    for g in range(GROUPS):
        lanes = slice(g * LANES, (g + 1) * LANES)
        rows_[g, 3 * ROWS:3 * ROWS + MODES, :] = weight[0][:, lanes]
        rows_[g, 3 * ROWS + MODES:4 * ROWS, :] = weight[1][:, lanes]

    keeps = []
    for n in range(3):
        s = 1 << n
        keeps.append((blocks >= s) & jnp.logical_not((blocks - s < b0) & (b0 <= blocks)))
    heard = blocks <= b0

    def group(g, unused):
        for m in range(MODES):
            state = (eb_ref[g, m], eb_ref[g, MODES + m])
            for n in range(3):
                moved = [jnp.where(keeps[n], pltpu.roll(part, 1 << n, 0), 0.0) for part in state]
                step = (rows_[g, n * ROWS + m:n * ROWS + m + 1, :],
                        rows_[g, n * ROWS + MODES + m:n * ROWS + MODES + m + 1, :])
                state = cadd(state, cmul(step, moved))
            before = [jnp.where(blocks >= 1, pltpu.roll(part, 1, 0), 0.0) for part in state]
            w = (rows_[g, 3 * ROWS + m:3 * ROWS + m + 1, :],
                 rows_[g, 3 * ROWS + MODES + m:3 * ROWS + MODES + m + 1, :])
            scaled = cmul(w, before)
            pz_ref[g, m] = scaled[0]
            pz_ref[g, MODES + m] = scaled[1]
            gz_ref[g, m] = jnp.where(heard, qre[g, pl.ds(m, BLOCKS, stride=MODES), :], 0.0)
            gz_ref[g, MODES + m] = jnp.where(heard, qim[g, pl.ds(m, BLOCKS, stride=MODES), :], 0.0)

        return unused

    lax.fori_loop(0, GROUPS, group, 0)


def put_state(ref, state, thru):
    for part, at in zip(state, (0, MODES)):
        high = part.astype(BF16)
        ref[at:at + MODES, :] = high
        ref[ROWS + at:ROWS + at + MODES, :] = (part - high.astype(F32)).astype(BF16)
    ref[2 * ROWS:SENT, :] = jnp.broadcast_to(thru, (FLAG, CH)).astype(BF16)


def get_state(ref):
    parts = [ref[at:at + MODES, :].astype(F32) + ref[ROWS + at:ROWS + at + MODES, :].astype(F32)
             for at in (0, MODES)]
    return parts, ref[2 * ROWS:2 * ROWS + 8, :].astype(F32)[:1]


def chip_kernel(own_ref, other_ref, p256_ref, sent_ref):
    core = lax.axis_index("ctx") % NC
    first = (core == 0).astype(F32)
    own, other = halves(own_ref), halves(other_ref)
    own_thru, other_thru = own_ref[ROWS:ROWS + 1, :], other_ref[ROWS:ROWS + 1, :]
    early = [first * a + (1.0 - first) * b for a, b in zip(own, other)]
    late = [first * b + (1.0 - first) * a for a, b in zip(own, other)]
    late_thru = first * other_thru + (1.0 - first) * own_thru
    moved = cmul(halves(p256_ref), early)
    put_state(sent_ref, [late_thru * a + b for a, b in zip(moved, late)], own_thru * other_thru)


def put_pair(out_ref, side, own_ref, other_ref):
    rows = own_ref.shape[0]
    out_ref[pl.ds(pl.multiple_of(side * rows, rows), rows), :] = own_ref[...]
    out_ref[pl.ds(pl.multiple_of((1 - side) * rows, rows), rows), :] = other_ref[...]


def pair_kernel(own_ref, pair_ref, after_ref, out_ref):
    put_pair(out_ref, lax.axis_index("ctx") // (NC * NY) % 2, own_ref, pair_ref)


def row_kernel(own_ref, one_ref, two_ref, three_ref, p256_ref, pay_ref, before_ref, factor_ref, held):
    mine = (lax.axis_index("ctx") // NC) % NY
    for k, ref in enumerate((own_ref, one_ref, two_ref, three_ref)):
        there = lax.rem(mine - k + NY, NY)
        state, thru = get_state(ref)
        held[there, :MODES, :] = state[0]
        held[there, MODES:ROWS, :] = state[1]
        held[there, ROWS:, :] = jnp.broadcast_to(thru, (PAY - ROWS, CH))
    p512 = square(halves(p256_ref))
    state = (jnp.zeros((MODES, CH), F32),) * 2
    factor = (jnp.ones((MODES, CH), F32), jnp.zeros((MODES, CH), F32))
    thru = jnp.ones((1, CH), F32)
    for i in range(NY):
        @pl.when(mine == i)
        def put(state=state, factor=factor):
            before_ref[:MODES, :] = state[0]
            before_ref[MODES:, :] = state[1]
            factor_ref[:MODES, :] = factor[0]
            factor_ref[MODES:, :] = factor[1]
        open_ = held[i, ROWS:ROWS + 1, :]
        step = (open_ * p512[0], open_ * p512[1])
        state = cadd(cmul(step, state), (held[i, :MODES, :], held[i, MODES:ROWS, :]))
        factor = cmul(step, factor)
        thru = thru * open_
    pay_ref[:MODES, :] = state[0]
    pay_ref[MODES:ROWS, :] = state[1]
    pay_ref[ROWS:, :] = jnp.broadcast_to(thru, (PAY - ROWS, CH))


def gate_kernel(query_ref, y_ref, pz_ref, gz_ref, tre, tim, starts_ref, own_ref, other_ref, p256_ref,
                before_ref, factor_ref, one_ref, two_ref, hidden_ref, conv, sin):
    index = lax.axis_index("ctx")
    core, row = index % NC, index // (NC * NY)
    p256 = halves(p256_ref)
    p2048 = square(square(square(p256)))
    has_one = (row >= 1).astype(F32)
    has_two = (row >= 2).astype(F32)
    far = cmul(p2048, halves(two_ref))
    open_one = has_two * one_ref[ROWS:ROWS + 1, :]
    incoming = [has_one * a + open_one * b for a, b in zip(halves(one_ref), far)]
    state = cadd(halves(before_ref), cmul(halves(factor_ref), incoming))
    second = (core == 1).astype(F32)
    moved = cmul(p256, state)
    early_thru = other_ref[ROWS:ROWS + 1, :]
    state = [(1.0 - second) * a + second * (early_thru * b + c)
             for a, b, c in zip(state, moved, halves(other_ref))]
    for g in range(GROUPS):
        lanes = slice(g * LANES, (g + 1) * LANES)
        sin[g, :MODES, :] = state[0][:, lanes]
        sin[g, MODES:, :] = state[1][:, lanes]
    s0 = first_start(starts_ref)
    b0 = s0 // STEPS
    blocks = block_iota()

    def group(g, unused):
        z = []
        for m in range(MODES):
            s = (sin[g, m:m + 1, :], sin[g, MODES + m:MODES + m + 1, :])
            z.append(cadd((pz_ref[g, m], pz_ref[g, MODES + m]),
                          cmul((gz_ref[g, m], gz_ref[g, MODES + m]), s)))

        def step(j, unused):
            base = (j + 1) * MODES
            total = [None] * 4
            for m in range(MODES):
                term = tre[g, pl.ds(base + m, 1), :] * z[m][0] - tim[g, pl.ds(base + m, 1), :] * z[m][1]
                total[m % 4] = term if total[m % 4] is None else total[m % 4] + term
            total = (total[0] + total[1]) + (total[2] + total[3])
            late = (blocks * STEPS + j >= s0) & (blocks == b0)
            conv[g, pl.ds(j, BLOCKS, stride=STEPS), :] = y_ref[g, j] + jnp.where(late, 0.0, total)
            return unused

        return lax.fori_loop(0, STEPS, step, unused, unroll=4)

    lax.fori_loop(0, GROUPS, group, 0)
    for g in range(GROUPS):
        lanes = slice(g * LANES, (g + 1) * LANES)
        gated = (query_ref[:, lanes].astype(F32) * conv[g]).astype(BF16)
        for q in range(FOLD):
            hidden_ref[:, q * CH + g * LANES:q * CH + (g + 1) * LANES] = gated[q * THIN:(q + 1) * THIN]


def four_kernel(both_ref, pair_ref, after_ref, even_ref, odd_ref):
    side = (lax.axis_index("ctx") // NC) % 2
    even_ref[...] = jnp.where(side == 0, both_ref[...], pair_ref[...])
    odd_ref[...] = jnp.where(side == 0, pair_ref[...], both_ref[...])


def eight_kernel(even_ref, even_x, odd_ref, odd_y, after_up, after_down, even_out, odd_out):
    n = even_ref.shape[0]
    for at, ref, out in ((0, even_ref, even_out), (0, odd_ref, odd_out), (n, even_x, even_out), (n, odd_y, odd_out)):
        out[at:at + n, :] = ref[...]


def join_kernel(even_ref, odd_ref, even_far, odd_far, after_up, after_down, out_ref):
    n = even_ref.shape[0]
    for at, ref in enumerate((even_ref, odd_ref, even_far, odd_far)):
        out_ref[at * n:(at + 1) * n, :] = ref[...]


def places(k):
    index = lax.axis_index("ctx")
    xb, yb = index // (NC * NY * 2), (index // NC) % NY // 2
    block = lax.rem(lax.axis_index("tp") - k + NZ, NZ)
    dx = (block // 4 != xb).astype(jnp.int32)
    dy = (lax.rem(block, 2) != yb).astype(jnp.int32)
    i = lax.rem(block // 2, 2)
    found = []
    for h in range(2):
        far, near = (dy, dx) if h == 0 else (dx, dy)
        at = far * 8 * WROWS + h * 4 * WROWS + near * 2 * WROWS + i * WROWS
        found.append(pl.ds(pl.multiple_of(at, WROWS), WROWS))
    return found


def most_kernel(here, up1, down1, up2, down2, up3, down3, own_ref, total_ref, left):
    core = lax.axis_index("ctx") % NC
    for k, ref in enumerate((here, up1, up2, up3, None, down3, down2, down1)):
        for h, lanes in enumerate(places(k)):
            for c in range(NC):
                side = jnp.where(core == c, 0, 1)
                if ref is None:
                    left[side, :, lanes] = jnp.zeros((TOK, WROWS), BF16)
                    continue
                for q in range(FOLD):
                    at = slice(q * CH + (NC * h + c) * WROWS, q * CH + (NC * h + c + 1) * WROWS)
                    left[side, q * THIN:(q + 1) * THIN, lanes] = ref[:, at]
    total_ref[...] = jnp.dot(left[0], own_ref[...], preferred_element_type=F32)


def rest_kernel(total_ref, left, up4, down4, own_ref, other_ref, out_ref, last, rows):
    core = lax.axis_index("ctx") % NC
    for h, at in enumerate(places(4)):
        for c in range(NC):
            lanes = slice((NC * h + c) * WROWS, (NC * h + c + 1) * WROWS)
            for q in range(FOLD):
                middle = q * THIN + THIN // 2
                source = slice(q * CH + (NC * h + c) * WROWS, q * CH + (NC * h + c + 1) * WROWS)
                last[q * THIN:middle, lanes] = up4[:, source]
                last[middle:(q + 1) * THIN, lanes] = down4[:, source]
            rows[lanes, :] = jnp.where(core == c, own_ref[at, :], other_ref[at, :])
    out_ref[...] = (total_ref[...] + jnp.dot(left[1], other_ref[...], preferred_element_type=F32)
                    + jnp.dot(last[...], rows[...], preferred_element_type=F32)).astype(BF16)


def ctx_index(x, y, c):
    return ((x % NX) * NY + y % NY) * NC + c % NC


def move(value, dx, dy, dc):
    pairs = [(ctx_index(x, y, c), ctx_index(x + dx, y + dy, c + dc))
             for x in range(NX) for y in range(NY) for c in range(NC)]
    return lax.ppermute(value, "ctx", pairs)


def trade(value, dx, dy):
    pairs = [(ctx_index(x, y, c), ctx_index(x ^ dx, y ^ dy, c))
             for x in range(NX) for y in range(NY) for c in range(NC)]
    return lax.ppermute(value, "ctx", pairs)


def turn(value, k):
    return lax.ppermute(value, "tp", [(i, (i + k) % NZ) for i in range(NZ)])


def shards(query, key, value, decay, freq, residue, skip, out_weight, doc_starts):
    starts = doc_starts.reshape(TOK // LANES, LANES)
    skip = skip.reshape(1, CH)
    sig = pltpu.VMEM((GROUPS, TOK, LANES), F32)
    qs = pltpu.VMEM((GROUPS, BLOCKS * MODES, LANES), F32)
    state_shape = struct(ROWS, CH)
    pay_shape = struct(PAY, CH)
    block_shape = struct(GROUPS, ROWS, BLOCKS, LANES)
    table = (GROUPS, (STEPS + 1) * MODES, LANES)

    magnitude = jnp.exp(-decay)
    q_shape = struct(GROUPS, BLOCKS * MODES, LANES)
    tre, tim, qre, qim, p256 = call(
        powers_kernel, (struct(*table), struct(*table), q_shape, q_shape, state_shape),
        (magnitude * jnp.cos(freq), magnitude * jnp.sin(freq)), (), 2_000_000_000, 5_000_000)
    pay, eb, signal = call(
        ends_kernel, (pay_shape, block_shape, struct(GROUPS, TOK, LANES)),
        (key, value, starts, tre, tim, qre, qim), (), 20_000_000, 5_000_000)
    other = move(pay, 0, 0, 1)
    chip = call(chip_kernel, struct(SENT, CH, dtype=BF16), (pay, other, p256))
    near = [move(chip, 0, k, 0) for k in (1, 2, 3)]
    row, before, factor = call(
        row_kernel, (pay_shape, state_shape, state_shape),
        (chip, *near, p256), [pltpu.VMEM((NY, PAY, CH), F32)])
    back = [move(row, k, 0, 0) for k in (1, 2)]
    y, gain = call(
        local_kernel, (struct(GROUPS, STEPS, BLOCKS, LANES), state_shape),
        (signal, tre, tim, decay, residue, skip, starts, chip),
        [pltpu.VMEM((GROUPS, STEPS, LANES), F32)], 30_000_000, 5_000_000)
    pz, gz = call(
        carry_kernel, (block_shape, block_shape), (eb, tre, tim, gain, starts),
        [qs, qs, pltpu.VMEM((GROUPS, 4 * ROWS, LANES), F32)], 30_000_000, 5_000_000)
    hidden = call(
        gate_kernel, struct(THIN, FOLD * CH, dtype=BF16),
        (query, y, pz, gz, tre, tim, starts, pay, other, p256, before, factor, *back),
        [sig, pltpu.VMEM((GROUPS, ROWS, LANES), F32)], 20_000_000, 5_000_000)

    both = call(pair_kernel, struct(2 * WROWS, CH, dtype=BF16), (out_weight, trade(out_weight, 1, 0), row))
    w2, w4 = [struct(n * WROWS, CH, dtype=BF16) for n in (2, 4)]
    even, odd = call(four_kernel, (w2, w2), (both, trade(both, 0, 1), hidden), (), 0, 2_000_000)
    half = THIN // 2
    up1, down1 = turn(hidden, 1), turn(hidden, -1)
    even, odd = call(
        eight_kernel, (w4, w4), (even, trade(even, 2, 0), odd, trade(odd, 0, 2), up1, down1), (), 0, 4_000_000)
    up2, down2 = turn(up1, 1), turn(down1, -1)
    up3, down3 = turn(up2, 1), turn(down2, -1)
    up4, down4 = turn(up3[:half], 1), turn(down3[half:], -1)
    own = call(join_kernel, struct(NZ * CH // 2, CH, dtype=BF16),
               (even, odd, trade(even, 0, 2), trade(odd, 2, 0), up3, down3), (), 0, 4_000_000)
    total, left = call(
        most_kernel, (struct(TOK, CH), struct(NC, TOK, NZ * CH // NC, dtype=BF16)),
        (hidden, up1, down1, up2, down2, up3, down3, own), (), TOK * CH * CH * NZ, 7_000_000)
    return call(
        rest_kernel, struct(TOK, CH, dtype=BF16), (total, left, up4, down4, own, move(own, 0, 0, 1)),
        [pltpu.VMEM((TOK, CH), BF16), pltpu.VMEM((CH, CH), BF16)], TOK * CH * CH * NZ, 7_000_000)


def solution(mesh):
    in_specs = (
        P("ctx", "tp"),
        P("ctx", "tp"),
        P("ctx", "tp"),
        P(None, "tp"),
        P(None, "tp"),
        P(None, None, "tp"),
        P("tp"),
        P("ctx", "tp"),
        P("ctx"),
    )
    return jax.shard_map(
        shards, mesh=mesh, in_specs=in_specs, out_specs=P("ctx", "tp"), check_vma=False
    )
```

```python
import jax
import jax.numpy as jnp
from jax import lax
from jax.experimental import pallas as pl
from jax.experimental.pallas import tpu as pltpu
from jax.sharding import PartitionSpec as P

F32 = jnp.float32
BF16 = jnp.bfloat16
NX, NY, NC, NZ = 4, 4, 2, 8
TOK, CH, MODES = 256, 512, 16
LANES = 128
GROUPS = CH // LANES
STEPS = 32
BLOCKS = TOK // STEPS
ROWS = 2 * MODES
PAY = ROWS + 8
VMEM = pl.BlockSpec(memory_space=pltpu.VMEM)
FLAG = 16
SENT = 2 * ROWS + FLAG
WROWS = 128
FOLD = 4
THIN = TOK // FOLD
PARAMS = pltpu.CompilerParams(vmem_limit_bytes=24 * 1024 * 1024)


def call(kernel, outs, args, scratch=(), flops=0, nbytes=0):
    return pl.pallas_call(
        kernel,
        out_shape=outs,
        in_specs=[VMEM] * len(args),
        out_specs=jax.tree.map(lambda unused: VMEM, outs),
        scratch_shapes=list(scratch),
        compiler_params=PARAMS,
        cost_estimate=pl.CostEstimate(flops=flops, bytes_accessed=nbytes, transcendentals=0),
    )(*args)


def struct(*shape, dtype=F32):
    return jax.ShapeDtypeStruct(shape, dtype)


def cmul(a, b):
    return a[0] * b[0] - a[1] * b[1], a[0] * b[1] + a[1] * b[0]


def cadd(a, b):
    return a[0] + b[0], a[1] + b[1]


def square(a):
    return a[0] * a[0] - a[1] * a[1], 2.0 * a[0] * a[1]


def halves(ref):
    return ref[:MODES, :], ref[MODES:ROWS, :]


def first_start(starts_ref):
    starts = starts_ref[...]
    at = lax.broadcasted_iota(jnp.int32, starts.shape, 0) * LANES
    at = at + lax.broadcasted_iota(jnp.int32, starts.shape, 1)
    where = jnp.where(starts > 0, at, TOK)
    return jnp.min(jnp.min(where, axis=1, keepdims=True), axis=0, keepdims=True)


def fill_powers(pole, table_re, table_im, count):
    def put(k, value):
        for g in range(GROUPS):
            rows = pl.ds(pl.multiple_of(k * MODES, MODES), MODES)
            lanes = slice(g * LANES, (g + 1) * LANES)
            table_re[g, rows, :] = value[0][:, lanes]
            table_im[g, rows, :] = value[1][:, lanes]

    def step(k, value):
        put(k, value)
        return cmul(value, pole)

    one = (jnp.ones((MODES, CH), F32), jnp.zeros((MODES, CH), F32))
    last = lax.fori_loop(0, count, step, one)
    return last


def fill_signal(key_ref, value_ref, sig):
    for g in range(GROUPS):
        lanes = slice(g * LANES, (g + 1) * LANES)
        sig[g] = key_ref[:, lanes].astype(F32) * value_ref[:, lanes].astype(F32)


def block_iota():
    return lax.broadcasted_iota(jnp.int32, (BLOCKS, LANES), 0)


def powers_kernel(pole_re, pole_im, tre, tim, qre, qim, p256_ref):
    fill_powers((pole_re[...], pole_im[...]), tre, tim, STEPS + 1)
    q = last_power(tre, tim)
    value = (jnp.ones((MODES, CH), F32), jnp.zeros((MODES, CH), F32))
    for n in range(BLOCKS):
        row = (BLOCKS - 1 - n) * MODES
        for g in range(GROUPS):
            lanes = slice(g * LANES, (g + 1) * LANES)
            qre[g, row:row + MODES, :] = value[0][:, lanes]
            qim[g, row:row + MODES, :] = value[1][:, lanes]
        value = cmul(value, q)
    p256_ref[:MODES, :] = value[0]
    p256_ref[MODES:, :] = value[1]


def ends_kernel(key_ref, value_ref, starts_ref, tre, tim, qre, qim, pay_ref, eb_ref, sig):
    s0 = first_start(starts_ref)
    b0 = s0 // STEPS
    fill_signal(key_ref, value_ref, sig)
    blocks = block_iota()
    reach = (s0 >= TOK) | (blocks >= b0)

    def group(g, unused):
        def step(j, acc):
            x = sig[g, pl.ds(j, BLOCKS, stride=STEPS), :]
            x = jnp.where((blocks * STEPS + j >= s0) | (blocks != b0), x, 0.0)
            base = (STEPS - 1 - j) * MODES
            out = []
            for m in range(MODES):
                out.append(acc[2 * m] + tre[g, pl.ds(base + m, 1), :] * x)
                out.append(acc[2 * m + 1] + tim[g, pl.ds(base + m, 1), :] * x)
            return tuple(out)

        zero = jnp.zeros((BLOCKS, LANES), F32)
        acc = lax.fori_loop(0, STEPS, step, (zero,) * ROWS, unroll=8)
        for m in range(MODES):
            re, im = acc[2 * m], acc[2 * m + 1]
            eb_ref[g, m] = re
            eb_ref[g, MODES + m] = im
            w = (qre[g, pl.ds(m, BLOCKS, stride=MODES), :], qim[g, pl.ds(m, BLOCKS, stride=MODES), :])
            end = cmul(w, (re, im))
            lanes = pl.ds(pl.multiple_of(g * LANES, LANES), LANES)
            pay_ref[pl.ds(m, 1), lanes] = jnp.sum(jnp.where(reach, end[0], 0.0), axis=0, keepdims=True)
            pay_ref[pl.ds(MODES + m, 1), lanes] = jnp.sum(jnp.where(reach, end[1], 0.0), axis=0, keepdims=True)
        return unused

    lax.fori_loop(0, GROUPS, group, 0)
    pay_ref[ROWS:, :] = jnp.broadcast_to((s0 >= TOK).astype(F32), (PAY - ROWS, CH))


def last_power(tre, tim):
    return [jnp.concatenate([t[g, STEPS * MODES:, :] for g in range(GROUPS)], axis=1) for t in (tre, tim)]


def local_kernel(sig, tre, tim, decay_ref, res_ref, skip_ref, starts_ref, after_ref,
                 y_ref, weight_ref, taps):
    s0 = first_start(starts_ref)
    b0 = s0 // STEPS
    blocks = block_iota()
    y = 2.0 * decay_ref[...]
    series = jnp.ones_like(y)
    for n in range(10, 1, -1):
        series = 1.0 - y * (1.0 / n) * series
    scale = jnp.sqrt(y * series)
    weight = (res_ref[0] * scale, res_ref[1] * scale)
    weight_ref[:MODES, :] = weight[0]
    weight_ref[MODES:, :] = weight[1]
    for g in range(GROUPS):
        lanes = slice(g * LANES, (g + 1) * LANES)
        w_re, w_im = weight[0][:, lanes], weight[1][:, lanes]
        for k in range(STEPS):
            term = w_re * tre[g, k * MODES:(k + 1) * MODES, :] - w_im * tim[g, k * MODES:(k + 1) * MODES, :]
            row = jnp.sum(term, axis=0, keepdims=True)
            if k == 0:
                row = row + skip_ref[:, lanes]
            taps[g, k:k + 1, :] = row

    def group(g, unused):
        tile = 8

        def fir(select):
            xs = []
            for j in range(STEPS):
                x = sig[g, pl.ds(j, BLOCKS, stride=STEPS), :]
                late = (blocks * STEPS + j >= s0) | (blocks != b0)
                xs.append(jnp.where(late if select else jnp.logical_not(late), x, 0.0))
            for top in range(0, STEPS, tile):
                acc = [jnp.zeros((BLOCKS, LANES), F32)] * tile
                for k in range(top + tile):
                    tap = taps[g, k:k + 1, :]
                    for i in range(tile):
                        if top + i - k >= 0:
                            acc[i] = acc[i] + tap * xs[top + i - k]
                for i in range(tile):
                    if select:
                        y_ref[g, top + i] = acc[i]
                    else:
                        early = (blocks * STEPS + top + i < s0) & (blocks == b0)
                        y_ref[g, top + i] = y_ref[g, top + i] + jnp.where(early, acc[i], 0.0)

        fir(True)
        fir(False)
        return unused

    lax.fori_loop(0, GROUPS, group, 0)


def carry_kernel(eb_ref, tre, tim, weight_ref, starts_ref, pz_ref, gz_ref, qre, qim, rows_):
    s0 = first_start(starts_ref)
    b0 = s0 // STEPS
    blocks = block_iota()
    weight = (weight_ref[:MODES, :], weight_ref[MODES:, :])
    q = last_power(tre, tim)
    value = weight
    for n in range(BLOCKS):
        for g in range(GROUPS):
            lanes = slice(g * LANES, (g + 1) * LANES)
            qre[g, n * MODES:(n + 1) * MODES, :] = value[0][:, lanes]
            qim[g, n * MODES:(n + 1) * MODES, :] = value[1][:, lanes]
        value = cmul(value, q)
    power = q
    for n in range(3):
        for g in range(GROUPS):
            lanes = slice(g * LANES, (g + 1) * LANES)
            rows_[g, n * ROWS:n * ROWS + MODES, :] = power[0][:, lanes]
            rows_[g, n * ROWS + MODES:(n + 1) * ROWS, :] = power[1][:, lanes]
        power = square(power)
    for g in range(GROUPS):
        lanes = slice(g * LANES, (g + 1) * LANES)
        rows_[g, 3 * ROWS:3 * ROWS + MODES, :] = weight[0][:, lanes]
        rows_[g, 3 * ROWS + MODES:4 * ROWS, :] = weight[1][:, lanes]

    keeps = []
    for n in range(3):
        s = 1 << n
        keeps.append((blocks >= s) & jnp.logical_not((blocks - s < b0) & (b0 <= blocks)))
    heard = blocks <= b0

    def group(g, unused):
        for m in range(MODES):
            state = (eb_ref[g, m], eb_ref[g, MODES + m])
            for n in range(3):
                moved = [jnp.where(keeps[n], pltpu.roll(part, 1 << n, 0), 0.0) for part in state]
                step = (rows_[g, n * ROWS + m:n * ROWS + m + 1, :],
                        rows_[g, n * ROWS + MODES + m:n * ROWS + MODES + m + 1, :])
                state = cadd(state, cmul(step, moved))
            before = [jnp.where(blocks >= 1, pltpu.roll(part, 1, 0), 0.0) for part in state]
            w = (rows_[g, 3 * ROWS + m:3 * ROWS + m + 1, :],
                 rows_[g, 3 * ROWS + MODES + m:3 * ROWS + MODES + m + 1, :])
            scaled = cmul(w, before)
            pz_ref[g, m] = scaled[0]
            pz_ref[g, MODES + m] = scaled[1]
            gz_ref[g, m] = jnp.where(heard, qre[g, pl.ds(m, BLOCKS, stride=MODES), :], 0.0)
            gz_ref[g, MODES + m] = jnp.where(heard, qim[g, pl.ds(m, BLOCKS, stride=MODES), :], 0.0)

        return unused

    lax.fori_loop(0, GROUPS, group, 0)


def put_state(ref, state, thru):
    for part, at in zip(state, (0, MODES)):
        high = part.astype(BF16)
        ref[at:at + MODES, :] = high
        ref[ROWS + at:ROWS + at + MODES, :] = (part - high.astype(F32)).astype(BF16)
    ref[2 * ROWS:SENT, :] = jnp.broadcast_to(thru, (FLAG, CH)).astype(BF16)


def get_state(ref):
    parts = [ref[at:at + MODES, :].astype(F32) + ref[ROWS + at:ROWS + at + MODES, :].astype(F32)
             for at in (0, MODES)]
    return parts, ref[2 * ROWS:2 * ROWS + 8, :].astype(F32)[:1]


def chip_kernel(own_ref, other_ref, p256_ref, sent_ref):
    core = lax.axis_index("ctx") % NC
    first = (core == 0).astype(F32)
    own, other = halves(own_ref), halves(other_ref)
    own_thru, other_thru = own_ref[ROWS:ROWS + 1, :], other_ref[ROWS:ROWS + 1, :]
    early = [first * a + (1.0 - first) * b for a, b in zip(own, other)]
    late = [first * b + (1.0 - first) * a for a, b in zip(own, other)]
    late_thru = first * other_thru + (1.0 - first) * own_thru
    moved = cmul(halves(p256_ref), early)
    put_state(sent_ref, [late_thru * a + b for a, b in zip(moved, late)], own_thru * other_thru)


def put_pair(out_ref, side, own_ref, other_ref):
    rows = own_ref.shape[0]
    out_ref[pl.ds(pl.multiple_of(side * rows, rows), rows), :] = own_ref[...]
    out_ref[pl.ds(pl.multiple_of((1 - side) * rows, rows), rows), :] = other_ref[...]


def pair_kernel(own_ref, pair_ref, after_ref, out_ref):
    put_pair(out_ref, lax.axis_index("ctx") // (NC * NY) % 2, own_ref, pair_ref)


def row_kernel(own_ref, one_ref, two_ref, three_ref, p256_ref, pay_ref, before_ref, factor_ref, held):
    mine = (lax.axis_index("ctx") // NC) % NY
    for k, ref in enumerate((own_ref, one_ref, two_ref, three_ref)):
        there = lax.rem(mine - k + NY, NY)
        state, thru = get_state(ref)
        held[there, :MODES, :] = state[0]
        held[there, MODES:ROWS, :] = state[1]
        held[there, ROWS:, :] = jnp.broadcast_to(thru, (PAY - ROWS, CH))
    p512 = square(halves(p256_ref))
    state = (jnp.zeros((MODES, CH), F32),) * 2
    factor = (jnp.ones((MODES, CH), F32), jnp.zeros((MODES, CH), F32))
    thru = jnp.ones((1, CH), F32)
    for i in range(NY):
        @pl.when(mine == i)
        def put(state=state, factor=factor):
            before_ref[:MODES, :] = state[0]
            before_ref[MODES:, :] = state[1]
            factor_ref[:MODES, :] = factor[0]
            factor_ref[MODES:, :] = factor[1]
        open_ = held[i, ROWS:ROWS + 1, :]
        step = (open_ * p512[0], open_ * p512[1])
        state = cadd(cmul(step, state), (held[i, :MODES, :], held[i, MODES:ROWS, :]))
        factor = cmul(step, factor)
        thru = thru * open_
    pay_ref[:MODES, :] = state[0]
    pay_ref[MODES:ROWS, :] = state[1]
    pay_ref[ROWS:, :] = jnp.broadcast_to(thru, (PAY - ROWS, CH))


def gate_kernel(query_ref, y_ref, pz_ref, gz_ref, tre, tim, starts_ref, own_ref, other_ref, p256_ref,
                before_ref, factor_ref, one_ref, two_ref, hidden_ref, conv, sin):
    index = lax.axis_index("ctx")
    core, row = index % NC, index // (NC * NY)
    p256 = halves(p256_ref)
    p2048 = square(square(square(p256)))
    has_one = (row >= 1).astype(F32)
    has_two = (row >= 2).astype(F32)
    far = cmul(p2048, halves(two_ref))
    open_one = has_two * one_ref[ROWS:ROWS + 1, :]
    incoming = [has_one * a + open_one * b for a, b in zip(halves(one_ref), far)]
    state = cadd(halves(before_ref), cmul(halves(factor_ref), incoming))
    second = (core == 1).astype(F32)
    moved = cmul(p256, state)
    early_thru = other_ref[ROWS:ROWS + 1, :]
    state = [(1.0 - second) * a + second * (early_thru * b + c)
             for a, b, c in zip(state, moved, halves(other_ref))]
    for g in range(GROUPS):
        lanes = slice(g * LANES, (g + 1) * LANES)
        sin[g, :MODES, :] = state[0][:, lanes]
        sin[g, MODES:, :] = state[1][:, lanes]
    s0 = first_start(starts_ref)
    b0 = s0 // STEPS
    blocks = block_iota()

    def group(g, unused):
        z = []
        for m in range(MODES):
            s = (sin[g, m:m + 1, :], sin[g, MODES + m:MODES + m + 1, :])
            z.append(cadd((pz_ref[g, m], pz_ref[g, MODES + m]),
                          cmul((gz_ref[g, m], gz_ref[g, MODES + m]), s)))

        def step(j, unused):
            base = (j + 1) * MODES
            total = [None] * 4
            for m in range(MODES):
                term = tre[g, pl.ds(base + m, 1), :] * z[m][0] - tim[g, pl.ds(base + m, 1), :] * z[m][1]
                total[m % 4] = term if total[m % 4] is None else total[m % 4] + term
            total = (total[0] + total[1]) + (total[2] + total[3])
            late = (blocks * STEPS + j >= s0) & (blocks == b0)
            conv[g, pl.ds(j, BLOCKS, stride=STEPS), :] = y_ref[g, j] + jnp.where(late, 0.0, total)
            return unused

        return lax.fori_loop(0, STEPS, step, unused, unroll=16)

    lax.fori_loop(0, GROUPS, group, 0)
    for g in range(GROUPS):
        lanes = slice(g * LANES, (g + 1) * LANES)
        gated = (query_ref[:, lanes].astype(F32) * conv[g]).astype(BF16)
        for q in range(FOLD):
            hidden_ref[:, q * CH + g * LANES:q * CH + (g + 1) * LANES] = gated[q * THIN:(q + 1) * THIN]


def four_kernel(both_ref, pair_ref, after_ref, even_ref, odd_ref):
    side = (lax.axis_index("ctx") // NC) % 2
    even_ref[...] = jnp.where(side == 0, both_ref[...], pair_ref[...])
    odd_ref[...] = jnp.where(side == 0, pair_ref[...], both_ref[...])


def eight_kernel(even_ref, even_x, odd_ref, odd_y, after_up, after_down, all_ref, even_out, odd_out):
    n = even_ref.shape[0]
    for at, ref, out in ((0, even_ref, even_out), (0, odd_ref, odd_out), (n, even_x, even_out), (n, odd_y, odd_out)):
        out[at:at + n, :] = ref[...]
        start = at if out is even_out else 2 * n + at
        all_ref[start:start + n, :] = ref[...]


def join_kernel(even_ref, odd_ref, after_up, after_down, out_ref):
    n = even_ref.shape[0]
    out_ref[:n, :] = even_ref[...]
    out_ref[n:, :] = odd_ref[...]


def places(k):
    index = lax.axis_index("ctx")
    xb, yb = index // (NC * NY * 2), (index // NC) % NY // 2
    block = lax.rem(lax.axis_index("tp") - k + NZ, NZ)
    dx = (block // 4 != xb).astype(jnp.int32)
    dy = (lax.rem(block, 2) != yb).astype(jnp.int32)
    i = lax.rem(block // 2, 2)
    found = []
    for h in range(2):
        far, near = (dy, dx) if h == 0 else (dx, dy)
        at = far * 8 * WROWS + h * 4 * WROWS + near * 2 * WROWS + i * WROWS
        found.append(pl.ds(pl.multiple_of(at, WROWS), WROWS))
    return found


def most_kernel(here, up1, down1, up2, down2, up3, down3, near_own, far_own, near_other, total_ref, left_ref, left):
    core = lax.axis_index("ctx") % NC
    wide = 8 * WROWS
    for k, ref in enumerate((here, up1, up2, up3, None, down3, down2, down1)):
        for h, lanes in enumerate(places(k)):
            for c in range(NC):
                side = jnp.where(core == c, 0, 1)
                if ref is None:
                    left[side, :, lanes] = jnp.zeros((TOK, WROWS), BF16)
                    continue
                for q in range(FOLD):
                    at = slice(q * CH + (NC * h + c) * WROWS, q * CH + (NC * h + c + 1) * WROWS)
                    left[side, q * THIN:(q + 1) * THIN, lanes] = ref[:, at]
    total_ref[...] = (jnp.dot(left[0, :, :wide], near_own[...], preferred_element_type=F32)
                      + jnp.dot(left[0, :, wide:], far_own[...], preferred_element_type=F32)
                      + jnp.dot(left[1, :, :wide], near_other[...], preferred_element_type=F32))
    left_ref[...] = left[1, :, wide:]


def last_kernel(up4, down4, out_ref):
    for q in range(FOLD):
        middle = q * THIN + THIN // 2
        lanes = slice(q * CH, (q + 1) * CH)
        out_ref[q * THIN:middle, :] = up4[:, lanes]
        out_ref[middle:(q + 1) * THIN, :] = down4[:, lanes]


def rest_kernel(total_ref, left, last, near_own, near_other, own_ref, other_ref, out_ref, rows):
    core = lax.axis_index("ctx") % NC
    wide = 8 * WROWS
    for h, place in enumerate(places(4)):
        far = place.start >= wide
        at = pl.ds(pl.multiple_of(jnp.where(far, place.start - wide, place.start), WROWS), WROWS)
        for c in range(NC):
            lanes = slice((NC * h + c) * WROWS, (NC * h + c + 1) * WROWS)
            rows[lanes, :] = jnp.where(core == c, jnp.where(far, own_ref[at, :], near_own[at, :]),
                                       jnp.where(far, other_ref[at, :], near_other[at, :]))
    out_ref[...] = (total_ref[...] + jnp.dot(left[...], other_ref[...], preferred_element_type=F32)
                    + jnp.dot(last[...], rows[...], preferred_element_type=F32)).astype(BF16)


def ctx_index(x, y, c):
    return ((x % NX) * NY + y % NY) * NC + c % NC


def move(value, dx, dy, dc):
    pairs = [(ctx_index(x, y, c), ctx_index(x + dx, y + dy, c + dc))
             for x in range(NX) for y in range(NY) for c in range(NC)]
    return lax.ppermute(value, "ctx", pairs)


def trade(value, dx, dy):
    pairs = [(ctx_index(x, y, c), ctx_index(x ^ dx, y ^ dy, c))
             for x in range(NX) for y in range(NY) for c in range(NC)]
    return lax.ppermute(value, "ctx", pairs)


def turn(value, k):
    return lax.ppermute(value, "tp", [(i, (i + k) % NZ) for i in range(NZ)])


def shards(query, key, value, decay, freq, residue, skip, out_weight, doc_starts):
    starts = doc_starts.reshape(TOK // LANES, LANES)
    skip = skip.reshape(1, CH)
    sig = pltpu.VMEM((GROUPS, TOK, LANES), F32)
    qs = pltpu.VMEM((GROUPS, BLOCKS * MODES, LANES), F32)
    state_shape = struct(ROWS, CH)
    pay_shape = struct(PAY, CH)
    block_shape = struct(GROUPS, ROWS, BLOCKS, LANES)
    table = (GROUPS, (STEPS + 1) * MODES, LANES)

    magnitude = jnp.exp(-decay)
    q_shape = struct(GROUPS, BLOCKS * MODES, LANES)
    tre, tim, qre, qim, p256 = call(
        powers_kernel, (struct(*table), struct(*table), q_shape, q_shape, state_shape),
        (magnitude * jnp.cos(freq), magnitude * jnp.sin(freq)), (), 2_000_000_000, 5_000_000)
    pay, eb, signal = call(
        ends_kernel, (pay_shape, block_shape, struct(GROUPS, TOK, LANES)),
        (key, value, starts, tre, tim, qre, qim), (), 20_000_000, 5_000_000)
    other = move(pay, 0, 0, 1)
    chip = call(chip_kernel, struct(SENT, CH, dtype=BF16), (pay, other, p256))
    near = [move(chip, 0, k, 0) for k in (1, 2, 3)]
    row, before, factor = call(
        row_kernel, (pay_shape, state_shape, state_shape),
        (chip, *near, p256), [pltpu.VMEM((NY, PAY, CH), F32)])
    back = [move(row, k, 0, 0) for k in (1, 2)]
    y, gain = call(
        local_kernel, (struct(GROUPS, STEPS, BLOCKS, LANES), state_shape),
        (signal, tre, tim, decay, residue, skip, starts, chip),
        [pltpu.VMEM((GROUPS, STEPS, LANES), F32)], 30_000_000, 5_000_000)
    pz, gz = call(
        carry_kernel, (block_shape, block_shape), (eb, tre, tim, gain, starts),
        [qs, qs, pltpu.VMEM((GROUPS, 4 * ROWS, LANES), F32)], 30_000_000, 5_000_000)
    hidden = call(
        gate_kernel, struct(THIN, FOLD * CH, dtype=BF16),
        (query, y, pz, gz, tre, tim, starts, pay, other, p256, before, factor, *back),
        [sig, pltpu.VMEM((GROUPS, ROWS, LANES), F32)], 2_000_000_000, 5_000_000)

    both = call(pair_kernel, struct(2 * WROWS, CH, dtype=BF16), (out_weight, trade(out_weight, 1, 0), row))
    w2, w4, w8 = [struct(n * WROWS, CH, dtype=BF16) for n in (2, 4, 8)]
    even, odd = call(four_kernel, (w2, w2), (both, trade(both, 0, 1), hidden), (), 0, 2_000_000)
    half = THIN // 2
    up1, down1 = turn(hidden, 1), turn(hidden, -1)
    near, even, odd = call(
        eight_kernel, (w8, w4, w4), (even, trade(even, 2, 0), odd, trade(odd, 0, 2), up1, down1), (), 0, 4_000_000)
    up2, down2 = turn(up1, 1), turn(down1, -1)
    up3, down3 = turn(up2, 1), turn(down2, -1)
    up4, down4 = turn(up3[:half], 1), turn(down3[half:], -1)
    far = call(join_kernel, w8, (trade(even, 0, 2), trade(odd, 2, 0), up3, down3), (), 0, 2_000_000)
    near_other = move(near, 0, 0, 1)
    total, left = call(
        most_kernel, (struct(TOK, CH), struct(TOK, 8 * WROWS, dtype=BF16)),
        (hidden, up1, down1, up2, down2, up3, down3, near, far, near_other),
        [pltpu.VMEM((NC, TOK, NZ * CH // NC), BF16)], 1_000_000_000, 7_000_000)
    last = call(last_kernel, struct(TOK, CH, dtype=BF16), (up4, down4), (), 20_000_000_000, 1_000_000)
    return call(
        rest_kernel, struct(TOK, CH, dtype=BF16), (total, left, last, near, near_other, far, move(far, 0, 0, 1)),
        [pltpu.VMEM((CH, CH), BF16)], TOK * CH * CH * NZ, 7_000_000)


def solution(mesh):
    in_specs = (
        P("ctx", "tp"),
        P("ctx", "tp"),
        P("ctx", "tp"),
        P(None, "tp"),
        P(None, "tp"),
        P(None, None, "tp"),
        P("tp"),
        P("ctx", "tp"),
        P("ctx"),
    )
    return jax.shard_map(
        shards, mesh=mesh, in_specs=in_specs, out_specs=P("ctx", "tp"), check_vma=False
    )
```

```python
import jax
import jax.numpy as jnp
from jax import lax
from jax.experimental import pallas as pl
from jax.experimental.pallas import tpu as pltpu
from jax.sharding import PartitionSpec as P

F32 = jnp.float32
BF16 = jnp.bfloat16
NX, NY, NC, NZ = 4, 4, 2, 8
TOK, CH, MODES = 256, 512, 16
LANES = 128
GROUPS = CH // LANES
STEPS = 32
BLOCKS = TOK // STEPS
ROWS = 2 * MODES
PAY = ROWS + 8
VMEM = pl.BlockSpec(memory_space=pltpu.VMEM)
FLAG = 16
SENT = 2 * ROWS + FLAG
WROWS = 128
FOLD = 4
THIN = TOK // FOLD
PARAMS = pltpu.CompilerParams(vmem_limit_bytes=24 * 1024 * 1024)


def call(kernel, outs, args, scratch=(), flops=0, nbytes=0):
    return pl.pallas_call(
        kernel,
        out_shape=outs,
        in_specs=[VMEM] * len(args),
        out_specs=jax.tree.map(lambda unused: VMEM, outs),
        scratch_shapes=list(scratch),
        compiler_params=PARAMS,
        cost_estimate=pl.CostEstimate(flops=flops, bytes_accessed=nbytes, transcendentals=0),
    )(*args)


def struct(*shape, dtype=F32):
    return jax.ShapeDtypeStruct(shape, dtype)


def cmul(a, b):
    return a[0] * b[0] - a[1] * b[1], a[0] * b[1] + a[1] * b[0]


def cadd(a, b):
    return a[0] + b[0], a[1] + b[1]


def square(a):
    return a[0] * a[0] - a[1] * a[1], 2.0 * a[0] * a[1]


def halves(ref):
    return ref[:MODES, :], ref[MODES:ROWS, :]


def first_start(starts_ref):
    starts = starts_ref[...]
    at = lax.broadcasted_iota(jnp.int32, starts.shape, 0) * LANES
    at = at + lax.broadcasted_iota(jnp.int32, starts.shape, 1)
    where = jnp.where(starts > 0, at, TOK)
    return jnp.min(jnp.min(where, axis=1, keepdims=True), axis=0, keepdims=True)


def fill_powers(pole, table_re, table_im, count):
    def put(k, value):
        for g in range(GROUPS):
            rows = pl.ds(pl.multiple_of(k * MODES, MODES), MODES)
            lanes = slice(g * LANES, (g + 1) * LANES)
            table_re[g, rows, :] = value[0][:, lanes]
            table_im[g, rows, :] = value[1][:, lanes]

    def step(k, value):
        put(k, value)
        return cmul(value, pole)

    one = (jnp.ones((MODES, CH), F32), jnp.zeros((MODES, CH), F32))
    last = lax.fori_loop(0, count, step, one)
    return last


def fill_signal(key_ref, value_ref, sig):
    for g in range(GROUPS):
        lanes = slice(g * LANES, (g + 1) * LANES)
        sig[g] = key_ref[:, lanes].astype(F32) * value_ref[:, lanes].astype(F32)


def block_iota():
    return lax.broadcasted_iota(jnp.int32, (BLOCKS, LANES), 0)


def powers_kernel(pole_re, pole_im, tre, tim, qre, qim, p256_ref):
    fill_powers((pole_re[...], pole_im[...]), tre, tim, STEPS + 1)
    q = last_power(tre, tim)
    value = (jnp.ones((MODES, CH), F32), jnp.zeros((MODES, CH), F32))
    for n in range(BLOCKS):
        row = (BLOCKS - 1 - n) * MODES
        for g in range(GROUPS):
            lanes = slice(g * LANES, (g + 1) * LANES)
            qre[g, row:row + MODES, :] = value[0][:, lanes]
            qim[g, row:row + MODES, :] = value[1][:, lanes]
        value = cmul(value, q)
    p256_ref[:MODES, :] = value[0]
    p256_ref[MODES:, :] = value[1]


def ends_kernel(key_ref, value_ref, starts_ref, tre, tim, qre, qim, pay_ref, eb_ref, sig):
    s0 = first_start(starts_ref)
    b0 = s0 // STEPS
    fill_signal(key_ref, value_ref, sig)
    blocks = block_iota()
    reach = (s0 >= TOK) | (blocks >= b0)

    def group(g, unused):
        def step(j, acc):
            x = sig[g, pl.ds(j, BLOCKS, stride=STEPS), :]
            x = jnp.where((blocks * STEPS + j >= s0) | (blocks != b0), x, 0.0)
            base = (STEPS - 1 - j) * MODES
            out = []
            for m in range(MODES):
                out.append(acc[2 * m] + tre[g, pl.ds(base + m, 1), :] * x)
                out.append(acc[2 * m + 1] + tim[g, pl.ds(base + m, 1), :] * x)
            return tuple(out)

        zero = jnp.zeros((BLOCKS, LANES), F32)
        acc = lax.fori_loop(0, STEPS, step, (zero,) * ROWS, unroll=8)
        for m in range(MODES):
            re, im = acc[2 * m], acc[2 * m + 1]
            eb_ref[g, m] = re
            eb_ref[g, MODES + m] = im
            w = (qre[g, pl.ds(m, BLOCKS, stride=MODES), :], qim[g, pl.ds(m, BLOCKS, stride=MODES), :])
            end = cmul(w, (re, im))
            lanes = pl.ds(pl.multiple_of(g * LANES, LANES), LANES)
            pay_ref[pl.ds(m, 1), lanes] = jnp.sum(jnp.where(reach, end[0], 0.0), axis=0, keepdims=True)
            pay_ref[pl.ds(MODES + m, 1), lanes] = jnp.sum(jnp.where(reach, end[1], 0.0), axis=0, keepdims=True)
        return unused

    lax.fori_loop(0, GROUPS, group, 0)
    pay_ref[ROWS:, :] = jnp.broadcast_to((s0 >= TOK).astype(F32), (PAY - ROWS, CH))


def last_power(tre, tim):
    return [jnp.concatenate([t[g, STEPS * MODES:, :] for g in range(GROUPS)], axis=1) for t in (tre, tim)]


def local_kernel(sig, tre, tim, decay_ref, res_ref, skip_ref, starts_ref, after_ref,
                 y_ref, weight_ref, taps):
    s0 = first_start(starts_ref)
    b0 = s0 // STEPS
    blocks = block_iota()
    y = 2.0 * decay_ref[...]
    series = jnp.ones_like(y)
    for n in range(10, 1, -1):
        series = 1.0 - y * (1.0 / n) * series
    scale = jnp.sqrt(y * series)
    weight = (res_ref[0] * scale, res_ref[1] * scale)
    weight_ref[:MODES, :] = weight[0]
    weight_ref[MODES:, :] = weight[1]
    for g in range(GROUPS):
        lanes = slice(g * LANES, (g + 1) * LANES)
        w_re, w_im = weight[0][:, lanes], weight[1][:, lanes]
        for k in range(STEPS):
            term = w_re * tre[g, k * MODES:(k + 1) * MODES, :] - w_im * tim[g, k * MODES:(k + 1) * MODES, :]
            row = jnp.sum(term, axis=0, keepdims=True)
            if k == 0:
                row = row + skip_ref[:, lanes]
            taps[g, k:k + 1, :] = row

    def group(g, unused):
        tile = 8

        def fir(select):
            xs = []
            for j in range(STEPS):
                x = sig[g, pl.ds(j, BLOCKS, stride=STEPS), :]
                late = (blocks * STEPS + j >= s0) | (blocks != b0)
                xs.append(jnp.where(late if select else jnp.logical_not(late), x, 0.0))
            for top in range(0, STEPS, tile):
                acc = [jnp.zeros((BLOCKS, LANES), F32)] * tile
                for k in range(top + tile):
                    tap = taps[g, k:k + 1, :]
                    for i in range(tile):
                        if top + i - k >= 0:
                            acc[i] = acc[i] + tap * xs[top + i - k]
                for i in range(tile):
                    if select:
                        y_ref[g, top + i] = acc[i]
                    else:
                        early = (blocks * STEPS + top + i < s0) & (blocks == b0)
                        y_ref[g, top + i] = y_ref[g, top + i] + jnp.where(early, acc[i], 0.0)

        fir(True)
        fir(False)
        return unused

    lax.fori_loop(0, GROUPS, group, 0)


def carry_kernel(eb_ref, tre, tim, weight_ref, starts_ref, pz_ref, gz_ref, qre, qim, rows_):
    s0 = first_start(starts_ref)
    b0 = s0 // STEPS
    blocks = block_iota()
    weight = (weight_ref[:MODES, :], weight_ref[MODES:, :])
    q = last_power(tre, tim)
    value = weight
    for n in range(BLOCKS):
        for g in range(GROUPS):
            lanes = slice(g * LANES, (g + 1) * LANES)
            qre[g, n * MODES:(n + 1) * MODES, :] = value[0][:, lanes]
            qim[g, n * MODES:(n + 1) * MODES, :] = value[1][:, lanes]
        value = cmul(value, q)
    power = q
    for n in range(3):
        for g in range(GROUPS):
            lanes = slice(g * LANES, (g + 1) * LANES)
            rows_[g, n * ROWS:n * ROWS + MODES, :] = power[0][:, lanes]
            rows_[g, n * ROWS + MODES:(n + 1) * ROWS, :] = power[1][:, lanes]
        power = square(power)
    for g in range(GROUPS):
        lanes = slice(g * LANES, (g + 1) * LANES)
        rows_[g, 3 * ROWS:3 * ROWS + MODES, :] = weight[0][:, lanes]
        rows_[g, 3 * ROWS + MODES:4 * ROWS, :] = weight[1][:, lanes]

    keeps = []
    for n in range(3):
        s = 1 << n
        keeps.append((blocks >= s) & jnp.logical_not((blocks - s < b0) & (b0 <= blocks)))
    heard = blocks <= b0

    def group(g, unused):
        for m in range(MODES):
            state = (eb_ref[g, m], eb_ref[g, MODES + m])
            for n in range(3):
                moved = [jnp.where(keeps[n], pltpu.roll(part, 1 << n, 0), 0.0) for part in state]
                step = (rows_[g, n * ROWS + m:n * ROWS + m + 1, :],
                        rows_[g, n * ROWS + MODES + m:n * ROWS + MODES + m + 1, :])
                state = cadd(state, cmul(step, moved))
            before = [jnp.where(blocks >= 1, pltpu.roll(part, 1, 0), 0.0) for part in state]
            w = (rows_[g, 3 * ROWS + m:3 * ROWS + m + 1, :],
                 rows_[g, 3 * ROWS + MODES + m:3 * ROWS + MODES + m + 1, :])
            scaled = cmul(w, before)
            pz_ref[g, m] = scaled[0]
            pz_ref[g, MODES + m] = scaled[1]
            gz_ref[g, m] = jnp.where(heard, qre[g, pl.ds(m, BLOCKS, stride=MODES), :], 0.0)
            gz_ref[g, MODES + m] = jnp.where(heard, qim[g, pl.ds(m, BLOCKS, stride=MODES), :], 0.0)

        return unused

    lax.fori_loop(0, GROUPS, group, 0)


def put_state(ref, state, thru):
    for part, at in zip(state, (0, MODES)):
        high = part.astype(BF16)
        ref[at:at + MODES, :] = high
        ref[ROWS + at:ROWS + at + MODES, :] = (part - high.astype(F32)).astype(BF16)
    ref[2 * ROWS:SENT, :] = jnp.broadcast_to(thru, (FLAG, CH)).astype(BF16)


def get_state(ref):
    parts = [ref[at:at + MODES, :].astype(F32) + ref[ROWS + at:ROWS + at + MODES, :].astype(F32)
             for at in (0, MODES)]
    return parts, ref[2 * ROWS:SENT, :].astype(F32)[:1]


def chip_kernel(own_ref, other_ref, p256_ref, sent_ref):
    core = lax.axis_index("ctx") % NC
    first = (core == 0).astype(F32)
    own, other = halves(own_ref), halves(other_ref)
    own_thru, other_thru = own_ref[ROWS:ROWS + 1, :], other_ref[ROWS:ROWS + 1, :]
    early = [first * a + (1.0 - first) * b for a, b in zip(own, other)]
    late = [first * b + (1.0 - first) * a for a, b in zip(own, other)]
    late_thru = first * other_thru + (1.0 - first) * own_thru
    moved = cmul(halves(p256_ref), early)
    put_state(sent_ref, [late_thru * a + b for a, b in zip(moved, late)], own_thru * other_thru)


def put_pair(out_ref, side, own_ref, other_ref):
    rows = own_ref.shape[0]
    out_ref[pl.ds(pl.multiple_of(side * rows, rows), rows), :] = own_ref[...]
    out_ref[pl.ds(pl.multiple_of((1 - side) * rows, rows), rows), :] = other_ref[...]


def pair_kernel(own_ref, pair_ref, after_ref, out_ref):
    put_pair(out_ref, lax.axis_index("ctx") // (NC * NY) % 2, own_ref, pair_ref)


def row_kernel(own_ref, one_ref, two_ref, three_ref, p256_ref, pay_ref, before_ref, factor_ref, held):
    mine = (lax.axis_index("ctx") // NC) % NY
    for k, ref in enumerate((own_ref, one_ref, two_ref, three_ref)):
        there = lax.rem(mine - k + NY, NY)
        state, thru = get_state(ref)
        held[there, :MODES, :] = state[0]
        held[there, MODES:ROWS, :] = state[1]
        held[there, ROWS:, :] = jnp.broadcast_to(thru, (PAY - ROWS, CH))
    p512 = square(halves(p256_ref))
    state = (jnp.zeros((MODES, CH), F32),) * 2
    factor = (jnp.ones((MODES, CH), F32), jnp.zeros((MODES, CH), F32))
    thru = jnp.ones((1, CH), F32)
    for i in range(NY):
        @pl.when(mine == i)
        def put(state=state, factor=factor):
            before_ref[:MODES, :] = state[0]
            before_ref[MODES:, :] = state[1]
            factor_ref[:MODES, :] = factor[0]
            factor_ref[MODES:, :] = factor[1]
        open_ = held[i, ROWS:ROWS + 1, :]
        step = (open_ * p512[0], open_ * p512[1])
        state = cadd(cmul(step, state), (held[i, :MODES, :], held[i, MODES:ROWS, :]))
        factor = cmul(step, factor)
        thru = thru * open_
    pay_ref[:MODES, :] = state[0]
    pay_ref[MODES:ROWS, :] = state[1]
    pay_ref[ROWS:, :] = jnp.broadcast_to(thru, (PAY - ROWS, CH))


def gate_kernel(query_ref, y_ref, pz_ref, gz_ref, tre, tim, starts_ref, own_ref, other_ref, p256_ref,
                before_ref, factor_ref, one_ref, two_ref, hidden_ref, conv, sin):
    index = lax.axis_index("ctx")
    core, row = index % NC, index // (NC * NY)
    p256 = halves(p256_ref)
    p2048 = square(square(square(p256)))
    has_one = (row >= 1).astype(F32)
    has_two = (row >= 2).astype(F32)
    far = cmul(p2048, halves(two_ref))
    open_one = has_two * one_ref[ROWS:ROWS + 1, :]
    incoming = [has_one * a + open_one * b for a, b in zip(halves(one_ref), far)]
    state = cadd(halves(before_ref), cmul(halves(factor_ref), incoming))
    second = (core == 1).astype(F32)
    moved = cmul(p256, state)
    early_thru = other_ref[ROWS:ROWS + 1, :]
    state = [(1.0 - second) * a + second * (early_thru * b + c)
             for a, b, c in zip(state, moved, halves(other_ref))]
    for g in range(GROUPS):
        lanes = slice(g * LANES, (g + 1) * LANES)
        sin[g, :MODES, :] = state[0][:, lanes]
        sin[g, MODES:, :] = state[1][:, lanes]
    s0 = first_start(starts_ref)
    b0 = s0 // STEPS
    blocks = block_iota()

    def group(g, unused):
        z = []
        for m in range(MODES):
            s = (sin[g, m:m + 1, :], sin[g, MODES + m:MODES + m + 1, :])
            z.append(cadd((pz_ref[g, m], pz_ref[g, MODES + m]),
                          cmul((gz_ref[g, m], gz_ref[g, MODES + m]), s)))

        def step(j, unused):
            base = (j + 1) * MODES
            total = [None] * 4
            for m in range(MODES):
                term = tre[g, pl.ds(base + m, 1), :] * z[m][0] - tim[g, pl.ds(base + m, 1), :] * z[m][1]
                total[m % 4] = term if total[m % 4] is None else total[m % 4] + term
            total = (total[0] + total[1]) + (total[2] + total[3])
            late = (blocks * STEPS + j >= s0) & (blocks == b0)
            conv[g, pl.ds(j, BLOCKS, stride=STEPS), :] = y_ref[g, j] + jnp.where(late, 0.0, total)
            return unused

        return lax.fori_loop(0, STEPS, step, unused, unroll=16)

    lax.fori_loop(0, GROUPS, group, 0)
    for g in range(GROUPS):
        lanes = slice(g * LANES, (g + 1) * LANES)
        gated = (query_ref[:, lanes].astype(F32) * conv[g]).astype(BF16)
        for q in range(FOLD):
            hidden_ref[:, q * CH + g * LANES:q * CH + (g + 1) * LANES] = gated[q * THIN:(q + 1) * THIN]


def four_kernel(both_ref, pair_ref, after_ref, even_ref, odd_ref):
    side = (lax.axis_index("ctx") // NC) % 2
    even_ref[...] = jnp.where(side == 0, both_ref[...], pair_ref[...])
    odd_ref[...] = jnp.where(side == 0, pair_ref[...], both_ref[...])


def eight_kernel(even_ref, even_x, odd_ref, odd_y, after_up, after_down, all_ref, even_out, odd_out):
    n = even_ref.shape[0]
    for at, ref, out in ((0, even_ref, even_out), (0, odd_ref, odd_out), (n, even_x, even_out), (n, odd_y, odd_out)):
        out[at:at + n, :] = ref[...]
        start = at if out is even_out else 2 * n + at
        all_ref[start:start + n, :] = ref[...]


def join_kernel(even_ref, odd_ref, after_up, after_down, out_ref):
    n = even_ref.shape[0]
    out_ref[:n, :] = even_ref[...]
    out_ref[n:, :] = odd_ref[...]


def places(k):
    index = lax.axis_index("ctx")
    xb, yb = index // (NC * NY * 2), (index // NC) % NY // 2
    block = lax.rem(lax.axis_index("tp") - k + NZ, NZ)
    dx = (block // 4 != xb).astype(jnp.int32)
    dy = (lax.rem(block, 2) != yb).astype(jnp.int32)
    i = lax.rem(block // 2, 2)
    found = []
    for h in range(2):
        far, near = (dy, dx) if h == 0 else (dx, dy)
        at = far * 8 * WROWS + h * 4 * WROWS + near * 2 * WROWS + i * WROWS
        found.append(pl.ds(pl.multiple_of(at, WROWS), WROWS))
    return found


def most_kernel(here, up1, down1, up2, down2, up3, down3, near_own, far_own, near_other, total_ref, left_ref, left):
    core = lax.axis_index("ctx") % NC
    wide = 8 * WROWS
    for k, ref in enumerate((here, up1, up2, up3, None, down3, down2, down1)):
        for h, lanes in enumerate(places(k)):
            for c in range(NC):
                side = jnp.where(core == c, 0, 1)
                if ref is None:
                    left[side, :, lanes] = jnp.zeros((TOK, WROWS), BF16)
                    continue
                for q in range(FOLD):
                    at = slice(q * CH + (NC * h + c) * WROWS, q * CH + (NC * h + c + 1) * WROWS)
                    left[side, q * THIN:(q + 1) * THIN, lanes] = ref[:, at]
    total_ref[...] = (jnp.dot(left[0, :, :wide], near_own[...], preferred_element_type=F32)
                      + jnp.dot(left[0, :, wide:], far_own[...], preferred_element_type=F32)
                      + jnp.dot(left[1, :, :wide], near_other[...], preferred_element_type=F32))
    left_ref[...] = left[1, :, wide:]


def last_kernel(up4, down4, out_ref):
    for q in range(FOLD):
        middle = q * THIN + THIN // 2
        lanes = slice(q * CH, (q + 1) * CH)
        out_ref[q * THIN:middle, :] = up4[:, lanes]
        out_ref[middle:(q + 1) * THIN, :] = down4[:, lanes]


def rest_kernel(total_ref, left, last, near_own, near_other, own_ref, other_ref, out_ref, rows):
    core = lax.axis_index("ctx") % NC
    wide = 8 * WROWS
    for h, place in enumerate(places(4)):
        far = place.start >= wide
        at = pl.ds(pl.multiple_of(jnp.where(far, place.start - wide, place.start), WROWS), WROWS)
        for c in range(NC):
            lanes = slice((NC * h + c) * WROWS, (NC * h + c + 1) * WROWS)
            rows[lanes, :] = jnp.where(core == c, jnp.where(far, own_ref[at, :], near_own[at, :]),
                                       jnp.where(far, other_ref[at, :], near_other[at, :]))
    out_ref[...] = (total_ref[...] + jnp.dot(left[...], other_ref[...], preferred_element_type=F32)
                    + jnp.dot(last[...], rows[...], preferred_element_type=F32)).astype(BF16)


def ctx_index(x, y, c):
    return ((x % NX) * NY + y % NY) * NC + c % NC


def move(value, dx, dy, dc):
    pairs = [(ctx_index(x, y, c), ctx_index(x + dx, y + dy, c + dc))
             for x in range(NX) for y in range(NY) for c in range(NC)]
    return lax.ppermute(value, "ctx", pairs)


def trade(value, dx, dy):
    pairs = [(ctx_index(x, y, c), ctx_index(x ^ dx, y ^ dy, c))
             for x in range(NX) for y in range(NY) for c in range(NC)]
    return lax.ppermute(value, "ctx", pairs)


def turn(value, k):
    return lax.ppermute(value, "tp", [(i, (i + k) % NZ) for i in range(NZ)])


def shards(query, key, value, decay, freq, residue, skip, out_weight, doc_starts):
    starts = doc_starts.reshape(TOK // LANES, LANES)
    skip = skip.reshape(1, CH)
    sig = pltpu.VMEM((GROUPS, TOK, LANES), F32)
    qs = pltpu.VMEM((GROUPS, BLOCKS * MODES, LANES), F32)
    state_shape = struct(ROWS, CH)
    pay_shape = struct(PAY, CH)
    block_shape = struct(GROUPS, ROWS, BLOCKS, LANES)
    table = (GROUPS, (STEPS + 1) * MODES, LANES)

    magnitude = jnp.exp(-decay)
    q_shape = struct(GROUPS, BLOCKS * MODES, LANES)
    tre, tim, qre, qim, p256 = call(
        powers_kernel, (struct(*table), struct(*table), q_shape, q_shape, state_shape),
        (magnitude * jnp.cos(freq), magnitude * jnp.sin(freq)), (), 300000000, 5_000_000)
    pay, eb, signal = call(
        ends_kernel, (pay_shape, block_shape, struct(GROUPS, TOK, LANES)),
        (key, value, starts, tre, tim, qre, qim), (), 20_000_000, 5_000_000)
    other = move(pay, 0, 0, 1)
    chip = call(chip_kernel, struct(SENT, CH, dtype=BF16), (pay, other, p256))
    near = [move(chip, 0, k, 0) for k in (1, 2, 3)]
    row, before, factor = call(
        row_kernel, (pay_shape, state_shape, state_shape),
        (chip, *near, p256), [pltpu.VMEM((NY, PAY, CH), F32)])
    back = [move(row, k, 0, 0) for k in (1, 2)]
    y, gain = call(
        local_kernel, (struct(GROUPS, STEPS, BLOCKS, LANES), state_shape),
        (signal, tre, tim, decay, residue, skip, starts, chip),
        [pltpu.VMEM((GROUPS, STEPS, LANES), F32)], 30_000_000, 5_000_000)
    pz, gz = call(
        carry_kernel, (block_shape, block_shape), (eb, tre, tim, gain, starts),
        [qs, qs, pltpu.VMEM((GROUPS, 4 * ROWS, LANES), F32)], 30_000_000, 5_000_000)
    hidden = call(
        gate_kernel, struct(THIN, FOLD * CH, dtype=BF16),
        (query, y, pz, gz, tre, tim, starts, pay, other, p256, before, factor, *back),
        [sig, pltpu.VMEM((GROUPS, ROWS, LANES), F32)], 2_000_000_000, 5_000_000)

    both = call(pair_kernel, struct(2 * WROWS, CH, dtype=BF16), (out_weight, trade(out_weight, 1, 0), row))
    w2, w4, w8 = [struct(n * WROWS, CH, dtype=BF16) for n in (2, 4, 8)]
    even, odd = call(four_kernel, (w2, w2), (both, trade(both, 0, 1), hidden), (), 0, 2_000_000)
    half = THIN // 2
    up1, down1 = turn(hidden, 1), turn(hidden, -1)
    near, even, odd = call(
        eight_kernel, (w8, w4, w4), (even, trade(even, 2, 0), odd, trade(odd, 0, 2), up1, down1), (), 0, 4_000_000)
    up2, down2 = turn(up1, 1), turn(down1, -1)
    up3, down3 = turn(up2, 1), turn(down2, -1)
    up4, down4 = turn(up3[:half], 1), turn(down3[half:], -1)
    far = call(join_kernel, w8, (trade(even, 0, 2), trade(odd, 2, 0), up3, down3), (), 0, 2_000_000)
    near_other = move(near, 0, 0, 1)
    total, left = call(
        most_kernel, (struct(TOK, CH), struct(TOK, 8 * WROWS, dtype=BF16)),
        (hidden, up1, down1, up2, down2, up3, down3, near, far, near_other),
        [pltpu.VMEM((NC, TOK, NZ * CH // NC), BF16)], 8000000000, 7_000_000)
    last = call(last_kernel, struct(TOK, CH, dtype=BF16), (up4, down4), (), 8000000000, 1_000_000)
    return call(
        rest_kernel, struct(TOK, CH, dtype=BF16), (total, left, last, near, near_other, far, move(far, 0, 0, 1)),
        [pltpu.VMEM((CH, CH), BF16)], TOK * CH * CH * NZ, 7_000_000)


def solution(mesh):
    in_specs = (
        P("ctx", "tp"),
        P("ctx", "tp"),
        P("ctx", "tp"),
        P(None, "tp"),
        P(None, "tp"),
        P(None, None, "tp"),
        P("tp"),
        P("ctx", "tp"),
        P("ctx"),
    )
    return jax.shard_map(
        shards, mesh=mesh, in_specs=in_specs, out_specs=P("ctx", "tp"), check_vma=False
    )
```

```python
import jax
import jax.numpy as jnp
from jax import lax
from jax.experimental import pallas as pl
from jax.experimental.pallas import tpu as pltpu
from jax.sharding import PartitionSpec as P

F32 = jnp.float32
BF16 = jnp.bfloat16
NX, NY, NC, NZ = 4, 4, 2, 8
TOK, CH, MODES = 256, 512, 16
LANES = 128
GROUPS = CH // LANES
STEPS = 32
BLOCKS = TOK // STEPS
ROWS = 2 * MODES
PAY = ROWS + 8
VMEM = pl.BlockSpec(memory_space=pltpu.VMEM)
FLAG = 16
SENT = 2 * ROWS + FLAG
WROWS = 128
FOLD = 8
THIN = TOK // FOLD
PARAMS = pltpu.CompilerParams(vmem_limit_bytes=24 * 1024 * 1024)


def call(kernel, outs, args, scratch=(), flops=0, nbytes=0):
    return pl.pallas_call(
        kernel,
        out_shape=outs,
        in_specs=[VMEM] * len(args),
        out_specs=jax.tree.map(lambda unused: VMEM, outs),
        scratch_shapes=list(scratch),
        compiler_params=PARAMS,
        cost_estimate=pl.CostEstimate(flops=flops, bytes_accessed=nbytes, transcendentals=0),
    )(*args)


def struct(*shape, dtype=F32):
    return jax.ShapeDtypeStruct(shape, dtype)


def cmul(a, b):
    return a[0] * b[0] - a[1] * b[1], a[0] * b[1] + a[1] * b[0]


def cadd(a, b):
    return a[0] + b[0], a[1] + b[1]


def square(a):
    return a[0] * a[0] - a[1] * a[1], 2.0 * a[0] * a[1]


def halves(ref):
    return ref[:MODES, :], ref[MODES:ROWS, :]


def first_start(starts_ref):
    starts = starts_ref[...]
    at = lax.broadcasted_iota(jnp.int32, starts.shape, 0) * LANES
    at = at + lax.broadcasted_iota(jnp.int32, starts.shape, 1)
    where = jnp.where(starts > 0, at, TOK)
    return jnp.min(jnp.min(where, axis=1, keepdims=True), axis=0, keepdims=True)


def fill_powers(pole, table_re, table_im, count):
    def put(k, value):
        for g in range(GROUPS):
            rows = pl.ds(pl.multiple_of(k * MODES, MODES), MODES)
            lanes = slice(g * LANES, (g + 1) * LANES)
            table_re[g, rows, :] = value[0][:, lanes]
            table_im[g, rows, :] = value[1][:, lanes]

    def step(k, value):
        put(k, value)
        return cmul(value, pole)

    one = (jnp.ones((MODES, CH), F32), jnp.zeros((MODES, CH), F32))
    last = lax.fori_loop(0, count, step, one)
    return last


def fill_signal(key_ref, value_ref, sig):
    for g in range(GROUPS):
        lanes = slice(g * LANES, (g + 1) * LANES)
        sig[g] = key_ref[:, lanes].astype(F32) * value_ref[:, lanes].astype(F32)


def block_iota():
    return lax.broadcasted_iota(jnp.int32, (BLOCKS, LANES), 0)


def powers_kernel(pole_re, pole_im, tre, tim, qre, qim, p256_ref):
    fill_powers((pole_re[...], pole_im[...]), tre, tim, STEPS + 1)
    q = last_power(tre, tim)
    value = (jnp.ones((MODES, CH), F32), jnp.zeros((MODES, CH), F32))
    for n in range(BLOCKS):
        row = (BLOCKS - 1 - n) * MODES
        for g in range(GROUPS):
            lanes = slice(g * LANES, (g + 1) * LANES)
            qre[g, row:row + MODES, :] = value[0][:, lanes]
            qim[g, row:row + MODES, :] = value[1][:, lanes]
        value = cmul(value, q)
    p256_ref[:MODES, :] = value[0]
    p256_ref[MODES:, :] = value[1]


def ends_kernel(key_ref, value_ref, starts_ref, tre, tim, qre, qim, pay_ref, eb_ref, sig):
    s0 = first_start(starts_ref)
    b0 = s0 // STEPS
    fill_signal(key_ref, value_ref, sig)
    blocks = block_iota()
    reach = (s0 >= TOK) | (blocks >= b0)

    def group(g, unused):
        def step(j, acc):
            x = sig[g, pl.ds(j, BLOCKS, stride=STEPS), :]
            x = jnp.where((blocks * STEPS + j >= s0) | (blocks != b0), x, 0.0)
            base = (STEPS - 1 - j) * MODES
            out = []
            for m in range(MODES):
                out.append(acc[2 * m] + tre[g, pl.ds(base + m, 1), :] * x)
                out.append(acc[2 * m + 1] + tim[g, pl.ds(base + m, 1), :] * x)
            return tuple(out)

        zero = jnp.zeros((BLOCKS, LANES), F32)
        acc = lax.fori_loop(0, STEPS, step, (zero,) * ROWS, unroll=8)
        for m in range(MODES):
            re, im = acc[2 * m], acc[2 * m + 1]
            eb_ref[g, m] = re
            eb_ref[g, MODES + m] = im
            w = (qre[g, pl.ds(m, BLOCKS, stride=MODES), :], qim[g, pl.ds(m, BLOCKS, stride=MODES), :])
            end = cmul(w, (re, im))
            lanes = pl.ds(pl.multiple_of(g * LANES, LANES), LANES)
            pay_ref[pl.ds(m, 1), lanes] = jnp.sum(jnp.where(reach, end[0], 0.0), axis=0, keepdims=True)
            pay_ref[pl.ds(MODES + m, 1), lanes] = jnp.sum(jnp.where(reach, end[1], 0.0), axis=0, keepdims=True)
        return unused

    lax.fori_loop(0, GROUPS, group, 0)
    pay_ref[ROWS:, :] = jnp.broadcast_to((s0 >= TOK).astype(F32), (PAY - ROWS, CH))


def last_power(tre, tim):
    return [jnp.concatenate([t[g, STEPS * MODES:, :] for g in range(GROUPS)], axis=1) for t in (tre, tim)]


def local_kernel(sig, tre, tim, decay_ref, res_ref, skip_ref, starts_ref, after_ref,
                 y_ref, weight_ref, taps):
    s0 = first_start(starts_ref)
    b0 = s0 // STEPS
    blocks = block_iota()
    y = 2.0 * decay_ref[...]
    series = jnp.ones_like(y)
    for n in range(10, 1, -1):
        series = 1.0 - y * (1.0 / n) * series
    scale = jnp.sqrt(y * series)
    weight = (res_ref[0] * scale, res_ref[1] * scale)
    weight_ref[:MODES, :] = weight[0]
    weight_ref[MODES:, :] = weight[1]
    for g in range(GROUPS):
        lanes = slice(g * LANES, (g + 1) * LANES)
        w_re, w_im = weight[0][:, lanes], weight[1][:, lanes]
        for k in range(STEPS):
            term = w_re * tre[g, k * MODES:(k + 1) * MODES, :] - w_im * tim[g, k * MODES:(k + 1) * MODES, :]
            row = jnp.sum(term, axis=0, keepdims=True)
            if k == 0:
                row = row + skip_ref[:, lanes]
            taps[g, k:k + 1, :] = row

    def group(g, unused):
        tile = 8

        def fir(select):
            xs = []
            for j in range(STEPS):
                x = sig[g, pl.ds(j, BLOCKS, stride=STEPS), :]
                late = (blocks * STEPS + j >= s0) | (blocks != b0)
                xs.append(jnp.where(late if select else jnp.logical_not(late), x, 0.0))
            for top in range(0, STEPS, tile):
                acc = [jnp.zeros((BLOCKS, LANES), F32)] * tile
                for k in range(top + tile):
                    tap = taps[g, k:k + 1, :]
                    for i in range(tile):
                        if top + i - k >= 0:
                            acc[i] = acc[i] + tap * xs[top + i - k]
                for i in range(tile):
                    if select:
                        y_ref[g, top + i] = acc[i]
                    else:
                        early = (blocks * STEPS + top + i < s0) & (blocks == b0)
                        y_ref[g, top + i] = y_ref[g, top + i] + jnp.where(early, acc[i], 0.0)

        fir(True)
        fir(False)
        return unused

    lax.fori_loop(0, GROUPS, group, 0)


def carry_kernel(eb_ref, tre, tim, weight_ref, starts_ref, pz_ref, gz_ref, qre, qim, rows_):
    s0 = first_start(starts_ref)
    b0 = s0 // STEPS
    blocks = block_iota()
    weight = (weight_ref[:MODES, :], weight_ref[MODES:, :])
    q = last_power(tre, tim)
    value = weight
    for n in range(BLOCKS):
        for g in range(GROUPS):
            lanes = slice(g * LANES, (g + 1) * LANES)
            qre[g, n * MODES:(n + 1) * MODES, :] = value[0][:, lanes]
            qim[g, n * MODES:(n + 1) * MODES, :] = value[1][:, lanes]
        value = cmul(value, q)
    power = q
    for n in range(3):
        for g in range(GROUPS):
            lanes = slice(g * LANES, (g + 1) * LANES)
            rows_[g, n * ROWS:n * ROWS + MODES, :] = power[0][:, lanes]
            rows_[g, n * ROWS + MODES:(n + 1) * ROWS, :] = power[1][:, lanes]
        power = square(power)
    for g in range(GROUPS):
        lanes = slice(g * LANES, (g + 1) * LANES)
        rows_[g, 3 * ROWS:3 * ROWS + MODES, :] = weight[0][:, lanes]
        rows_[g, 3 * ROWS + MODES:4 * ROWS, :] = weight[1][:, lanes]

    keeps = []
    for n in range(3):
        s = 1 << n
        keeps.append((blocks >= s) & jnp.logical_not((blocks - s < b0) & (b0 <= blocks)))
    heard = blocks <= b0

    def group(g, unused):
        for m in range(MODES):
            state = (eb_ref[g, m], eb_ref[g, MODES + m])
            for n in range(3):
                moved = [jnp.where(keeps[n], pltpu.roll(part, 1 << n, 0), 0.0) for part in state]
                step = (rows_[g, n * ROWS + m:n * ROWS + m + 1, :],
                        rows_[g, n * ROWS + MODES + m:n * ROWS + MODES + m + 1, :])
                state = cadd(state, cmul(step, moved))
            before = [jnp.where(blocks >= 1, pltpu.roll(part, 1, 0), 0.0) for part in state]
            w = (rows_[g, 3 * ROWS + m:3 * ROWS + m + 1, :],
                 rows_[g, 3 * ROWS + MODES + m:3 * ROWS + MODES + m + 1, :])
            scaled = cmul(w, before)
            pz_ref[g, m] = scaled[0]
            pz_ref[g, MODES + m] = scaled[1]
            gz_ref[g, m] = jnp.where(heard, qre[g, pl.ds(m, BLOCKS, stride=MODES), :], 0.0)
            gz_ref[g, MODES + m] = jnp.where(heard, qim[g, pl.ds(m, BLOCKS, stride=MODES), :], 0.0)

        return unused

    lax.fori_loop(0, GROUPS, group, 0)


def put_state(ref, state, thru):
    for part, at in zip(state, (0, MODES)):
        high = part.astype(BF16)
        ref[at:at + MODES, :] = high
        ref[ROWS + at:ROWS + at + MODES, :] = (part - high.astype(F32)).astype(BF16)
    ref[2 * ROWS:SENT, :] = jnp.broadcast_to(thru, (FLAG, CH)).astype(BF16)


def get_state(ref):
    parts = [ref[at:at + MODES, :].astype(F32) + ref[ROWS + at:ROWS + at + MODES, :].astype(F32)
             for at in (0, MODES)]
    return parts, ref[2 * ROWS:SENT, :].astype(F32)[:1]


def chip_kernel(own_ref, other_ref, p256_ref, sent_ref):
    core = lax.axis_index("ctx") % NC
    first = (core == 0).astype(F32)
    own, other = halves(own_ref), halves(other_ref)
    own_thru, other_thru = own_ref[ROWS:ROWS + 1, :], other_ref[ROWS:ROWS + 1, :]
    early = [first * a + (1.0 - first) * b for a, b in zip(own, other)]
    late = [first * b + (1.0 - first) * a for a, b in zip(own, other)]
    late_thru = first * other_thru + (1.0 - first) * own_thru
    moved = cmul(halves(p256_ref), early)
    put_state(sent_ref, [late_thru * a + b for a, b in zip(moved, late)], own_thru * other_thru)


def put_pair(out_ref, side, own_ref, other_ref):
    rows = own_ref.shape[0]
    out_ref[pl.ds(pl.multiple_of(side * rows, rows), rows), :] = own_ref[...]
    out_ref[pl.ds(pl.multiple_of((1 - side) * rows, rows), rows), :] = other_ref[...]


def pair_kernel(own_ref, pair_ref, after_ref, out_ref):
    put_pair(out_ref, lax.axis_index("ctx") // (NC * NY * 2), own_ref, pair_ref)


def row_kernel(own_ref, one_ref, two_ref, three_ref, p256_ref, after_ref, pay_ref, before_ref, factor_ref, held):
    mine = (lax.axis_index("ctx") // NC) % NY
    for k, ref in enumerate((own_ref, one_ref, two_ref, three_ref)):
        there = lax.rem(mine - k + NY, NY)
        state, thru = get_state(ref)
        held[there, :MODES, :] = state[0]
        held[there, MODES:ROWS, :] = state[1]
        held[there, ROWS:, :] = jnp.broadcast_to(thru, (PAY - ROWS, CH))
    p512 = square(halves(p256_ref))
    state = (jnp.zeros((MODES, CH), F32),) * 2
    factor = (jnp.ones((MODES, CH), F32), jnp.zeros((MODES, CH), F32))
    thru = jnp.ones((1, CH), F32)
    for i in range(NY):
        @pl.when(mine == i)
        def put(state=state, factor=factor):
            before_ref[:MODES, :] = state[0]
            before_ref[MODES:, :] = state[1]
            factor_ref[:MODES, :] = factor[0]
            factor_ref[MODES:, :] = factor[1]
        open_ = held[i, ROWS:ROWS + 1, :]
        step = (open_ * p512[0], open_ * p512[1])
        state = cadd(cmul(step, state), (held[i, :MODES, :], held[i, MODES:ROWS, :]))
        factor = cmul(step, factor)
        thru = thru * open_
    pay_ref[:MODES, :] = state[0]
    pay_ref[MODES:ROWS, :] = state[1]
    pay_ref[ROWS:, :] = jnp.broadcast_to(thru, (PAY - ROWS, CH))


def gate_kernel(query_ref, y_ref, pz_ref, gz_ref, tre, tim, starts_ref, own_ref, other_ref, p256_ref,
                before_ref, factor_ref, one_ref, two_ref, hidden_ref, conv, sin):
    index = lax.axis_index("ctx")
    core, row = index % NC, index // (NC * NY)
    p256 = halves(p256_ref)
    p2048 = square(square(square(p256)))
    has_one = (row >= 1).astype(F32)
    has_two = (row >= 2).astype(F32)
    far = cmul(p2048, halves(two_ref))
    open_one = has_two * one_ref[ROWS:ROWS + 1, :]
    incoming = [has_one * a + open_one * b for a, b in zip(halves(one_ref), far)]
    state = cadd(halves(before_ref), cmul(halves(factor_ref), incoming))
    second = (core == 1).astype(F32)
    moved = cmul(p256, state)
    early_thru = other_ref[ROWS:ROWS + 1, :]
    state = [(1.0 - second) * a + second * (early_thru * b + c)
             for a, b, c in zip(state, moved, halves(other_ref))]
    for g in range(GROUPS):
        lanes = slice(g * LANES, (g + 1) * LANES)
        sin[g, :MODES, :] = state[0][:, lanes]
        sin[g, MODES:, :] = state[1][:, lanes]
    s0 = first_start(starts_ref)
    b0 = s0 // STEPS
    blocks = block_iota()

    def group(g, unused):
        z = []
        for m in range(MODES):
            s = (sin[g, m:m + 1, :], sin[g, MODES + m:MODES + m + 1, :])
            z.append(cadd((pz_ref[g, m], pz_ref[g, MODES + m]),
                          cmul((gz_ref[g, m], gz_ref[g, MODES + m]), s)))

        def step(j, unused):
            base = (j + 1) * MODES
            total = [None] * 4
            for m in range(MODES):
                term = tre[g, pl.ds(base + m, 1), :] * z[m][0] - tim[g, pl.ds(base + m, 1), :] * z[m][1]
                total[m % 4] = term if total[m % 4] is None else total[m % 4] + term
            total = (total[0] + total[1]) + (total[2] + total[3])
            late = (blocks * STEPS + j >= s0) & (blocks == b0)
            conv[g, pl.ds(j, BLOCKS, stride=STEPS), :] = y_ref[g, j] + jnp.where(late, 0.0, total)
            return unused

        return lax.fori_loop(0, STEPS, step, unused, unroll=16)

    lax.fori_loop(0, GROUPS, group, 0)
    for g in range(GROUPS):
        lanes = slice(g * LANES, (g + 1) * LANES)
        gated = (query_ref[:, lanes].astype(F32) * conv[g]).astype(BF16)
        for q in range(FOLD):
            hidden_ref[:, q * CH + g * LANES:q * CH + (g + 1) * LANES] = gated[q * THIN:(q + 1) * THIN]


def four_kernel(both_ref, pair_ref, after_ref, even_ref, odd_ref):
    side = (lax.axis_index("ctx") // NC) % NY // 2
    even_ref[...] = jnp.where(side == 0, both_ref[...], pair_ref[...])
    odd_ref[...] = jnp.where(side == 0, pair_ref[...], both_ref[...])


def eight_kernel(even_ref, even_x, odd_ref, odd_y, after_up, after_down, all_ref, even_out, odd_out):
    n = even_ref.shape[0]
    for at, ref, out in ((0, even_ref, even_out), (0, odd_ref, odd_out), (n, even_x, even_out), (n, odd_y, odd_out)):
        out[at:at + n, :] = ref[...]
        start = at if out is even_out else 2 * n + at
        all_ref[start:start + n, :] = ref[...]


def join_kernel(even_ref, odd_ref, after_up, after_down, out_ref):
    n = even_ref.shape[0]
    out_ref[:n, :] = even_ref[...]
    out_ref[n:, :] = odd_ref[...]


def places(k):
    index = lax.axis_index("ctx")
    x, y = index // (NC * NY), (index // NC) % NY
    block = lax.rem(lax.axis_index("tp") - k + NZ, NZ)
    odd, i = lax.rem(block, 2), block // 4
    dx = (lax.rem(block // 2, 2) != lax.rem(x, 2)).astype(jnp.int32)
    found = []
    for h in range(2):
        dy = (lax.rem(y, 2) != h).astype(jnp.int32)
        far, near = jnp.where(odd == 1, dx, dy), jnp.where(odd == 1, dy, dx)
        at = far * 8 * WROWS + odd * 4 * WROWS + near * 2 * WROWS + i * WROWS
        found.append(pl.ds(pl.multiple_of(at, WROWS), WROWS))
    return found


def most_kernel(here, up1, down1, up2, down2, up3, down3, near_own, far_own, near_other, total_ref, left_ref, left):
    core = lax.axis_index("ctx") % NC
    wide = 8 * WROWS
    for k, ref in enumerate((here, up1, up2, up3, None, down3, down2, down1)):
        for h, lanes in enumerate(places(k)):
            for c in range(NC):
                side = jnp.where(core == c, 0, 1)
                if ref is None:
                    left[side, :, lanes] = jnp.zeros((TOK, WROWS), BF16)
                    continue
                for q in range(FOLD):
                    at = slice(q * CH + (NC * h + c) * WROWS, q * CH + (NC * h + c + 1) * WROWS)
                    left[side, q * THIN:(q + 1) * THIN, lanes] = ref[:, at]
    total_ref[...] = (jnp.dot(left[0, :, :wide], near_own[...], preferred_element_type=F32)
                      + jnp.dot(left[0, :, wide:], far_own[...], preferred_element_type=F32)
                      + jnp.dot(left[1, :, :wide], near_other[...], preferred_element_type=F32))
    left_ref[...] = left[1, :, wide:]


def last_kernel(up4, down4, after_ref, out_ref):
    for q in range(FOLD):
        middle = q * THIN + THIN // 2
        lanes = slice(q * CH, (q + 1) * CH)
        out_ref[q * THIN:middle, :] = up4[:, lanes]
        out_ref[middle:(q + 1) * THIN, :] = down4[:, lanes]


def rest_kernel(total_ref, left, last, near_own, near_other, own_ref, other_ref, out_ref, rows):
    core = lax.axis_index("ctx") % NC
    wide = 8 * WROWS
    for h, place in enumerate(places(4)):
        far = place.start >= wide
        at = pl.ds(pl.multiple_of(jnp.where(far, place.start - wide, place.start), WROWS), WROWS)
        for c in range(NC):
            lanes = slice((NC * h + c) * WROWS, (NC * h + c + 1) * WROWS)
            rows[lanes, :] = jnp.where(core == c, jnp.where(far, own_ref[at, :], near_own[at, :]),
                                       jnp.where(far, other_ref[at, :], near_other[at, :]))
    out_ref[...] = (total_ref[...] + jnp.dot(left[...], other_ref[...], preferred_element_type=F32)
                    + jnp.dot(last[...], rows[...], preferred_element_type=F32)).astype(BF16)


def ctx_index(x, y, c):
    return ((x % NX) * NY + y % NY) * NC + c % NC


def move(value, dx, dy, dc):
    pairs = [(ctx_index(x, y, c), ctx_index(x + dx, y + dy, c + dc))
             for x in range(NX) for y in range(NY) for c in range(NC)]
    return lax.ppermute(value, "ctx", pairs)


def trade(value, dx, dy):
    pairs = [(ctx_index(x, y, c), ctx_index(x ^ dx, y ^ dy, c))
             for x in range(NX) for y in range(NY) for c in range(NC)]
    return lax.ppermute(value, "ctx", pairs)


def turn(value, k):
    return lax.ppermute(value, "tp", [(i, (i + k) % NZ) for i in range(NZ)])


def shards(query, key, value, decay, freq, residue, skip, out_weight, doc_starts):
    starts = doc_starts.reshape(TOK // LANES, LANES)
    skip = skip.reshape(1, CH)
    sig = pltpu.VMEM((GROUPS, TOK, LANES), F32)
    qs = pltpu.VMEM((GROUPS, BLOCKS * MODES, LANES), F32)
    state_shape = struct(ROWS, CH)
    pay_shape = struct(PAY, CH)
    block_shape = struct(GROUPS, ROWS, BLOCKS, LANES)
    table = (GROUPS, (STEPS + 1) * MODES, LANES)

    magnitude = jnp.exp(-decay)
    q_shape = struct(GROUPS, BLOCKS * MODES, LANES)
    tre, tim, qre, qim, p256 = call(
        powers_kernel, (struct(*table), struct(*table), q_shape, q_shape, state_shape),
        (magnitude * jnp.cos(freq), magnitude * jnp.sin(freq)), (), 300_000_000, 5_000_000)
    pay, eb, signal = call(
        ends_kernel, (pay_shape, block_shape, struct(GROUPS, TOK, LANES)),
        (key, value, starts, tre, tim, qre, qim), (), 20_000_000, 5_000_000)
    other = move(pay, 0, 0, 1)
    chip = call(chip_kernel, struct(SENT, CH, dtype=BF16), (pay, other, p256))
    near = [move(chip, 0, k, 0) for k in (1, 2, 3)]
    y, gain = call(
        local_kernel, (struct(GROUPS, STEPS, BLOCKS, LANES), state_shape),
        (signal, tre, tim, decay, residue, skip, starts, chip),
        [pltpu.VMEM((GROUPS, STEPS, LANES), F32)], 30_000_000, 5_000_000)
    row, before, factor = call(
        row_kernel, (pay_shape, state_shape, state_shape),
        (chip, *near, p256, gain), [pltpu.VMEM((NY, PAY, CH), F32)])
    back = [move(row, k, 0, 0) for k in (1, 2)]
    pz, gz = call(
        carry_kernel, (block_shape, block_shape), (eb, tre, tim, gain, starts),
        [qs, qs, pltpu.VMEM((GROUPS, 4 * ROWS, LANES), F32)], 30_000_000, 5_000_000)
    hidden = call(
        gate_kernel, struct(THIN, FOLD * CH, dtype=BF16),
        (query, y, pz, gz, tre, tim, starts, pay, other, p256, before, factor, *back),
        [sig, pltpu.VMEM((GROUPS, ROWS, LANES), F32)], 2_000_000_000, 5_000_000)

    both = call(pair_kernel, struct(2 * WROWS, CH, dtype=BF16), (out_weight, trade(out_weight, 2, 0), row))
    w2, w4, w8 = [struct(n * WROWS, CH, dtype=BF16) for n in (2, 4, 8)]
    even, odd = call(four_kernel, (w2, w2), (both, trade(both, 0, 2), hidden), (), 0, 2_000_000)
    half = THIN // 2
    up1, down1 = turn(hidden, 1), turn(hidden, -1)
    near, even, odd = call(
        eight_kernel, (w8, w4, w4), (even, trade(even, 1, 0), odd, trade(odd, 0, 1), up1, down1), (), 0, 4_000_000)
    up2, down2 = turn(up1, 1), turn(down1, -1)
    up3, down3 = turn(up2, 1), turn(down2, -1)
    up4, down4 = turn(up3[:half], 1), turn(down3[half:], -1)
    far = call(join_kernel, w8, (trade(even, 0, 1), trade(odd, 1, 0), up3, down3), (), 10000000000, 2_000_000)
    near_other = move(near, 0, 0, 1)
    total, left = call(
        most_kernel, (struct(TOK, CH), struct(TOK, 8 * WROWS, dtype=BF16)),
        (hidden, up1, down1, up2, down2, up3, down3, near, far, near_other),
        [pltpu.VMEM((NC, TOK, NZ * CH // NC), BF16)], 8000000000, 7_000_000)
    last = call(last_kernel, struct(TOK, CH, dtype=BF16), (up4, down4, total), (), 8000000000, 1_000_000)
    return call(
        rest_kernel, struct(TOK, CH, dtype=BF16), (total, left, last, near, near_other, far, move(far, 0, 0, 1)),
        [pltpu.VMEM((CH, CH), BF16)], TOK * CH * CH * NZ, 7_000_000)


def solution(mesh):
    in_specs = (
        P("ctx", "tp"),
        P("ctx", "tp"),
        P("ctx", "tp"),
        P(None, "tp"),
        P(None, "tp"),
        P(None, None, "tp"),
        P("tp"),
        P("ctx", "tp"),
        P("ctx"),
    )
    return jax.shard_map(
        shards, mesh=mesh, in_specs=in_specs, out_specs=P("ctx", "tp"), check_vma=False
    )
```

```python
import jax
import jax.numpy as jnp
from jax import lax
from jax.experimental import pallas as pl
from jax.experimental.pallas import tpu as pltpu
from jax.sharding import PartitionSpec as P

F32 = jnp.float32
BF16 = jnp.bfloat16
NX, NY, NC, NZ = 4, 4, 2, 8
TOK, CH, MODES = 256, 512, 16
LANES = 128
GROUPS = CH // LANES
STEPS = 32
BLOCKS = TOK // STEPS
ROWS = 2 * MODES
PAY = ROWS + 8
VMEM = pl.BlockSpec(memory_space=pltpu.VMEM)
FLAG = 16
SENT = 2 * ROWS + FLAG
WROWS = 128
FOLD = 8
THIN = TOK // FOLD
PARAMS = pltpu.CompilerParams(vmem_limit_bytes=24 * 1024 * 1024)


def call(kernel, outs, args, scratch=(), flops=0, nbytes=0):
    return pl.pallas_call(
        kernel,
        out_shape=outs,
        in_specs=[VMEM] * len(args),
        out_specs=jax.tree.map(lambda unused: VMEM, outs),
        scratch_shapes=list(scratch),
        compiler_params=PARAMS,
        cost_estimate=pl.CostEstimate(flops=flops, bytes_accessed=nbytes, transcendentals=0),
    )(*args)


def struct(*shape, dtype=F32):
    return jax.ShapeDtypeStruct(shape, dtype)


def cmul(a, b):
    return a[0] * b[0] - a[1] * b[1], a[0] * b[1] + a[1] * b[0]


def cadd(a, b):
    return a[0] + b[0], a[1] + b[1]


def square(a):
    return a[0] * a[0] - a[1] * a[1], 2.0 * a[0] * a[1]


def halves(ref):
    return ref[:MODES, :], ref[MODES:ROWS, :]


def first_start(starts_ref):
    starts = starts_ref[...]
    at = lax.broadcasted_iota(jnp.int32, starts.shape, 0) * LANES
    at = at + lax.broadcasted_iota(jnp.int32, starts.shape, 1)
    where = jnp.where(starts > 0, at, TOK)
    return jnp.min(jnp.min(where, axis=1, keepdims=True), axis=0, keepdims=True)


def fill_powers(pole, table_re, table_im, count):
    def put(k, value):
        for g in range(GROUPS):
            rows = pl.ds(pl.multiple_of(k * MODES, MODES), MODES)
            lanes = slice(g * LANES, (g + 1) * LANES)
            table_re[g, rows, :] = value[0][:, lanes]
            table_im[g, rows, :] = value[1][:, lanes]

    def step(k, value):
        put(k, value)
        return cmul(value, pole)

    one = (jnp.ones((MODES, CH), F32), jnp.zeros((MODES, CH), F32))
    last = lax.fori_loop(0, count, step, one)
    return last


def fill_signal(key_ref, value_ref, sig):
    for g in range(GROUPS):
        lanes = slice(g * LANES, (g + 1) * LANES)
        sig[g] = key_ref[:, lanes].astype(F32) * value_ref[:, lanes].astype(F32)


def block_iota():
    return lax.broadcasted_iota(jnp.int32, (BLOCKS, LANES), 0)


def powers_kernel(pole_re, pole_im, tre, tim, p256_ref):
    fill_powers((pole_re[...], pole_im[...]), tre, tim, STEPS + 1)
    value = square(square(square(last_power(tre, tim))))
    p256_ref[:MODES, :] = value[0]
    p256_ref[MODES:, :] = value[1]


def ends_kernel(key_ref, value_ref, starts_ref, tre, tim, pay_ref, eb_ref, sig):
    s0 = first_start(starts_ref)
    b0 = s0 // STEPS
    fill_signal(key_ref, value_ref, sig)
    blocks = block_iota()

    def group(g, unused):
        def step(j, acc):
            x = sig[g, pl.ds(j, BLOCKS, stride=STEPS), :]
            x = jnp.where((blocks * STEPS + j >= s0) | (blocks != b0), x, 0.0)
            base = (STEPS - 1 - j) * MODES
            out = []
            for m in range(MODES):
                out.append(acc[2 * m] + tre[g, pl.ds(base + m, 1), :] * x)
                out.append(acc[2 * m + 1] + tim[g, pl.ds(base + m, 1), :] * x)
            return tuple(out)

        zero = jnp.zeros((BLOCKS, LANES), F32)
        acc = lax.fori_loop(0, STEPS, step, (zero,) * ROWS, unroll=8)
        for m in range(MODES):
            eb_ref[g, m * BLOCKS:(m + 1) * BLOCKS, :] = acc[2 * m]
            eb_ref[g, (MODES + m) * BLOCKS:(MODES + m + 1) * BLOCKS, :] = acc[2 * m + 1]
        q = (tre[g, STEPS * MODES:, :], tim[g, STEPS * MODES:, :])
        state = (jnp.zeros((MODES, LANES), F32),) * 2
        for n in range(BLOCKS):
            state = [jnp.where(b0 == n, 0.0, part) for part in state]
            add = [eb_ref[g, pl.ds(at * BLOCKS + n, MODES, stride=BLOCKS), :] for at in (0, MODES)]
            state = cadd(cmul(q, state), add)
        lanes = pl.ds(pl.multiple_of(g * LANES, LANES), LANES)
        pay_ref[:MODES, lanes] = state[0]
        pay_ref[MODES:ROWS, lanes] = state[1]
        return unused

    lax.fori_loop(0, GROUPS, group, 0)
    pay_ref[ROWS:, :] = jnp.broadcast_to((s0 >= TOK).astype(F32), (PAY - ROWS, CH))


def last_power(tre, tim):
    return [jnp.concatenate([t[g, STEPS * MODES:, :] for g in range(GROUPS)], axis=1) for t in (tre, tim)]


def local_kernel(sig, tre, tim, decay_ref, res_ref, skip_ref, starts_ref, after_ref,
                 y_ref, weight_ref, taps):
    s0 = first_start(starts_ref)
    b0 = s0 // STEPS
    blocks = block_iota()
    y = 2.0 * decay_ref[...]
    series = jnp.ones_like(y)
    for n in range(10, 1, -1):
        series = 1.0 - y * (1.0 / n) * series
    scale = jnp.sqrt(y * series)
    weight = (res_ref[0] * scale, res_ref[1] * scale)
    weight_ref[:MODES, :] = weight[0]
    weight_ref[MODES:, :] = weight[1]
    for g in range(GROUPS):
        lanes = slice(g * LANES, (g + 1) * LANES)
        w_re, w_im = weight[0][:, lanes], weight[1][:, lanes]
        for k in range(STEPS):
            term = w_re * tre[g, k * MODES:(k + 1) * MODES, :] - w_im * tim[g, k * MODES:(k + 1) * MODES, :]
            row = jnp.sum(term, axis=0, keepdims=True)
            if k == 0:
                row = row + skip_ref[:, lanes]
            taps[g, k:k + 1, :] = row

    def group(g, unused):
        tile = 8

        def fir(select):
            xs = []
            for j in range(STEPS):
                x = sig[g, pl.ds(j, BLOCKS, stride=STEPS), :]
                late = (blocks * STEPS + j >= s0) | (blocks != b0)
                xs.append(jnp.where(late if select else jnp.logical_not(late), x, 0.0))
            for top in range(0, STEPS, tile):
                acc = [jnp.zeros((BLOCKS, LANES), F32)] * tile
                for k in range(top + tile):
                    tap = taps[g, k:k + 1, :]
                    for i in range(tile):
                        if top + i - k >= 0:
                            acc[i] = acc[i] + tap * xs[top + i - k]
                for i in range(tile):
                    if select:
                        y_ref[g, top + i] = acc[i]
                    else:
                        early = (blocks * STEPS + top + i < s0) & (blocks == b0)
                        y_ref[g, top + i] = y_ref[g, top + i] + jnp.where(early, acc[i], 0.0)

        fir(True)
        fir(False)
        return unused

    lax.fori_loop(0, GROUPS, group, 0)


def carry_kernel(eb_ref, tre, tim, weight_ref, starts_ref, pz_ref, gz_ref, qre, qim, rows_):
    s0 = first_start(starts_ref)
    b0 = s0 // STEPS
    blocks = block_iota()
    weight = (weight_ref[:MODES, :], weight_ref[MODES:, :])
    q = last_power(tre, tim)
    value = weight
    for n in range(BLOCKS):
        for g in range(GROUPS):
            lanes = slice(g * LANES, (g + 1) * LANES)
            qre[g, n * MODES:(n + 1) * MODES, :] = value[0][:, lanes]
            qim[g, n * MODES:(n + 1) * MODES, :] = value[1][:, lanes]
        value = cmul(value, q)
    power = q
    for n in range(3):
        for g in range(GROUPS):
            lanes = slice(g * LANES, (g + 1) * LANES)
            rows_[g, n * ROWS:n * ROWS + MODES, :] = power[0][:, lanes]
            rows_[g, n * ROWS + MODES:(n + 1) * ROWS, :] = power[1][:, lanes]
        power = square(power)
    for g in range(GROUPS):
        lanes = slice(g * LANES, (g + 1) * LANES)
        rows_[g, 3 * ROWS:3 * ROWS + MODES, :] = weight[0][:, lanes]
        rows_[g, 3 * ROWS + MODES:4 * ROWS, :] = weight[1][:, lanes]

    keeps = []
    for n in range(3):
        s = 1 << n
        keeps.append((blocks >= s) & jnp.logical_not((blocks - s < b0) & (b0 <= blocks)))
    heard = blocks <= b0

    def group(g, unused):
        for m in range(MODES):
            state = (eb_ref[g, m * BLOCKS:(m + 1) * BLOCKS, :],
                     eb_ref[g, (MODES + m) * BLOCKS:(MODES + m + 1) * BLOCKS, :])
            for n in range(3):
                moved = [jnp.where(keeps[n], pltpu.roll(part, 1 << n, 0), 0.0) for part in state]
                step = (rows_[g, n * ROWS + m:n * ROWS + m + 1, :],
                        rows_[g, n * ROWS + MODES + m:n * ROWS + MODES + m + 1, :])
                state = cadd(state, cmul(step, moved))
            before = [jnp.where(blocks >= 1, pltpu.roll(part, 1, 0), 0.0) for part in state]
            w = (rows_[g, 3 * ROWS + m:3 * ROWS + m + 1, :],
                 rows_[g, 3 * ROWS + MODES + m:3 * ROWS + MODES + m + 1, :])
            scaled = cmul(w, before)
            pz_ref[g, m] = scaled[0]
            pz_ref[g, MODES + m] = scaled[1]
            gz_ref[g, m] = jnp.where(heard, qre[g, pl.ds(m, BLOCKS, stride=MODES), :], 0.0)
            gz_ref[g, MODES + m] = jnp.where(heard, qim[g, pl.ds(m, BLOCKS, stride=MODES), :], 0.0)

        return unused

    lax.fori_loop(0, GROUPS, group, 0)


def put_state(ref, state, thru):
    for part, at in zip(state, (0, MODES)):
        high = part.astype(BF16)
        ref[at:at + MODES, :] = high
        ref[ROWS + at:ROWS + at + MODES, :] = (part - high.astype(F32)).astype(BF16)
    ref[2 * ROWS:SENT, :] = jnp.broadcast_to(thru, (FLAG, CH)).astype(BF16)


def get_state(ref):
    parts = [ref[at:at + MODES, :].astype(F32) + ref[ROWS + at:ROWS + at + MODES, :].astype(F32)
             for at in (0, MODES)]
    return parts, ref[2 * ROWS:SENT, :].astype(F32)[:1]


def chip_kernel(own_ref, other_ref, p256_ref, sent_ref):
    core = lax.axis_index("ctx") % NC
    first = (core == 0).astype(F32)
    own, other = halves(own_ref), halves(other_ref)
    own_thru, other_thru = own_ref[ROWS:ROWS + 1, :], other_ref[ROWS:ROWS + 1, :]
    early = [first * a + (1.0 - first) * b for a, b in zip(own, other)]
    late = [first * b + (1.0 - first) * a for a, b in zip(own, other)]
    late_thru = first * other_thru + (1.0 - first) * own_thru
    moved = cmul(halves(p256_ref), early)
    put_state(sent_ref, [late_thru * a + b for a, b in zip(moved, late)], own_thru * other_thru)


def put_pair(out_ref, side, own_ref, other_ref):
    rows = own_ref.shape[0]
    out_ref[pl.ds(pl.multiple_of(side * rows, rows), rows), :] = own_ref[...]
    out_ref[pl.ds(pl.multiple_of((1 - side) * rows, rows), rows), :] = other_ref[...]


def pair_kernel(own_ref, pair_ref, after_ref, out_ref):
    put_pair(out_ref, lax.axis_index("ctx") // (NC * NY) % 2, own_ref, pair_ref)


def row_kernel(own_ref, one_ref, two_ref, three_ref, p256_ref, after_ref, pay_ref, before_ref, factor_ref, held):
    mine = (lax.axis_index("ctx") // NC) % NY
    for k, ref in enumerate((own_ref, one_ref, two_ref, three_ref)):
        there = lax.rem(mine - k + NY, NY)
        state, thru = get_state(ref)
        held[there, :MODES, :] = state[0]
        held[there, MODES:ROWS, :] = state[1]
        held[there, ROWS:, :] = jnp.broadcast_to(thru, (PAY - ROWS, CH))
    p512 = square(halves(p256_ref))
    state = (jnp.zeros((MODES, CH), F32),) * 2
    factor = (jnp.ones((MODES, CH), F32), jnp.zeros((MODES, CH), F32))
    thru = jnp.ones((1, CH), F32)
    for i in range(NY):
        @pl.when(mine == i)
        def put(state=state, factor=factor):
            before_ref[:MODES, :] = state[0]
            before_ref[MODES:, :] = state[1]
            factor_ref[:MODES, :] = factor[0]
            factor_ref[MODES:, :] = factor[1]
        open_ = held[i, ROWS:ROWS + 1, :]
        step = (open_ * p512[0], open_ * p512[1])
        state = cadd(cmul(step, state), (held[i, :MODES, :], held[i, MODES:ROWS, :]))
        factor = cmul(step, factor)
        thru = thru * open_
    pay_ref[:MODES, :] = state[0]
    pay_ref[MODES:ROWS, :] = state[1]
    pay_ref[ROWS:, :] = jnp.broadcast_to(thru, (PAY - ROWS, CH))


def gate_kernel(query_ref, y_ref, pz_ref, gz_ref, tre, tim, starts_ref, own_ref, other_ref, p256_ref,
                before_ref, factor_ref, one_ref, two_ref, hidden_ref, conv, sin):
    index = lax.axis_index("ctx")
    core, row = index % NC, index // (NC * NY)
    p256 = halves(p256_ref)
    p2048 = square(square(square(p256)))
    has_one = (row >= 1).astype(F32)
    has_two = (row >= 2).astype(F32)
    far = cmul(p2048, halves(two_ref))
    open_one = has_two * one_ref[ROWS:ROWS + 1, :]
    incoming = [has_one * a + open_one * b for a, b in zip(halves(one_ref), far)]
    state = cadd(halves(before_ref), cmul(halves(factor_ref), incoming))
    second = (core == 1).astype(F32)
    moved = cmul(p256, state)
    early_thru = other_ref[ROWS:ROWS + 1, :]
    state = [(1.0 - second) * a + second * (early_thru * b + c)
             for a, b, c in zip(state, moved, halves(other_ref))]
    for g in range(GROUPS):
        lanes = slice(g * LANES, (g + 1) * LANES)
        sin[g, :MODES, :] = state[0][:, lanes]
        sin[g, MODES:, :] = state[1][:, lanes]
    s0 = first_start(starts_ref)
    b0 = s0 // STEPS
    blocks = block_iota()

    def group(g, unused):
        z = []
        for m in range(MODES):
            s = (sin[g, m:m + 1, :], sin[g, MODES + m:MODES + m + 1, :])
            z.append(cadd((pz_ref[g, m], pz_ref[g, MODES + m]),
                          cmul((gz_ref[g, m], gz_ref[g, MODES + m]), s)))

        def step(j, unused):
            base = (j + 1) * MODES
            total = [None] * 4
            for m in range(MODES):
                term = tre[g, pl.ds(base + m, 1), :] * z[m][0] - tim[g, pl.ds(base + m, 1), :] * z[m][1]
                total[m % 4] = term if total[m % 4] is None else total[m % 4] + term
            total = (total[0] + total[1]) + (total[2] + total[3])
            late = (blocks * STEPS + j >= s0) & (blocks == b0)
            conv[g, pl.ds(j, BLOCKS, stride=STEPS), :] = y_ref[g, j] + jnp.where(late, 0.0, total)
            return unused

        return lax.fori_loop(0, STEPS, step, unused, unroll=16)

    lax.fori_loop(0, GROUPS, group, 0)
    for g in range(GROUPS):
        lanes = slice(g * LANES, (g + 1) * LANES)
        gated = (query_ref[:, lanes].astype(F32) * conv[g]).astype(BF16)
        for q in range(FOLD):
            hidden_ref[:, q * CH + g * LANES:q * CH + (g + 1) * LANES] = gated[q * THIN:(q + 1) * THIN]


def four_kernel(both_ref, pair_ref, after_ref, even_ref, odd_ref):
    side = (lax.axis_index("ctx") // NC) % NY // 2
    even_ref[...] = jnp.where(side == 0, both_ref[...], pair_ref[...])
    odd_ref[...] = jnp.where(side == 0, pair_ref[...], both_ref[...])


def eight_kernel(even_ref, even_x, odd_ref, odd_y, after_up, after_down, all_ref, even_out, odd_out):
    n = even_ref.shape[0]
    for at, ref, out in ((0, even_ref, even_out), (0, odd_ref, odd_out), (n, even_x, even_out), (n, odd_y, odd_out)):
        out[at:at + n, :] = ref[...]
        start = at if out is even_out else 2 * n + at
        all_ref[start:start + n, :] = ref[...]


def join_kernel(even_ref, odd_ref, after_up, after_down, out_ref):
    n = even_ref.shape[0]
    out_ref[:n, :] = even_ref[...]
    out_ref[n:, :] = odd_ref[...]


def places(k):
    index = lax.axis_index("ctx")
    x, y = index // (NC * NY), (index // NC) % NY
    block = lax.rem(lax.axis_index("tp") - k + NZ, NZ)
    odd, i = lax.rem(block, 2), lax.rem(block // 2, 2)
    dx = (block // 4 != x // 2).astype(jnp.int32)
    found = []
    for h in range(2):
        dy = (lax.rem(y, 2) != h).astype(jnp.int32)
        far, near = jnp.where(odd == 1, dx, dy), jnp.where(odd == 1, dy, dx)
        at = far * 8 * WROWS + odd * 4 * WROWS + near * 2 * WROWS + i * WROWS
        found.append(pl.ds(pl.multiple_of(at, WROWS), WROWS))
    return found


def most_kernel(here, up1, down1, up2, down2, up3, down3, near_own, far_own, near_other, total_ref, left_ref, left):
    core = lax.axis_index("ctx") % NC
    wide = 8 * WROWS
    for k, ref in enumerate((here, up1, up2, up3, None, down3, down2, down1)):
        for h, lanes in enumerate(places(k)):
            for c in range(NC):
                side = jnp.where(core == c, 0, 1)
                if ref is None:
                    left[side, :, lanes] = jnp.zeros((TOK, WROWS), BF16)
                    continue
                for q in range(FOLD):
                    at = slice(q * CH + (NC * h + c) * WROWS, q * CH + (NC * h + c + 1) * WROWS)
                    left[side, q * THIN:(q + 1) * THIN, lanes] = ref[:, at]
    total_ref[...] = (jnp.dot(left[0, :, :wide], near_own[...], preferred_element_type=F32)
                      + jnp.dot(left[0, :, wide:], far_own[...], preferred_element_type=F32)
                      + jnp.dot(left[1, :, :wide], near_other[...], preferred_element_type=F32))
    left_ref[...] = left[1, :, wide:]


def last_kernel(up4, down4, after_ref, out_ref):
    for q in range(FOLD):
        middle = q * THIN + THIN // 2
        lanes = slice(q * CH, (q + 1) * CH)
        out_ref[q * THIN:middle, :] = up4[:, lanes]
        out_ref[middle:(q + 1) * THIN, :] = down4[:, lanes]


def rest_kernel(total_ref, left, last, near_own, near_other, own_ref, other_ref, out_ref, rows):
    core = lax.axis_index("ctx") % NC
    wide = 8 * WROWS
    for h, place in enumerate(places(4)):
        far = place.start >= wide
        at = pl.ds(pl.multiple_of(jnp.where(far, place.start - wide, place.start), WROWS), WROWS)
        for c in range(NC):
            lanes = slice((NC * h + c) * WROWS, (NC * h + c + 1) * WROWS)
            rows[lanes, :] = jnp.where(core == c, jnp.where(far, own_ref[at, :], near_own[at, :]),
                                       jnp.where(far, other_ref[at, :], near_other[at, :]))
    out_ref[...] = (total_ref[...] + jnp.dot(left[...], other_ref[...], preferred_element_type=F32)
                    + jnp.dot(last[...], rows[...], preferred_element_type=F32)).astype(BF16)


def ctx_index(x, y, c):
    return ((x % NX) * NY + y % NY) * NC + c % NC


def move(value, dx, dy, dc):
    pairs = [(ctx_index(x, y, c), ctx_index(x + dx, y + dy, c + dc))
             for x in range(NX) for y in range(NY) for c in range(NC)]
    return lax.ppermute(value, "ctx", pairs)


def trade(value, dx, dy):
    pairs = [(ctx_index(x, y, c), ctx_index(x ^ dx, y ^ dy, c))
             for x in range(NX) for y in range(NY) for c in range(NC)]
    return lax.ppermute(value, "ctx", pairs)


def turn(value, k):
    return lax.ppermute(value, "tp", [(i, (i + k) % NZ) for i in range(NZ)])


def shards(query, key, value, decay, freq, residue, skip, out_weight, doc_starts):
    starts = doc_starts.reshape(TOK // LANES, LANES)
    skip = skip.reshape(1, CH)
    sig = pltpu.VMEM((GROUPS, TOK, LANES), F32)
    qs = pltpu.VMEM((GROUPS, BLOCKS * MODES, LANES), F32)
    state_shape = struct(ROWS, CH)
    pay_shape = struct(PAY, CH)
    block_shape = struct(GROUPS, ROWS, BLOCKS, LANES)
    table = (GROUPS, (STEPS + 1) * MODES, LANES)

    magnitude = jnp.exp(-decay)
    tre, tim, p256 = call(
        powers_kernel, (struct(*table), struct(*table), state_shape),
        (magnitude * jnp.cos(freq), magnitude * jnp.sin(freq)), (), 300_000_000, 5_000_000)
    pay, eb, signal = call(
        ends_kernel, (pay_shape, struct(GROUPS, ROWS * BLOCKS, LANES), struct(GROUPS, TOK, LANES)),
        (key, value, starts, tre, tim), (), 20_000_000, 5_000_000)
    other = move(pay, 0, 0, 1)
    chip = call(chip_kernel, struct(SENT, CH, dtype=BF16), (pay, other, p256))
    near = [move(chip, 0, k, 0) for k in (1, 2, 3)]
    y, gain = call(
        local_kernel, (struct(GROUPS, STEPS, BLOCKS, LANES), state_shape),
        (signal, tre, tim, decay, residue, skip, starts, chip),
        [pltpu.VMEM((GROUPS, STEPS, LANES), F32)], 30_000_000, 5_000_000)
    row, before, factor = call(
        row_kernel, (pay_shape, state_shape, state_shape),
        (chip, *near, p256, gain), [pltpu.VMEM((NY, PAY, CH), F32)])
    back = [move(row, k, 0, 0) for k in (1, 2)]
    pz, gz = call(
        carry_kernel, (block_shape, block_shape), (eb, tre, tim, gain, starts),
        [qs, qs, pltpu.VMEM((GROUPS, 4 * ROWS, LANES), F32)], 30_000_000, 5_000_000)
    hidden = call(
        gate_kernel, struct(THIN, FOLD * CH, dtype=BF16),
        (query, y, pz, gz, tre, tim, starts, pay, other, p256, before, factor, *back),
        [sig, pltpu.VMEM((GROUPS, ROWS, LANES), F32)], 2_000_000_000, 5_000_000)

    both = call(pair_kernel, struct(2 * WROWS, CH, dtype=BF16), (out_weight, trade(out_weight, 1, 0), row))
    w2, w4, w8 = [struct(n * WROWS, CH, dtype=BF16) for n in (2, 4, 8)]
    even, odd = call(four_kernel, (w2, w2), (both, trade(both, 0, 2), hidden), (), 0, 2_000_000)
    half = THIN // 2
    up1, down1 = turn(hidden, 1), turn(hidden, -1)
    near, even, odd = call(
        eight_kernel, (w8, w4, w4), (even, trade(even, 2, 0), odd, trade(odd, 0, 1), up1, down1), (), 0, 4_000_000)
    up2, down2 = turn(up1, 1), turn(down1, -1)
    up3, down3 = turn(up2, 1), turn(down2, -1)
    up4, down4 = turn(up3[:half], 1), turn(down3[half:], -1)
    far = call(join_kernel, w8, (trade(even, 0, 1), trade(odd, 2, 0), up3, down3), (), 10000000000, 2_000_000)
    near_other = move(near, 0, 0, 1)
    total, left = call(
        most_kernel, (struct(TOK, CH), struct(TOK, 8 * WROWS, dtype=BF16)),
        (hidden, up1, down1, up2, down2, up3, down3, near, far, near_other),
        [pltpu.VMEM((NC, TOK, NZ * CH // NC), BF16)], 8000000000, 7_000_000)
    last = call(last_kernel, struct(TOK, CH, dtype=BF16), (up4, down4, total), (), 8000000000, 1_000_000)
    return call(
        rest_kernel, struct(TOK, CH, dtype=BF16), (total, left, last, near, near_other, far, move(far, 0, 0, 1)),
        [pltpu.VMEM((CH, CH), BF16)], TOK * CH * CH * NZ, 7_000_000)


def solution(mesh):
    in_specs = (
        P("ctx", "tp"),
        P("ctx", "tp"),
        P("ctx", "tp"),
        P(None, "tp"),
        P(None, "tp"),
        P(None, None, "tp"),
        P("tp"),
        P("ctx", "tp"),
        P("ctx"),
    )
    return jax.shard_map(
        shards, mesh=mesh, in_specs=in_specs, out_specs=P("ctx", "tp"), check_vma=False
    )
```

```python
import jax
import jax.numpy as jnp
from jax import lax
from jax.experimental import pallas as pl
from jax.experimental.pallas import tpu as pltpu
from jax.sharding import PartitionSpec as P

F32 = jnp.float32
BF16 = jnp.bfloat16
NX, NY, NC, NZ = 4, 4, 2, 8
TOK, CH, MODES = 256, 512, 16
LANES = 128
GROUPS = CH // LANES
STEPS = 32
BLOCKS = TOK // STEPS
HALF = STEPS // 2
ROWS = 2 * MODES
PAY = ROWS + 8
VMEM = pl.BlockSpec(memory_space=pltpu.VMEM)
FLAG = 16
SENT = 2 * ROWS + FLAG
WROWS = 128
FOLD = 8
THIN = TOK // FOLD
PARAMS = pltpu.CompilerParams(vmem_limit_bytes=24 * 1024 * 1024)


def call(kernel, outs, args, scratch=(), flops=0, nbytes=0):
    return pl.pallas_call(
        kernel,
        out_shape=outs,
        in_specs=[VMEM] * len(args),
        out_specs=jax.tree.map(lambda unused: VMEM, outs),
        scratch_shapes=list(scratch),
        compiler_params=PARAMS,
        cost_estimate=pl.CostEstimate(flops=flops, bytes_accessed=nbytes, transcendentals=0),
    )(*args)


def struct(*shape, dtype=F32):
    return jax.ShapeDtypeStruct(shape, dtype)


def cmul(a, b):
    return a[0] * b[0] - a[1] * b[1], a[0] * b[1] + a[1] * b[0]


def cadd(a, b):
    return a[0] + b[0], a[1] + b[1]


def square(a):
    return a[0] * a[0] - a[1] * a[1], 2.0 * a[0] * a[1]


def halves(ref):
    return ref[:MODES, :], ref[MODES:ROWS, :]


def first_start(starts_ref):
    starts = starts_ref[...]
    at = lax.broadcasted_iota(jnp.int32, starts.shape, 0) * LANES
    at = at + lax.broadcasted_iota(jnp.int32, starts.shape, 1)
    where = jnp.where(starts > 0, at, TOK)
    return jnp.min(jnp.min(where, axis=1, keepdims=True), axis=0, keepdims=True)


def fill_powers(pole, table_re, table_im, count):
    def put(k, value):
        for g in range(GROUPS):
            rows = pl.ds(pl.multiple_of(k * MODES, MODES), MODES)
            lanes = slice(g * LANES, (g + 1) * LANES)
            table_re[g, rows, :] = value[0][:, lanes]
            table_im[g, rows, :] = value[1][:, lanes]

    def step(k, value):
        put(k, value)
        return cmul(value, pole)

    one = (jnp.ones((MODES, CH), F32), jnp.zeros((MODES, CH), F32))
    last = lax.fori_loop(0, count, step, one)
    return last


def fill_signal(key_ref, value_ref, sig):
    for g in range(GROUPS):
        lanes = slice(g * LANES, (g + 1) * LANES)
        sig[g] = key_ref[:, lanes].astype(F32) * value_ref[:, lanes].astype(F32)


def block_iota():
    return lax.broadcasted_iota(jnp.int32, (BLOCKS, LANES), 0)


def powers_kernel(pole_re, pole_im, tre, tim, p256_ref):
    fill_powers((pole_re[...], pole_im[...]), tre, tim, STEPS + 1)
    value = square(square(square(last_power(tre, tim))))
    p256_ref[:MODES, :] = value[0]
    p256_ref[MODES:, :] = value[1]


def table_row(tre, tim, g, at):
    return [jnp.broadcast_to(t[g, pl.ds(at, 1), :], (BLOCKS, LANES)) for t in (tre, tim)]


def ends_kernel(key_ref, value_ref, starts_ref, tre, tim, pay_ref, eb_ref, sig):
    s0 = first_start(starts_ref)
    b0 = s0 // STEPS
    fill_signal(key_ref, value_ref, sig)
    blocks = block_iota()

    def group(g, unused):
        zero = jnp.zeros((BLOCKS, LANES), F32)
        for low in range(0, MODES, MODES // 2):
            def step(j, acc, low=low):
                xs = []
                for at in (j, j + HALF):
                    x = sig[g, pl.ds(at, BLOCKS, stride=STEPS), :]
                    xs.append(jnp.where((blocks * STEPS + at >= s0) | (blocks != b0), x, 0.0))
                base = (HALF - 1 - j) * MODES + low
                out = []
                for m in range(MODES // 2):
                    row = table_row(tre, tim, g, base + m)
                    for n in range(4):
                        out.append(acc[4 * m + n] + row[n % 2] * xs[n // 2])
                return tuple(out)

            acc = lax.fori_loop(0, HALF, step, (zero,) * (2 * MODES), unroll=16)
            for m in range(MODES // 2):
                row = table_row(tre, tim, g, HALF * MODES + low + m)
                end = cadd(cmul(row, acc[4 * m:4 * m + 2]), acc[4 * m + 2:4 * m + 4])
                at = low + m
                eb_ref[g, at * BLOCKS:(at + 1) * BLOCKS, :] = end[0]
                eb_ref[g, (MODES + at) * BLOCKS:(MODES + at + 1) * BLOCKS, :] = end[1]
        q = (tre[g, STEPS * MODES:, :], tim[g, STEPS * MODES:, :])
        state = (jnp.zeros((MODES, LANES), F32),) * 2
        for n in range(BLOCKS):
            state = [jnp.where(b0 == n, 0.0, part) for part in state]
            add = [eb_ref[g, pl.ds(at * BLOCKS + n, MODES, stride=BLOCKS), :] for at in (0, MODES)]
            state = cadd(cmul(q, state), add)
        lanes = slice(g * LANES, (g + 1) * LANES)
        pay_ref[:MODES, lanes] = state[0]
        pay_ref[MODES:ROWS, lanes] = state[1]
        return unused

    for g in range(GROUPS):
        group(g, 0)
    pay_ref[ROWS:, :] = jnp.broadcast_to((s0 >= TOK).astype(F32), (PAY - ROWS, CH))


def last_power(tre, tim):
    return [jnp.concatenate([t[g, STEPS * MODES:, :] for g in range(GROUPS)], axis=1) for t in (tre, tim)]


def local_kernel(sig, tre, tim, decay_ref, res_ref, skip_ref, starts_ref, after_ref,
                 y_ref, weight_ref, taps):
    s0 = first_start(starts_ref)
    b0 = s0 // STEPS
    blocks = block_iota()
    y = 2.0 * decay_ref[...]
    series = jnp.ones_like(y)
    for n in range(10, 1, -1):
        series = 1.0 - y * (1.0 / n) * series
    scale = jnp.sqrt(y * series)
    weight = (res_ref[0] * scale, res_ref[1] * scale)
    weight_ref[:MODES, :] = weight[0]
    weight_ref[MODES:, :] = weight[1]
    for g in range(GROUPS):
        lanes = slice(g * LANES, (g + 1) * LANES)
        w_re, w_im = weight[0][:, lanes], weight[1][:, lanes]
        for k in range(STEPS):
            term = w_re * tre[g, k * MODES:(k + 1) * MODES, :] - w_im * tim[g, k * MODES:(k + 1) * MODES, :]
            row = jnp.sum(term, axis=0, keepdims=True)
            if k == 0:
                row = row + skip_ref[:, lanes]
            taps[g, k:k + 1, :] = row

    def group(g, unused):
        tile = 8

        def fir(select):
            xs = []
            for j in range(STEPS):
                x = sig[g, pl.ds(j, BLOCKS, stride=STEPS), :]
                late = (blocks * STEPS + j >= s0) | (blocks != b0)
                xs.append(jnp.where(late if select else jnp.logical_not(late), x, 0.0))
            for top in range(0, STEPS, tile):
                acc = [jnp.zeros((BLOCKS, LANES), F32)] * tile
                for k in range(top + tile):
                    tap = taps[g, k:k + 1, :]
                    for i in range(tile):
                        if top + i - k >= 0:
                            acc[i] = acc[i] + tap * xs[top + i - k]
                for i in range(tile):
                    if select:
                        y_ref[g, top + i] = acc[i]
                    else:
                        early = (blocks * STEPS + top + i < s0) & (blocks == b0)
                        y_ref[g, top + i] = y_ref[g, top + i] + jnp.where(early, acc[i], 0.0)

        fir(True)
        fir(False)
        return unused

    lax.fori_loop(0, GROUPS, group, 0)


def carry_kernel(eb_ref, tre, tim, weight_ref, starts_ref, pz_ref, gz_ref, qre, qim, rows_):
    s0 = first_start(starts_ref)
    b0 = s0 // STEPS
    blocks = block_iota()
    weight = (weight_ref[:MODES, :], weight_ref[MODES:, :])
    q = last_power(tre, tim)
    value = weight
    for n in range(BLOCKS):
        for g in range(GROUPS):
            lanes = slice(g * LANES, (g + 1) * LANES)
            qre[g, n * MODES:(n + 1) * MODES, :] = value[0][:, lanes]
            qim[g, n * MODES:(n + 1) * MODES, :] = value[1][:, lanes]
        value = cmul(value, q)
    power = q
    for n in range(3):
        for g in range(GROUPS):
            lanes = slice(g * LANES, (g + 1) * LANES)
            rows_[g, n * ROWS:n * ROWS + MODES, :] = power[0][:, lanes]
            rows_[g, n * ROWS + MODES:(n + 1) * ROWS, :] = power[1][:, lanes]
        power = square(power)
    for g in range(GROUPS):
        lanes = slice(g * LANES, (g + 1) * LANES)
        rows_[g, 3 * ROWS:3 * ROWS + MODES, :] = weight[0][:, lanes]
        rows_[g, 3 * ROWS + MODES:4 * ROWS, :] = weight[1][:, lanes]

    keeps = []
    for n in range(3):
        s = 1 << n
        keeps.append((blocks >= s) & jnp.logical_not((blocks - s < b0) & (b0 <= blocks)))
    heard = blocks <= b0

    def group(g, unused):
        for m in range(MODES):
            state = (eb_ref[g, m * BLOCKS:(m + 1) * BLOCKS, :],
                     eb_ref[g, (MODES + m) * BLOCKS:(MODES + m + 1) * BLOCKS, :])
            for n in range(3):
                moved = [jnp.where(keeps[n], pltpu.roll(part, 1 << n, 0), 0.0) for part in state]
                step = (rows_[g, n * ROWS + m:n * ROWS + m + 1, :],
                        rows_[g, n * ROWS + MODES + m:n * ROWS + MODES + m + 1, :])
                state = cadd(state, cmul(step, moved))
            before = [jnp.where(blocks >= 1, pltpu.roll(part, 1, 0), 0.0) for part in state]
            w = (rows_[g, 3 * ROWS + m:3 * ROWS + m + 1, :],
                 rows_[g, 3 * ROWS + MODES + m:3 * ROWS + MODES + m + 1, :])
            scaled = cmul(w, before)
            pz_ref[g, m] = scaled[0]
            pz_ref[g, MODES + m] = scaled[1]
            gz_ref[g, m] = jnp.where(heard, qre[g, pl.ds(m, BLOCKS, stride=MODES), :], 0.0)
            gz_ref[g, MODES + m] = jnp.where(heard, qim[g, pl.ds(m, BLOCKS, stride=MODES), :], 0.0)

        return unused

    lax.fori_loop(0, GROUPS, group, 0)


def put_state(ref, state, thru):
    for part, at in zip(state, (0, MODES)):
        high = part.astype(BF16)
        ref[at:at + MODES, :] = high
        ref[ROWS + at:ROWS + at + MODES, :] = (part - high.astype(F32)).astype(BF16)
    ref[2 * ROWS:SENT, :] = jnp.broadcast_to(thru, (FLAG, CH)).astype(BF16)


def get_state(ref):
    parts = [ref[at:at + MODES, :].astype(F32) + ref[ROWS + at:ROWS + at + MODES, :].astype(F32)
             for at in (0, MODES)]
    return parts, ref[2 * ROWS:SENT, :].astype(F32)[:1]


def chip_kernel(own_ref, other_ref, p256_ref, sent_ref):
    core = lax.axis_index("ctx") % NC
    first = (core == 0).astype(F32)
    own, other = halves(own_ref), halves(other_ref)
    own_thru, other_thru = own_ref[ROWS:ROWS + 1, :], other_ref[ROWS:ROWS + 1, :]
    early = [first * a + (1.0 - first) * b for a, b in zip(own, other)]
    late = [first * b + (1.0 - first) * a for a, b in zip(own, other)]
    late_thru = first * other_thru + (1.0 - first) * own_thru
    moved = cmul(halves(p256_ref), early)
    put_state(sent_ref, [late_thru * a + b for a, b in zip(moved, late)], own_thru * other_thru)


def put_pair(out_ref, side, own_ref, other_ref):
    rows = own_ref.shape[0]
    out_ref[pl.ds(pl.multiple_of(side * rows, rows), rows), :] = own_ref[...]
    out_ref[pl.ds(pl.multiple_of((1 - side) * rows, rows), rows), :] = other_ref[...]


def pair_kernel(own_ref, pair_ref, after_ref, out_ref):
    put_pair(out_ref, lax.axis_index("ctx") // (NC * NY) % 2, own_ref, pair_ref)


def row_kernel(own_ref, one_ref, two_ref, three_ref, p256_ref, after_ref, pay_ref, before_ref, factor_ref, held):
    mine = (lax.axis_index("ctx") // NC) % NY
    for k, ref in enumerate((own_ref, one_ref, two_ref, three_ref)):
        there = lax.rem(mine - k + NY, NY)
        state, thru = get_state(ref)
        held[there, :MODES, :] = state[0]
        held[there, MODES:ROWS, :] = state[1]
        held[there, ROWS:, :] = jnp.broadcast_to(thru, (PAY - ROWS, CH))
    p512 = square(halves(p256_ref))
    state = (jnp.zeros((MODES, CH), F32),) * 2
    factor = (jnp.ones((MODES, CH), F32), jnp.zeros((MODES, CH), F32))
    thru = jnp.ones((1, CH), F32)
    for i in range(NY):
        @pl.when(mine == i)
        def put(state=state, factor=factor):
            before_ref[:MODES, :] = state[0]
            before_ref[MODES:, :] = state[1]
            factor_ref[:MODES, :] = factor[0]
            factor_ref[MODES:, :] = factor[1]
        open_ = held[i, ROWS:ROWS + 1, :]
        step = (open_ * p512[0], open_ * p512[1])
        state = cadd(cmul(step, state), (held[i, :MODES, :], held[i, MODES:ROWS, :]))
        factor = cmul(step, factor)
        thru = thru * open_
    pay_ref[:MODES, :] = state[0]
    pay_ref[MODES:ROWS, :] = state[1]
    pay_ref[ROWS:, :] = jnp.broadcast_to(thru, (PAY - ROWS, CH))


def gate_kernel(query_ref, y_ref, pz_ref, gz_ref, tre, tim, starts_ref, own_ref, other_ref, p256_ref,
                before_ref, factor_ref, one_ref, two_ref, hidden_ref, conv, sin):
    index = lax.axis_index("ctx")
    core, row = index % NC, index // (NC * NY)
    p256 = halves(p256_ref)
    p2048 = square(square(square(p256)))
    has_one = (row >= 1).astype(F32)
    has_two = (row >= 2).astype(F32)
    far = cmul(p2048, halves(two_ref))
    open_one = has_two * one_ref[ROWS:ROWS + 1, :]
    incoming = [has_one * a + open_one * b for a, b in zip(halves(one_ref), far)]
    state = cadd(halves(before_ref), cmul(halves(factor_ref), incoming))
    second = (core == 1).astype(F32)
    moved = cmul(p256, state)
    early_thru = other_ref[ROWS:ROWS + 1, :]
    state = [(1.0 - second) * a + second * (early_thru * b + c)
             for a, b, c in zip(state, moved, halves(other_ref))]
    for g in range(GROUPS):
        lanes = slice(g * LANES, (g + 1) * LANES)
        sin[g, :MODES, :] = state[0][:, lanes]
        sin[g, MODES:, :] = state[1][:, lanes]
    s0 = first_start(starts_ref)
    b0 = s0 // STEPS
    blocks = block_iota()

    def group(g, unused):
        z = []
        for m in range(MODES):
            s = (sin[g, m:m + 1, :], sin[g, MODES + m:MODES + m + 1, :])
            z.append(cadd((pz_ref[g, m], pz_ref[g, MODES + m]),
                          cmul((gz_ref[g, m], gz_ref[g, MODES + m]), s)))

        def step(j, unused):
            base = (j + 1) * MODES
            total = [None] * 4
            for m in range(MODES):
                term = tre[g, pl.ds(base + m, 1), :] * z[m][0] - tim[g, pl.ds(base + m, 1), :] * z[m][1]
                total[m % 4] = term if total[m % 4] is None else total[m % 4] + term
            total = (total[0] + total[1]) + (total[2] + total[3])
            late = (blocks * STEPS + j >= s0) & (blocks == b0)
            conv[g, pl.ds(j, BLOCKS, stride=STEPS), :] = y_ref[g, j] + jnp.where(late, 0.0, total)
            return unused

        return lax.fori_loop(0, STEPS, step, unused, unroll=16)

    for g in range(GROUPS):
        group(g, 0)
    for g in range(GROUPS):
        lanes = slice(g * LANES, (g + 1) * LANES)
        gated = (query_ref[:, lanes].astype(F32) * conv[g]).astype(BF16)
        for q in range(FOLD):
            hidden_ref[:, q * CH + g * LANES:q * CH + (g + 1) * LANES] = gated[q * THIN:(q + 1) * THIN]


def four_kernel(both_ref, pair_ref, after_ref, even_ref, odd_ref):
    side = (lax.axis_index("ctx") // NC) % NY // 2
    even_ref[...] = jnp.where(side == 0, both_ref[...], pair_ref[...])
    odd_ref[...] = jnp.where(side == 0, pair_ref[...], both_ref[...])


def eight_kernel(even_ref, even_x, odd_ref, odd_y, after_up, after_down, all_ref, even_out, odd_out):
    n = even_ref.shape[0]
    for at, ref, out in ((0, even_ref, even_out), (0, odd_ref, odd_out), (n, even_x, even_out), (n, odd_y, odd_out)):
        out[at:at + n, :] = ref[...]
        start = at if out is even_out else 2 * n + at
        all_ref[start:start + n, :] = ref[...]


def join_kernel(even_ref, odd_ref, after_up, after_down, out_ref):
    n = even_ref.shape[0]
    out_ref[:n, :] = even_ref[...]
    out_ref[n:, :] = odd_ref[...]


def places(k):
    index = lax.axis_index("ctx")
    x, y = index // (NC * NY), (index // NC) % NY
    block = lax.rem(lax.axis_index("tp") - k + NZ, NZ)
    odd, i = lax.rem(block, 2), lax.rem(block // 2, 2)
    dx = (block // 4 != x // 2).astype(jnp.int32)
    found = []
    for h in range(2):
        dy = (lax.rem(y, 2) != h).astype(jnp.int32)
        far, near = jnp.where(odd == 1, dx, dy), jnp.where(odd == 1, dy, dx)
        at = far * 8 * WROWS + odd * 4 * WROWS + near * 2 * WROWS + i * WROWS
        found.append(pl.ds(pl.multiple_of(at, WROWS), WROWS))
    return found


def most_kernel(here, up1, down1, up2, down2, up3, down3, near_own, far_own, near_other, total_ref, left_ref, left):
    core = lax.axis_index("ctx") % NC
    wide = 8 * WROWS
    for k, ref in enumerate((here, up1, up2, up3, None, down3, down2, down1)):
        for h, lanes in enumerate(places(k)):
            for c in range(NC):
                side = jnp.where(core == c, 0, 1)
                if ref is None:
                    left[side, :, lanes] = jnp.zeros((TOK, WROWS), BF16)
                    continue
                for q in range(FOLD):
                    at = slice(q * CH + (NC * h + c) * WROWS, q * CH + (NC * h + c + 1) * WROWS)
                    left[side, q * THIN:(q + 1) * THIN, lanes] = ref[:, at]
    total_ref[...] = (jnp.dot(left[0, :, :wide], near_own[...], preferred_element_type=F32)
                      + jnp.dot(left[0, :, wide:], far_own[...], preferred_element_type=F32)
                      + jnp.dot(left[1, :, :wide], near_other[...], preferred_element_type=F32))
    left_ref[...] = left[1, :, wide:]


def last_kernel(up4, down4, after_ref, out_ref):
    for q in range(FOLD):
        middle = q * THIN + THIN // 2
        lanes = slice(q * CH, (q + 1) * CH)
        out_ref[q * THIN:middle, :] = up4[:, lanes]
        out_ref[middle:(q + 1) * THIN, :] = down4[:, lanes]


def rest_kernel(total_ref, left, last, near_own, near_other, own_ref, other_ref, out_ref, rows):
    core = lax.axis_index("ctx") % NC
    wide = 8 * WROWS
    for h, place in enumerate(places(4)):
        far = place.start >= wide
        at = pl.ds(pl.multiple_of(jnp.where(far, place.start - wide, place.start), WROWS), WROWS)
        for c in range(NC):
            lanes = slice((NC * h + c) * WROWS, (NC * h + c + 1) * WROWS)
            rows[lanes, :] = jnp.where(core == c, jnp.where(far, own_ref[at, :], near_own[at, :]),
                                       jnp.where(far, other_ref[at, :], near_other[at, :]))
    out_ref[...] = (total_ref[...] + jnp.dot(left[...], other_ref[...], preferred_element_type=F32)
                    + jnp.dot(last[...], rows[...], preferred_element_type=F32)).astype(BF16)


def ctx_index(x, y, c):
    return ((x % NX) * NY + y % NY) * NC + c % NC


def move(value, dx, dy, dc):
    pairs = [(ctx_index(x, y, c), ctx_index(x + dx, y + dy, c + dc))
             for x in range(NX) for y in range(NY) for c in range(NC)]
    return lax.ppermute(value, "ctx", pairs)


def trade(value, dx, dy):
    pairs = [(ctx_index(x, y, c), ctx_index(x ^ dx, y ^ dy, c))
             for x in range(NX) for y in range(NY) for c in range(NC)]
    return lax.ppermute(value, "ctx", pairs)


def turn(value, k):
    return lax.ppermute(value, "tp", [(i, (i + k) % NZ) for i in range(NZ)])


def shards(query, key, value, decay, freq, residue, skip, out_weight, doc_starts):
    starts = doc_starts.reshape(TOK // LANES, LANES)
    skip = skip.reshape(1, CH)
    sig = pltpu.VMEM((GROUPS, TOK, LANES), F32)
    qs = pltpu.VMEM((GROUPS, BLOCKS * MODES, LANES), F32)
    state_shape = struct(ROWS, CH)
    pay_shape = struct(PAY, CH)
    block_shape = struct(GROUPS, ROWS, BLOCKS, LANES)
    table = (GROUPS, (STEPS + 1) * MODES, LANES)

    magnitude = jnp.exp(-decay)
    tre, tim, p256 = call(
        powers_kernel, (struct(*table), struct(*table), state_shape),
        (magnitude * jnp.cos(freq), magnitude * jnp.sin(freq)), (), 300_000_000, 5_000_000)
    pay, eb, signal = call(
        ends_kernel, (pay_shape, struct(GROUPS, ROWS * BLOCKS, LANES), struct(GROUPS, TOK, LANES)),
        (key, value, starts, tre, tim), (), 20_000_000, 5_000_000)
    other = move(pay, 0, 0, 1)
    chip = call(chip_kernel, struct(SENT, CH, dtype=BF16), (pay, other, p256))
    near = [move(chip, 0, k, 0) for k in (1, 2, 3)]
    y, gain = call(
        local_kernel, (struct(GROUPS, STEPS, BLOCKS, LANES), state_shape),
        (signal, tre, tim, decay, residue, skip, starts, chip),
        [pltpu.VMEM((GROUPS, STEPS, LANES), F32)], 30_000_000, 5_000_000)
    row, before, factor = call(
        row_kernel, (pay_shape, state_shape, state_shape),
        (chip, *near, p256, gain), [pltpu.VMEM((NY, PAY, CH), F32)])
    back = [move(row, k, 0, 0) for k in (1, 2)]
    pz, gz = call(
        carry_kernel, (block_shape, block_shape), (eb, tre, tim, gain, starts),
        [qs, qs, pltpu.VMEM((GROUPS, 4 * ROWS, LANES), F32)], 30_000_000, 5_000_000)
    hidden = call(
        gate_kernel, struct(THIN, FOLD * CH, dtype=BF16),
        (query, y, pz, gz, tre, tim, starts, pay, other, p256, before, factor, *back),
        [sig, pltpu.VMEM((GROUPS, ROWS, LANES), F32)], 2_000_000_000, 5_000_000)

    both = call(pair_kernel, struct(2 * WROWS, CH, dtype=BF16), (out_weight, trade(out_weight, 1, 0), row))
    w2, w4, w8 = [struct(n * WROWS, CH, dtype=BF16) for n in (2, 4, 8)]
    even, odd = call(four_kernel, (w2, w2), (both, trade(both, 0, 2), hidden), (), 0, 2_000_000)
    half = THIN // 2
    up1, down1 = turn(hidden, 1), turn(hidden, -1)
    near, even, odd = call(
        eight_kernel, (w8, w4, w4), (even, trade(even, 2, 0), odd, trade(odd, 0, 1), up1, down1), (), 0, 4_000_000)
    up2, down2 = turn(up1, 1), turn(down1, -1)
    up3, down3 = turn(up2, 1), turn(down2, -1)
    up4, down4 = turn(up3[:half], 1), turn(down3[half:], -1)
    far = call(join_kernel, w8, (trade(even, 0, 1), trade(odd, 2, 0), up3, down3), (), 10000000000, 2_000_000)
    near_other = move(near, 0, 0, 1)
    total, left = call(
        most_kernel, (struct(TOK, CH), struct(TOK, 8 * WROWS, dtype=BF16)),
        (hidden, up1, down1, up2, down2, up3, down3, near, far, near_other),
        [pltpu.VMEM((NC, TOK, NZ * CH // NC), BF16)], 8000000000, 7_000_000)
    last = call(last_kernel, struct(TOK, CH, dtype=BF16), (up4, down4, total), (), 8000000000, 1_000_000)
    return call(
        rest_kernel, struct(TOK, CH, dtype=BF16), (total, left, last, near, near_other, far, move(far, 0, 0, 1)),
        [pltpu.VMEM((CH, CH), BF16)], TOK * CH * CH * NZ, 7_000_000)


def solution(mesh):
    in_specs = (
        P("ctx", "tp"),
        P("ctx", "tp"),
        P("ctx", "tp"),
        P(None, "tp"),
        P(None, "tp"),
        P(None, None, "tp"),
        P("tp"),
        P("ctx", "tp"),
        P("ctx"),
    )
    return jax.shard_map(
        shards, mesh=mesh, in_specs=in_specs, out_specs=P("ctx", "tp"), check_vma=False
    )
```

```python
import jax
import jax.numpy as jnp
from jax import lax
from jax.experimental import pallas as pl
from jax.experimental.pallas import tpu as pltpu
from jax.sharding import PartitionSpec as P

F32 = jnp.float32
BF16 = jnp.bfloat16
NX, NY, NC, NZ = 4, 4, 2, 8
TOK, CH, MODES = 256, 512, 16
LANES = 128
GROUPS = CH // LANES
STEPS = 32
BLOCKS = TOK // STEPS
HALF = STEPS // 2
ROWS = 2 * MODES
PAY = ROWS + 8
VMEM = pl.BlockSpec(memory_space=pltpu.VMEM)
FLAG = 16
SENT = 2 * ROWS + FLAG
WROWS = 128
FOLD = 8
THIN = TOK // FOLD
PARAMS = pltpu.CompilerParams(vmem_limit_bytes=24 * 1024 * 1024)


def call(kernel, outs, args, scratch=(), flops=0, nbytes=0):
    return pl.pallas_call(
        kernel,
        out_shape=outs,
        in_specs=[VMEM] * len(args),
        out_specs=jax.tree.map(lambda unused: VMEM, outs),
        scratch_shapes=list(scratch),
        compiler_params=PARAMS,
        cost_estimate=pl.CostEstimate(flops=flops, bytes_accessed=nbytes, transcendentals=0),
    )(*args)


def struct(*shape, dtype=F32):
    return jax.ShapeDtypeStruct(shape, dtype)


def cmul(a, b):
    return a[0] * b[0] - a[1] * b[1], a[0] * b[1] + a[1] * b[0]


def cadd(a, b):
    return a[0] + b[0], a[1] + b[1]


def square(a):
    return a[0] * a[0] - a[1] * a[1], 2.0 * a[0] * a[1]


def halves(ref):
    return ref[:MODES, :], ref[MODES:ROWS, :]


def first_start(starts_ref):
    starts = starts_ref[...]
    at = lax.broadcasted_iota(jnp.int32, starts.shape, 0) * LANES
    at = at + lax.broadcasted_iota(jnp.int32, starts.shape, 1)
    where = jnp.where(starts > 0, at, TOK)
    return jnp.min(jnp.min(where, axis=1, keepdims=True), axis=0, keepdims=True)


def fill_powers(pole, table_re, table_im, count):
    def put(k, value):
        for g in range(GROUPS):
            rows = pl.ds(pl.multiple_of(k * MODES, MODES), MODES)
            lanes = slice(g * LANES, (g + 1) * LANES)
            table_re[g, rows, :] = value[0][:, lanes]
            table_im[g, rows, :] = value[1][:, lanes]

    def step(k, value):
        put(k, value)
        return cmul(value, pole)

    one = (jnp.ones((MODES, CH), F32), jnp.zeros((MODES, CH), F32))
    last = lax.fori_loop(0, count, step, one)
    return last


def fill_signal(key_ref, value_ref, sig):
    for g in range(GROUPS):
        lanes = slice(g * LANES, (g + 1) * LANES)
        sig[g, :TOK, :] = key_ref[:, lanes].astype(F32) * value_ref[:, lanes].astype(F32)


def block_iota():
    return lax.broadcasted_iota(jnp.int32, (BLOCKS, LANES), 0)


def powers_kernel(pole_re, pole_im, tre, tim, p256_ref):
    fill_powers((pole_re[...], pole_im[...]), tre, tim, STEPS + 1)
    value = square(square(square(last_power(tre, tim))))
    p256_ref[:MODES, :] = value[0]
    p256_ref[MODES:, :] = value[1]


def table_row(tre, tim, g, at):
    return [jnp.broadcast_to(t[g, pl.ds(at, 1), :], (BLOCKS, LANES)) for t in (tre, tim)]


def ends_kernel(key_ref, value_ref, starts_ref, tre, tim, pay_ref, eb_ref, sig):
    s0 = first_start(starts_ref)
    b0 = s0 // STEPS
    fill_signal(key_ref, value_ref, sig)
    blocks = block_iota()

    def group(g, unused):
        zero = jnp.zeros((BLOCKS, LANES), F32)
        for low in range(0, MODES, MODES // 2):
            def step(j, acc, low=low):
                xs = []
                for at in (j, j + HALF):
                    x = sig[g, pl.ds(at, BLOCKS, stride=STEPS), :]
                    xs.append(jnp.where((blocks * STEPS + at >= s0) | (blocks != b0), x, 0.0))
                base = (HALF - 1 - j) * MODES + low
                out = []
                for m in range(MODES // 2):
                    row = table_row(tre, tim, g, base + m)
                    for n in range(4):
                        out.append(acc[4 * m + n] + row[n % 2] * xs[n // 2])
                return tuple(out)

            acc = lax.fori_loop(0, HALF, step, (zero,) * (2 * MODES), unroll=16)
            for m in range(MODES // 2):
                row = table_row(tre, tim, g, HALF * MODES + low + m)
                end = cadd(cmul(row, acc[4 * m:4 * m + 2]), acc[4 * m + 2:4 * m + 4])
                at = low + m
                eb_ref[g, at * BLOCKS:(at + 1) * BLOCKS, :] = end[0]
                eb_ref[g, (MODES + at) * BLOCKS:(MODES + at + 1) * BLOCKS, :] = end[1]
        q = (tre[g, STEPS * MODES:, :], tim[g, STEPS * MODES:, :])
        state = (jnp.zeros((MODES, LANES), F32),) * 2
        for n in range(BLOCKS):
            state = [jnp.where(b0 == n, 0.0, part) for part in state]
            add = [eb_ref[g, pl.ds(at * BLOCKS + n, MODES, stride=BLOCKS), :] for at in (0, MODES)]
            state = cadd(cmul(q, state), add)
        lanes = slice(g * LANES, (g + 1) * LANES)
        pay_ref[:MODES, lanes] = state[0]
        pay_ref[MODES:ROWS, lanes] = state[1]
        return unused

    for g in range(GROUPS):
        group(g, 0)
    pay_ref[ROWS:, :] = jnp.broadcast_to((s0 >= TOK).astype(F32), (PAY - ROWS, CH))


def last_power(tre, tim):
    return [jnp.concatenate([t[g, STEPS * MODES:, :] for g in range(GROUPS)], axis=1) for t in (tre, tim)]


def local_kernel(sig, tre, tim, decay_ref, res_ref, skip_ref, starts_ref, after_ref,
                 y_ref, weight_ref, taps):
    s0 = first_start(starts_ref)
    b0 = s0 // STEPS
    blocks = block_iota()
    y = 2.0 * decay_ref[...]
    series = jnp.ones_like(y)
    for n in range(10, 1, -1):
        series = 1.0 - y * (1.0 / n) * series
    scale = jnp.sqrt(y * series)
    weight = (res_ref[0] * scale, res_ref[1] * scale)
    weight_ref[:MODES, :] = weight[0]
    weight_ref[MODES:, :] = weight[1]
    for g in range(GROUPS):
        lanes = slice(g * LANES, (g + 1) * LANES)
        w_re, w_im = weight[0][:, lanes], weight[1][:, lanes]
        for k in range(STEPS):
            term = w_re * tre[g, k * MODES:(k + 1) * MODES, :] - w_im * tim[g, k * MODES:(k + 1) * MODES, :]
            row = jnp.sum(term, axis=0, keepdims=True)
            if k == 0:
                row = row + skip_ref[:, lanes]
            taps[g, k:k + 1, :] = row

    def group(g, unused):
        tile = 8

        def fir(select):
            xs = []
            for j in range(STEPS):
                x = sig[g, pl.ds(j, BLOCKS, stride=STEPS), :]
                late = (blocks * STEPS + j >= s0) | (blocks != b0)
                xs.append(jnp.where(late if select else jnp.logical_not(late), x, 0.0))
            for top in range(0, STEPS, tile):
                acc = [jnp.zeros((BLOCKS, LANES), F32)] * tile
                for k in range(top + tile):
                    tap = taps[g, k:k + 1, :]
                    for i in range(tile):
                        if top + i - k >= 0:
                            acc[i] = acc[i] + tap * xs[top + i - k]
                for i in range(tile):
                    if select:
                        y_ref[g, top + i] = acc[i]
                    else:
                        early = (blocks * STEPS + top + i < s0) & (blocks == b0)
                        y_ref[g, top + i] = y_ref[g, top + i] + jnp.where(early, acc[i], 0.0)

        fir(True)
        fir(False)
        return unused

    lax.fori_loop(0, GROUPS, group, 0)


def carry_kernel(eb_ref, tre, tim, weight_ref, starts_ref, pz_ref, gz_ref, qre, qim, rows_):
    s0 = first_start(starts_ref)
    b0 = s0 // STEPS
    blocks = block_iota()
    weight = (weight_ref[:MODES, :], weight_ref[MODES:, :])
    q = last_power(tre, tim)
    value = weight
    for n in range(BLOCKS):
        for g in range(GROUPS):
            lanes = slice(g * LANES, (g + 1) * LANES)
            qre[g, n * MODES:(n + 1) * MODES, :] = value[0][:, lanes]
            qim[g, n * MODES:(n + 1) * MODES, :] = value[1][:, lanes]
        value = cmul(value, q)
    power = q
    for n in range(3):
        for g in range(GROUPS):
            lanes = slice(g * LANES, (g + 1) * LANES)
            rows_[g, n * ROWS:n * ROWS + MODES, :] = power[0][:, lanes]
            rows_[g, n * ROWS + MODES:(n + 1) * ROWS, :] = power[1][:, lanes]
        power = square(power)
    for g in range(GROUPS):
        lanes = slice(g * LANES, (g + 1) * LANES)
        rows_[g, 3 * ROWS:3 * ROWS + MODES, :] = weight[0][:, lanes]
        rows_[g, 3 * ROWS + MODES:4 * ROWS, :] = weight[1][:, lanes]

    keeps = []
    for n in range(3):
        s = 1 << n
        keeps.append((blocks >= s) & jnp.logical_not((blocks - s < b0) & (b0 <= blocks)))
    heard = blocks <= b0

    def group(g, unused):
        for m in range(MODES):
            state = (eb_ref[g, m * BLOCKS:(m + 1) * BLOCKS, :],
                     eb_ref[g, (MODES + m) * BLOCKS:(MODES + m + 1) * BLOCKS, :])
            for n in range(3):
                moved = [jnp.where(keeps[n], pltpu.roll(part, 1 << n, 0), 0.0) for part in state]
                step = (rows_[g, n * ROWS + m:n * ROWS + m + 1, :],
                        rows_[g, n * ROWS + MODES + m:n * ROWS + MODES + m + 1, :])
                state = cadd(state, cmul(step, moved))
            before = [jnp.where(blocks >= 1, pltpu.roll(part, 1, 0), 0.0) for part in state]
            w = (rows_[g, 3 * ROWS + m:3 * ROWS + m + 1, :],
                 rows_[g, 3 * ROWS + MODES + m:3 * ROWS + MODES + m + 1, :])
            scaled = cmul(w, before)
            pz_ref[g, m] = scaled[0]
            pz_ref[g, MODES + m] = scaled[1]
            gz_ref[g, m] = jnp.where(heard, qre[g, pl.ds(m, BLOCKS, stride=MODES), :], 0.0)
            gz_ref[g, MODES + m] = jnp.where(heard, qim[g, pl.ds(m, BLOCKS, stride=MODES), :], 0.0)

        return unused

    lax.fori_loop(0, GROUPS, group, 0)


def put_state(ref, state, thru):
    for part, at in zip(state, (0, MODES)):
        high = part.astype(BF16)
        ref[at:at + MODES, :] = high
        ref[ROWS + at:ROWS + at + MODES, :] = (part - high.astype(F32)).astype(BF16)
    ref[2 * ROWS:SENT, :] = jnp.broadcast_to(thru, (FLAG, CH)).astype(BF16)


def get_state(ref):
    parts = [ref[at:at + MODES, :].astype(F32) + ref[ROWS + at:ROWS + at + MODES, :].astype(F32)
             for at in (0, MODES)]
    return parts, ref[2 * ROWS:SENT, :].astype(F32)[:1]


def chip_kernel(own_ref, other_ref, p256_ref, sent_ref):
    core = lax.axis_index("ctx") % NC
    first = (core == 0).astype(F32)
    own, other = halves(own_ref), halves(other_ref)
    own_thru, other_thru = own_ref[ROWS:ROWS + 1, :], other_ref[ROWS:ROWS + 1, :]
    early = [first * a + (1.0 - first) * b for a, b in zip(own, other)]
    late = [first * b + (1.0 - first) * a for a, b in zip(own, other)]
    late_thru = first * other_thru + (1.0 - first) * own_thru
    moved = cmul(halves(p256_ref), early)
    put_state(sent_ref, [late_thru * a + b for a, b in zip(moved, late)], own_thru * other_thru)


def put_pair(out_ref, side, own_ref, other_ref):
    rows = own_ref.shape[0]
    out_ref[pl.ds(pl.multiple_of(side * rows, rows), rows), :] = own_ref[...]
    out_ref[pl.ds(pl.multiple_of((1 - side) * rows, rows), rows), :] = other_ref[...]


def pair_kernel(own_ref, pair_ref, after_ref, out_ref):
    put_pair(out_ref, lax.axis_index("ctx") // (NC * NY) % 2, own_ref, pair_ref)


def row_kernel(own_ref, one_ref, two_ref, three_ref, p256_ref, after_ref, pay_ref, before_ref, factor_ref, held):
    mine = (lax.axis_index("ctx") // NC) % NY
    for k, ref in enumerate((own_ref, one_ref, two_ref, three_ref)):
        there = lax.rem(mine - k + NY, NY)
        state, thru = get_state(ref)
        held[there, :MODES, :] = state[0]
        held[there, MODES:ROWS, :] = state[1]
        held[there, ROWS:, :] = jnp.broadcast_to(thru, (PAY - ROWS, CH))
    p512 = square(halves(p256_ref))
    state = (jnp.zeros((MODES, CH), F32),) * 2
    factor = (jnp.ones((MODES, CH), F32), jnp.zeros((MODES, CH), F32))
    thru = jnp.ones((1, CH), F32)
    for i in range(NY):
        @pl.when(mine == i)
        def put(state=state, factor=factor):
            before_ref[:MODES, :] = state[0]
            before_ref[MODES:, :] = state[1]
            factor_ref[:MODES, :] = factor[0]
            factor_ref[MODES:, :] = factor[1]
        open_ = held[i, ROWS:ROWS + 1, :]
        step = (open_ * p512[0], open_ * p512[1])
        state = cadd(cmul(step, state), (held[i, :MODES, :], held[i, MODES:ROWS, :]))
        factor = cmul(step, factor)
        thru = thru * open_
    pay_ref[:MODES, :] = state[0]
    pay_ref[MODES:ROWS, :] = state[1]
    pay_ref[ROWS:, :] = jnp.broadcast_to(thru, (PAY - ROWS, CH))


def gate_kernel(query_ref, y_ref, pz_ref, gz_ref, tre, tim, starts_ref, own_ref, other_ref, p256_ref,
                before_ref, factor_ref, one_ref, two_ref, hidden_ref, conv, sin):
    index = lax.axis_index("ctx")
    core, row = index % NC, index // (NC * NY)
    p256 = halves(p256_ref)
    p2048 = square(square(square(p256)))
    has_one = (row >= 1).astype(F32)
    has_two = (row >= 2).astype(F32)
    far = cmul(p2048, halves(two_ref))
    open_one = has_two * one_ref[ROWS:ROWS + 1, :]
    incoming = [has_one * a + open_one * b for a, b in zip(halves(one_ref), far)]
    state = cadd(halves(before_ref), cmul(halves(factor_ref), incoming))
    second = (core == 1).astype(F32)
    moved = cmul(p256, state)
    early_thru = other_ref[ROWS:ROWS + 1, :]
    state = [(1.0 - second) * a + second * (early_thru * b + c)
             for a, b, c in zip(state, moved, halves(other_ref))]
    for g in range(GROUPS):
        lanes = slice(g * LANES, (g + 1) * LANES)
        sin[g, :MODES, :] = state[0][:, lanes]
        sin[g, MODES:, :] = state[1][:, lanes]
    s0 = first_start(starts_ref)
    b0 = s0 // STEPS
    blocks = block_iota()

    def group(g, unused):
        z = []
        for m in range(MODES):
            s = (sin[g, m:m + 1, :], sin[g, MODES + m:MODES + m + 1, :])
            z.append(cadd((pz_ref[g, m], pz_ref[g, MODES + m]),
                          cmul((gz_ref[g, m], gz_ref[g, MODES + m]), s)))

        def step(j, unused):
            base = (j + 1) * MODES
            total = [None] * 4
            for m in range(MODES):
                term = tre[g, pl.ds(base + m, 1), :] * z[m][0] - tim[g, pl.ds(base + m, 1), :] * z[m][1]
                total[m % 4] = term if total[m % 4] is None else total[m % 4] + term
            total = (total[0] + total[1]) + (total[2] + total[3])
            late = (blocks * STEPS + j >= s0) & (blocks == b0)
            conv[g, pl.ds(j, BLOCKS, stride=STEPS), :] = y_ref[g, j] + jnp.where(late, 0.0, total)
            return unused

        return lax.fori_loop(0, STEPS, step, unused, unroll=16)

    for g in range(GROUPS):
        group(g, 0)
    for g in range(GROUPS):
        lanes = slice(g * LANES, (g + 1) * LANES)
        gated = (query_ref[:, lanes].astype(F32) * conv[g, :TOK, :]).astype(BF16)
        for q in range(FOLD):
            hidden_ref[:, q * CH + g * LANES:q * CH + (g + 1) * LANES] = gated[q * THIN:(q + 1) * THIN]


def four_kernel(both_ref, pair_ref, after_ref, even_ref, odd_ref):
    side = (lax.axis_index("ctx") // NC) % NY // 2
    even_ref[...] = jnp.where(side == 0, both_ref[...], pair_ref[...])
    odd_ref[...] = jnp.where(side == 0, pair_ref[...], both_ref[...])


def eight_kernel(even_ref, even_x, odd_ref, odd_y, after_up, after_down, all_ref, even_out, odd_out):
    n = even_ref.shape[0]
    for at, ref, out in ((0, even_ref, even_out), (0, odd_ref, odd_out), (n, even_x, even_out), (n, odd_y, odd_out)):
        out[at:at + n, :] = ref[...]
        start = at if out is even_out else 2 * n + at
        all_ref[start:start + n, :] = ref[...]


def join_kernel(even_ref, odd_ref, after_up, after_down, out_ref):
    n = even_ref.shape[0]
    out_ref[:n, :] = even_ref[...]
    out_ref[n:, :] = odd_ref[...]


def places(k):
    index = lax.axis_index("ctx")
    x, y = index // (NC * NY), (index // NC) % NY
    block = lax.rem(lax.axis_index("tp") - k + NZ, NZ)
    odd, i = lax.rem(block, 2), lax.rem(block // 2, 2)
    dx = (block // 4 != x // 2).astype(jnp.int32)
    found = []
    for h in range(2):
        dy = (lax.rem(y, 2) != h).astype(jnp.int32)
        far, near = jnp.where(odd == 1, dx, dy), jnp.where(odd == 1, dy, dx)
        at = far * 8 * WROWS + odd * 4 * WROWS + near * 2 * WROWS + i * WROWS
        found.append(pl.ds(pl.multiple_of(at, WROWS), WROWS))
    return found


def most_kernel(here, up1, down1, up2, down2, up3, down3, near_own, far_own, near_other, total_ref, left_ref, left):
    core = lax.axis_index("ctx") % NC
    wide = 8 * WROWS
    for k, ref in enumerate((here, up1, up2, up3, None, down3, down2, down1)):
        for h, lanes in enumerate(places(k)):
            for c in range(NC):
                side = jnp.where(core == c, 0, 1)
                if ref is None:
                    left[side, :, lanes] = jnp.zeros((TOK, WROWS), BF16)
                    continue
                for q in range(FOLD):
                    at = slice(q * CH + (NC * h + c) * WROWS, q * CH + (NC * h + c + 1) * WROWS)
                    left[side, q * THIN:(q + 1) * THIN, lanes] = ref[:, at]
    total_ref[...] = (jnp.dot(left[0, :, :wide], near_own[...], preferred_element_type=F32)
                      + jnp.dot(left[0, :, wide:], far_own[...], preferred_element_type=F32)
                      + jnp.dot(left[1, :, :wide], near_other[...], preferred_element_type=F32))
    left_ref[...] = left[1, :, wide:]


def last_kernel(up4, down4, after_ref, out_ref):
    for q in range(FOLD):
        middle = q * THIN + THIN // 2
        lanes = slice(q * CH, (q + 1) * CH)
        out_ref[q * THIN:middle, :] = up4[:, lanes]
        out_ref[middle:(q + 1) * THIN, :] = down4[:, lanes]


def rest_kernel(total_ref, left, last, near_own, near_other, own_ref, other_ref, out_ref, rows):
    core = lax.axis_index("ctx") % NC
    wide = 8 * WROWS
    for h, place in enumerate(places(4)):
        far = place.start >= wide
        at = pl.ds(pl.multiple_of(jnp.where(far, place.start - wide, place.start), WROWS), WROWS)
        for c in range(NC):
            lanes = slice((NC * h + c) * WROWS, (NC * h + c + 1) * WROWS)
            rows[lanes, :] = jnp.where(core == c, jnp.where(far, own_ref[at, :], near_own[at, :]),
                                       jnp.where(far, other_ref[at, :], near_other[at, :]))
    out_ref[...] = (total_ref[...] + jnp.dot(left[...], other_ref[...], preferred_element_type=F32)
                    + jnp.dot(last[...], rows[...], preferred_element_type=F32)).astype(BF16)


def ctx_index(x, y, c):
    return ((x % NX) * NY + y % NY) * NC + c % NC


def move(value, dx, dy, dc):
    pairs = [(ctx_index(x, y, c), ctx_index(x + dx, y + dy, c + dc))
             for x in range(NX) for y in range(NY) for c in range(NC)]
    return lax.ppermute(value, "ctx", pairs)


def trade(value, dx, dy):
    pairs = [(ctx_index(x, y, c), ctx_index(x ^ dx, y ^ dy, c))
             for x in range(NX) for y in range(NY) for c in range(NC)]
    return lax.ppermute(value, "ctx", pairs)


def turn(value, k):
    return lax.ppermute(value, "tp", [(i, (i + k) % NZ) for i in range(NZ)])


def shards(query, key, value, decay, freq, residue, skip, out_weight, doc_starts):
    starts = doc_starts.reshape(TOK // LANES, LANES)
    skip = skip.reshape(1, CH)
    sig = pltpu.VMEM((GROUPS, TOK + STEPS, LANES), F32)
    qs = pltpu.VMEM((GROUPS, (BLOCKS + 1) * MODES, LANES), F32)
    state_shape = struct(ROWS, CH)
    pay_shape = struct(PAY, CH)
    block_shape = struct(GROUPS, ROWS, BLOCKS, LANES)
    table = (GROUPS, (STEPS + 1) * MODES, LANES)

    magnitude = jnp.exp(-decay)
    tre, tim, p256 = call(
        powers_kernel, (struct(*table), struct(*table), state_shape),
        (magnitude * jnp.cos(freq), magnitude * jnp.sin(freq)), (), 300_000_000, 5_000_000)
    pay, eb, signal = call(
        ends_kernel, (pay_shape, struct(GROUPS, (ROWS + 1) * BLOCKS, LANES), struct(GROUPS, TOK + STEPS, LANES)),
        (key, value, starts, tre, tim), (), 20_000_000, 5_000_000)
    other = move(pay, 0, 0, 1)
    chip = call(chip_kernel, struct(SENT, CH, dtype=BF16), (pay, other, p256))
    near = [move(chip, 0, k, 0) for k in (1, 2, 3)]
    y, gain = call(
        local_kernel, (struct(GROUPS, STEPS, BLOCKS, LANES), state_shape),
        (signal, tre, tim, decay, residue, skip, starts, chip),
        [pltpu.VMEM((GROUPS, STEPS, LANES), F32)], 30_000_000, 5_000_000)
    row, before, factor = call(
        row_kernel, (pay_shape, state_shape, state_shape),
        (chip, *near, p256, gain), [pltpu.VMEM((NY, PAY, CH), F32)])
    back = [move(row, k, 0, 0) for k in (1, 2)]
    pz, gz = call(
        carry_kernel, (block_shape, block_shape), (eb, tre, tim, gain, starts),
        [qs, qs, pltpu.VMEM((GROUPS, 4 * ROWS, LANES), F32)], 30_000_000, 5_000_000)
    hidden = call(
        gate_kernel, struct(THIN, FOLD * CH, dtype=BF16),
        (query, y, pz, gz, tre, tim, starts, pay, other, p256, before, factor, *back),
        [sig, pltpu.VMEM((GROUPS, ROWS, LANES), F32)], 2_000_000_000, 5_000_000)

    both = call(pair_kernel, struct(2 * WROWS, CH, dtype=BF16), (out_weight, trade(out_weight, 1, 0), row))
    w2, w4, w8 = [struct(n * WROWS, CH, dtype=BF16) for n in (2, 4, 8)]
    even, odd = call(four_kernel, (w2, w2), (both, trade(both, 0, 2), hidden), (), 0, 2_000_000)
    half = THIN // 2
    up1, down1 = turn(hidden, 1), turn(hidden, -1)
    near, even, odd = call(
        eight_kernel, (w8, w4, w4), (even, trade(even, 2, 0), odd, trade(odd, 0, 1), up1, down1), (), 0, 4_000_000)
    up2, down2 = turn(up1, 1), turn(down1, -1)
    up3, down3 = turn(up2, 1), turn(down2, -1)
    up4, down4 = turn(up3[:half], 1), turn(down3[half:], -1)
    far = call(join_kernel, w8, (trade(even, 0, 1), trade(odd, 2, 0), up3, down3), (), 10000000000, 2_000_000)
    near_other = move(near, 0, 0, 1)
    total, left = call(
        most_kernel, (struct(TOK, CH), struct(TOK, 8 * WROWS, dtype=BF16)),
        (hidden, up1, down1, up2, down2, up3, down3, near, far, near_other),
        [pltpu.VMEM((NC, TOK, NZ * CH // NC), BF16)], 8000000000, 7_000_000)
    last = call(last_kernel, struct(TOK, CH, dtype=BF16), (up4, down4, total), (), 8000000000, 1_000_000)
    return call(
        rest_kernel, struct(TOK, CH, dtype=BF16), (total, left, last, near, near_other, far, move(far, 0, 0, 1)),
        [pltpu.VMEM((CH, CH), BF16)], TOK * CH * CH * NZ, 7_000_000)


def solution(mesh):
    in_specs = (
        P("ctx", "tp"),
        P("ctx", "tp"),
        P("ctx", "tp"),
        P(None, "tp"),
        P(None, "tp"),
        P(None, None, "tp"),
        P("tp"),
        P("ctx", "tp"),
        P("ctx"),
    )
    return jax.shard_map(
        shards, mesh=mesh, in_specs=in_specs, out_specs=P("ctx", "tp"), check_vma=False
    )
```
